32 devices in a mesh: batch: 16 (over z, y, x), seq: 2 (over core).
Axes of the slice: x: 2, y: 2, z: 4, core: 2. Of those that a mesh axis runs over, the one named last changes fastest.
Arguments:
- input_short: bfloat16 [64, 64, 768], P('batch', 'seq'), may hold values from -6 to 6
- input_middle: bfloat16 [32, 128, 768], P('batch', 'seq'), may hold values from -6 to 6
- input_long: bfloat16 [16, 256, 768], P('batch', 'seq'), may hold values from -6 to 6
- length_short: int32 [64], P('batch'), may hold values from 33 to 64, as said below
- length_middle: int32 [32], P('batch'), may hold values from 65 to 128, as said below
- length_long: int32 [16], P('batch'), may hold values from 129 to 256, as said below
- cotangent_short: bfloat16 [64, 64, 768], P('batch', 'seq'), may hold values from -6 to 6
- cotangent_middle: bfloat16 [32, 128, 768], P('batch', 'seq'), may hold values from -6 to 6
- cotangent_long: bfloat16 [16, 256, 768], P('batch', 'seq'), may hold values from -6 to 6
- query_weight: bfloat16 [768, 768], P(('batch', 'seq')), may hold values from -0.109375 to 0.109375
- key_weight: bfloat16 [768, 768], P(('batch', 'seq')), may hold values from -0.109375 to 0.109375
- value_weight: bfloat16 [768, 768], P(('batch', 'seq')), may hold values from -0.21875 to 0.21875
- output_weight: bfloat16 [768, 768], P(('batch', 'seq')), may hold values from -0.875 to 0.875
- query_bias: bfloat16 [768], P(('batch', 'seq')), may hold values from -1.5 to 1.5
- key_bias: bfloat16 [768], P(('batch', 'seq')), may hold values from -1.5 to 1.5
- value_bias: bfloat16 [768], P(('batch', 'seq')), may hold values from -3 to 3
- output_bias: bfloat16 [768], P(('batch', 'seq')), may hold values from -3 to 3
- attn_gain: bfloat16 [768], P(('batch', 'seq')), may hold values from 0.5 to 1.5
- attn_shift: bfloat16 [768], P(('batch', 'seq')), may hold values from -3 to 3
- up_weight: bfloat16 [768, 3072], P(None, ('batch', 'seq')), may hold values from -0.21875 to 0.21875
- up_bias: bfloat16 [3072], P(('batch', 'seq')), may hold values from -3 to 3
- down_weight: bfloat16 [3072, 768], P(('batch', 'seq')), may hold values from -0.109375 to 0.109375
- down_bias: bfloat16 [768], P(('batch', 'seq')), may hold values from -3 to 3
- ffn_gain: bfloat16 [768], P(('batch', 'seq')), may hold values from 0.5 to 1.5
- ffn_shift: bfloat16 [768], P(('batch', 'seq')), may hold values from -3 to 3
- projection: float32 [64, 32], replicated, may hold values from -4 to 4
Outputs:
- output_short: bfloat16 [64, 64, 768], P('batch', 'seq')
- output_middle: bfloat16 [32, 128, 768], P('batch', 'seq')
- output_long: bfloat16 [16, 256, 768], P('batch', 'seq')
- grad_short: bfloat16 [64, 64, 768], P('batch', 'seq')
- grad_middle: bfloat16 [32, 128, 768], P('batch', 'seq')
- grad_long: bfloat16 [16, 256, 768], P('batch', 'seq')
- grad_query_weight: float32 [768, 768], P(('batch', 'seq'))
- grad_key_weight: float32 [768, 768], P(('batch', 'seq'))
- grad_value_weight: float32 [768, 768], P(('batch', 'seq'))
- grad_output_weight: float32 [768, 768], P(('batch', 'seq'))
- grad_query_bias: float32 [768], P(('batch', 'seq'))
- grad_key_bias: float32 [768], P(('batch', 'seq'))
- grad_value_bias: float32 [768], P(('batch', 'seq'))
- grad_output_bias: float32 [768], P(('batch', 'seq'))
- grad_attn_gain: float32 [768], P(('batch', 'seq'))
- grad_attn_shift: float32 [768], P(('batch', 'seq'))
- grad_up_weight: float32 [768, 3072], P(None, ('batch', 'seq'))
- grad_up_bias: float32 [3072], P(('batch', 'seq'))
- grad_down_weight: float32 [3072, 768], P(('batch', 'seq'))
- grad_down_bias: float32 [768], P(('batch', 'seq'))
- grad_ffn_gain: float32 [768], P(('batch', 'seq'))
- grad_ffn_shift: float32 [768], P(('batch', 'seq'))
The draws below stay inside these ranges and needn't reach their ends.
Inputs may be any that keep to these rules, and one draw needn't show every extreme that they name: `length_short`: rows at or past a molecule's length are padding. In every draw some molecule has 64 rows in use and some 64 // 2 + 1. `length_middle`: rows at or past a molecule's length are padding. In every draw some molecule has 128 rows in use and some 128 // 2 + 1. `length_long`: rows at or past a molecule's length are padding. In every draw some molecule has 256 rows in use and some 256 // 2 + 1.
All inputs are finite; a program needn't handle non-finite values.
Results may differ from the reference program's by a relative error of at most 0.029.
Values may be sent and summed in bfloat16 or wider, within the bound.
No kernel may reach another device: no remote copies, remote signals or barrier semaphores. Data moves between devices by JAX's collectives and lax.ppermute only.
A program may use at most 192 MiB of HBM per device.

```python
import math
import jax
import jax.numpy as jnp
from jax import lax

D = 768
FF = 3072
HD = 64
R = 32
L1 = 64
L2 = 128
L3 = 256
M1 = 64
M2 = 32
M3 = 16


def lengths_of(key, count, longest):
    first, second, third = jax.random.split(key, 3)
    drawn = jax.random.randint(first, (count,), longest // 2 + 1, longest + 1)
    top = jax.random.randint(second, (), 0, count)
    bottom = (top + 1 + jax.random.randint(third, (), 0, count - 1)) % count
    drawn = drawn.at[top].set(longest)
    drawn = drawn.at[bottom].set(longest // 2 + 1)
    return drawn.astype(jnp.int32)


def draw_length_short(key, part):
    key = jax.random.fold_in(key, 1)
    return lengths_of(key, M1, L1)


def draw_length_middle(key, part):
    key = jax.random.fold_in(key, 2)
    return lengths_of(key, M2, L2)


def draw_length_long(key, part):
    key = jax.random.fold_in(key, 3)
    return lengths_of(key, M3, L3)


def steps_of(stream_key, dims, cuts, smallest, top_value):
    factor_of = 1.0
    for dim, blocks in cuts:
        heights = jax.random.uniform(jax.random.fold_in(jax.random.fold_in(stream_key, 6), dim), (blocks,), jnp.float32, smallest / len(cuts), top_value / len(cuts))
        factor_of = factor_of * jnp.repeat(jnp.exp(heights), dims[dim] // blocks).reshape((-1,) + (1,) * (len(dims) - 1 - dim))
    return factor_of


def scatter_about(stream_key, dims, scale, most, cuts=(), held_as=jnp.bfloat16):
    values = jax.random.normal(stream_key, dims, jnp.float32) * scale
    if len(cuts) > 0:
        values = steps_of(stream_key, dims, cuts, -0.22, 0.18) * values
    return jnp.clip(values, min=-most, max=most).astype(held_as)


def setup_inputs(seed: int = 0) -> dict:
    key_list = jax.random.split(jax.random.key(seed), 27)
    return {
        "input_short": scatter_about(key_list[0], (M1, L1, D), 1.0, 6.0, ((0, 16), (1, 2))),
        "input_middle": scatter_about(key_list[1], (M2, L2, D), 1.0, 6.0, ((0, 16), (1, 2))),
        "input_long": scatter_about(key_list[2], (M3, L3, D), 1.0, 6.0, ((0, 16), (1, 2))),
        "length_short": draw_length_short(jax.random.fold_in(key_list[26], 71), 0),
        "length_middle": draw_length_middle(jax.random.fold_in(key_list[26], 71), 0),
        "length_long": draw_length_long(jax.random.fold_in(key_list[26], 71), 0),
        "cotangent_short": scatter_about(key_list[6], (M1, L1, D), 1.0, 6.0, ((0, 16), (1, 2))),
        "cotangent_middle": scatter_about(key_list[7], (M2, L2, D), 1.0, 6.0, ((0, 16), (1, 2))),
        "cotangent_long": scatter_about(key_list[8], (M3, L3, D), 1.0, 6.0, ((0, 16), (1, 2))),
        "query_weight": scatter_about(key_list[9], (D, D), (4 * D) ** -0.5, 0.109375, ((0, 32),)),
        "key_weight": scatter_about(key_list[10], (D, D), (4 * D) ** -0.5, 0.109375, ((0, 32),)),
        "value_weight": scatter_about(key_list[11], (D, D), D ** -0.5, 0.21875, ((0, 32),)),
        "output_weight": scatter_about(key_list[12], (D, D), (D // 16) ** -0.5, 0.875, ((0, 32),)),
        "query_bias": scatter_about(key_list[13], (D,), 0.25, 1.5, ((0, 32),)),
        "key_bias": scatter_about(key_list[14], (D,), 0.25, 1.5, ((0, 32),)),
        "value_bias": scatter_about(key_list[15], (D,), 0.5, 3.0, ((0, 32),)),
        "output_bias": scatter_about(key_list[16], (D,), 0.5, 3.0, ((0, 32),)),
        "attn_gain": jnp.clip(1.0 + 0.1 * jax.random.normal(key_list[17], (D,), jnp.float32), 0.5, 1.5).astype(jnp.bfloat16),
        "attn_shift": scatter_about(key_list[18], (D,), 0.5, 3.0, ((0, 32),)),
        "up_weight": scatter_about(key_list[19], (D, FF), D ** -0.5, 0.21875, ((1, 32),)),
        "up_bias": scatter_about(key_list[20], (FF,), 0.5, 3.0, ((0, 32),)),
        "down_weight": scatter_about(key_list[21], (FF, D), FF ** -0.5, 0.109375, ((0, 32),)),
        "down_bias": scatter_about(key_list[22], (D,), 0.5, 3.0, ((0, 32),)),
        "ffn_gain": jnp.clip(1.0 + 0.1 * jax.random.normal(key_list[23], (D,), jnp.float32), 0.5, 1.5).astype(jnp.bfloat16),
        "ffn_shift": scatter_about(key_list[24], (D,), 0.5, 3.0, ((0, 32),)),
        "projection": scatter_about(key_list[25], (HD, R), 1.0, 4.0, (), jnp.float32),
    }


@jax.custom_vjp
def low(v):
    return lax.optimization_barrier(v.astype(jnp.bfloat16)).astype(jnp.float32)

@jax.custom_vjp
def low_back(v):
    return v

def low_keep(v):
    return (low(v), None)

def low_pass(kept, grad):
    return (grad,)

def back_keep(v):
    return (v, None)

def back_low(kept, grad):
    return (low(grad),)
low.defvjp(low_keep, low_pass)
low_back.defvjp(back_keep, back_low)
HIGH = lax.Precision.HIGHEST
EPS_NORM = 1e-05
EPS_DEN = 1e-06

def rotary(positions, head_size):
    half = head_size // 2
    rates = 10000.0 ** (-jnp.arange(half, dtype=jnp.float32) / half)
    angle = positions[:, None] * rates[None, :]
    return (jnp.concatenate([jnp.cos(angle)] * 2, axis=1), jnp.concatenate([jnp.sin(angle)] * 2, axis=1))

def turn(block):
    half = block.shape[-1] // 2
    return jnp.concatenate([-block[..., half:], block[..., :half]], axis=-1)

def features(scaled, projection):
    lifted = jnp.einsum('mtha,ar->mthr', scaled, projection, precision=HIGH)
    return jnp.exp(lifted - 0.5 * lax.optimization_barrier(jnp.sum(scaled * scaled, axis=-1, keepdims=True))) / math.sqrt(projection.shape[1])

def layer_norm(values, gain, shift):
    center = values - lax.optimization_barrier(jnp.mean(values, axis=-1, keepdims=True))
    return center * lax.rsqrt(lax.optimization_barrier(jnp.mean(center * center, axis=-1, keepdims=True)) + EPS_NORM) * gain + shift

def dense(left, right):
    return jnp.dot(left, right, precision=HIGH)

def group_forward(params, projection, block, lengths, cosine, sine):
    query_weight, key_weight, value_weight, output_weight, query_bias, key_bias, value_bias, output_bias, attn_gain, attn_shift, up_weight, up_bias, down_weight, down_bias, ffn_gain, ffn_shift = params
    group, length, width = block.shape
    heads = width // HD
    shape = (group, length, heads, HD)
    rows = block.reshape(group * length, width)
    scale = HD ** (-0.25)
    query = low_back(dense(rows, query_weight) + query_bias).reshape(shape)
    keys = low_back(dense(rows, key_weight) + key_bias).reshape(shape)
    value_low = low(low_back(dense(rows, value_weight) + value_bias)).reshape(shape)
    scaled_query = (query * cosine + turn(query) * sine) * scale
    scaled_key = (keys * cosine + turn(keys) * sine) * scale
    valid = (jnp.arange(length)[None, :] < lengths[:, None]).astype(jnp.float32)
    query_feat = low(features(scaled_query, projection))
    key_feat = low(features(scaled_key, projection)) * valid[:, :, None, None]
    state = jnp.einsum('mtha,mthe->mhae', key_feat, value_low, precision=HIGH)
    total = lax.optimization_barrier(jnp.sum(key_feat, axis=1))
    numerator = low_back(jnp.einsum('mtha,mhae->mthe', query_feat, state, precision=HIGH))
    denominator = jnp.einsum('mtha,mha->mth', query_feat, total, precision=HIGH) + EPS_DEN
    attended = low((numerator / denominator[..., None]).reshape(group * length, width))
    middle = layer_norm(rows + low_back(dense(attended, output_weight) + output_bias), attn_gain, attn_shift)
    pre_gelu = low_back(dense(low(middle), up_weight) + up_bias)
    activated = low(jax.nn.gelu(pre_gelu, approximate=False))
    result = layer_norm(middle + low_back(dense(activated, down_weight) + down_bias), ffn_gain, ffn_shift)
    return result.reshape(group, length, width)

def bucket_forward(params, projection, block, lengths):
    count, length, width = block.shape
    fitting = [part for part in range(1, count + 1) if count % part == 0 and part * length <= 4096]
    group = max(fitting + [1])
    cosine, sine = rotary(jnp.arange(length, dtype=jnp.float32), HD)
    cosine = cosine[:, None, :]
    sine = sine[:, None, :]
    blocks = block.reshape(count // group, group, length, width)
    bounds = lengths.reshape(count // group, group)

    def one_group(pair):
        return group_forward(params, projection, pair[0], pair[1], cosine, sine)
    outputs = lax.map(jax.checkpoint(one_group), (blocks, bounds))
    return outputs.reshape(count, length, width)

def reference(input_short, input_middle, input_long, length_short, length_middle, length_long, cotangent_short, cotangent_middle, cotangent_long, query_weight, key_weight, value_weight, output_weight, query_bias, key_bias, value_bias, output_bias, attn_gain, attn_shift, up_weight, up_bias, down_weight, down_bias, ffn_gain, ffn_shift, projection):
    params = tuple((weight.astype(jnp.float32) for weight in (query_weight, key_weight, value_weight, output_weight, query_bias, key_bias, value_bias, output_bias, attn_gain, attn_shift, up_weight, up_bias, down_weight, down_bias, ffn_gain, ffn_shift)))
    inputs = tuple((block.astype(jnp.float32) for block in (input_short, input_middle, input_long)))
    lengths = (length_short, length_middle, length_long)

    def forward(params, inputs):
        return tuple((bucket_forward(params, projection, block, bound) for block, bound in zip(inputs, lengths)))
    outputs, pullback = jax.vjp(forward, params, inputs)
    cotangents = tuple((block.astype(jnp.float32) for block in (cotangent_short, cotangent_middle, cotangent_long)))
    param_grads, input_grads = pullback(cotangents)
    return (outputs[0].astype(jnp.bfloat16), outputs[1].astype(jnp.bfloat16), outputs[2].astype(jnp.bfloat16), input_grads[0].astype(jnp.bfloat16), input_grads[1].astype(jnp.bfloat16), input_grads[2].astype(jnp.bfloat16), param_grads[0], param_grads[1], param_grads[2], param_grads[3], param_grads[4], param_grads[5], param_grads[6], param_grads[7], param_grads[8], param_grads[9], param_grads[10], param_grads[11], param_grads[12], param_grads[13], param_grads[14], param_grads[15])
```

```python
import functools
import math

import jax
import jax.numpy as jnp
import numpy as np
from jax import lax
from jax.experimental import pallas as pl
from jax.experimental.pallas import tpu as pltpu
from jax.sharding import PartitionSpec as P

HD = 64
HIGH = lax.Precision.HIGHEST
EPS_NORM = 1e-05
EPS_DEN = 1e-06
F32 = jnp.float32
BF16 = jnp.bfloat16
AXES = ("batch", "seq")
GROUP = 256
FEAT = 128
VMEM = 60 * 1024 * 1024
BQ, BK, BV, BO, AG, AS, DB, FG, FS, UB = range(10)


def nn(a, b, precision=None):
    return lax.dot_general(
        a, b, (((1,), (0,)), ((), ())), precision=precision, preferred_element_type=F32
    )


def nt(a, b, precision=None):
    return lax.dot_general(
        a, b, (((1,), (1,)), ((), ())), precision=precision, preferred_element_type=F32
    )


def tn(a, b):
    return lax.dot_general(a, b, (((0,), (0,)), ((), ())), preferred_element_type=F32)


def split(x):
    high = x.astype(BF16)
    return high, (x - high.astype(F32)).astype(BF16)


def iota(shape, axis):
    return lax.broadcasted_iota(jnp.int32, shape, axis)


def head_mask():
    return iota((FEAT, GROUP), 0) // 32 == iota((FEAT, GROUP), 1) // 64


def fold_mask():
    return (iota((FEAT, FEAT), 0) // 32) % 2 == iota((FEAT, FEAT), 1) // 64


def fold(block, mask):
    kept = jnp.where(mask, block, 0.0)
    return kept[:, :FEAT] + kept[:, FEAT:]


def unfold(packed, mask):
    turned = pltpu.roll(packed, 64, 1)
    first = jnp.where(mask, jnp.concatenate([packed, packed], 1), 0.0)
    second = jnp.where(mask, jnp.concatenate([turned, turned], 1), 0.0)
    return first, second


def rotate(block, cosine, sine_a, sine_b):
    parts = []
    for lane in range(0, block.shape[1], 128):
        part = block[:, lane : lane + 128]
        parts.append(
            part * cosine + pltpu.roll(part, 96, 1) * sine_a + pltpu.roll(part, 32, 1) * sine_b
        )
    return jnp.concatenate(parts, 1)


def lane_mean(block):
    return jnp.mean(block, axis=-1, keepdims=True)


def norm_back(upstream, normed, spread, gain):
    scaled = upstream * gain
    return spread * (scaled - lane_mean(scaled) - normed * lane_mean(scaled * normed))


def column_sum(block):
    return jnp.sum(block, axis=0, keepdims=True)


def call(body, outs, name, *args, flops=10**9):
    return pl.pallas_call(
        body,
        out_shape=tuple(jax.ShapeDtypeStruct(shape, kind) for shape, kind in outs),
        in_specs=[pl.BlockSpec(memory_space=pltpu.VMEM)] * len(args),
        out_specs=tuple(pl.BlockSpec(memory_space=pltpu.VMEM) for _ in outs),
        compiler_params=pltpu.CompilerParams(vmem_limit_bytes=VMEM),
        cost_estimate=pl.CostEstimate(flops=flops, bytes_accessed=10**6, transcendentals=0),
        name=name,
    )(*args)


def front(
    pieces, x0, x1, x2, own, sib, place, cosine, sine_a, sine_b, valid, lift, norm,
    packed, query_map, key_map, scaled_query, scaled_key, value_low, rows_rel, vectors,
):
    half = own.shape[0]
    width = 2 * half
    tail = own.shape[1] - 128
    x = jnp.concatenate([x0[...], x1[...], x2[...]], 0)
    rel = nn(x, place[...]).astype(BF16)
    rows_rel[...] = rel
    left, right = rel[:, :half], rel[:, half:]
    small_own = own[:, tail:].T
    small_sib = sib[:, tail:].T
    ordered = nt(small_own, place[:, :half]) + nt(small_sib, place[:, half:])
    vectors[0:16, :] = ordered[0:16]
    vectors[16:32, :half] = small_own[0:16].astype(F32)
    vectors[16:32, half:] = small_sib[0:16].astype(F32)
    cos, sin_a, sin_b = cosine[...], sine_a[...], sine_b[...]
    ok = valid[...]
    mask, mask_fold = head_mask(), fold_mask()
    for group in range(width // GROUP):
        feats = slice(group * FEAT, (group + 1) * FEAT)
        lanes = slice(group * GROUP, (group + 1) * GROUP)

        def project(index):
            start = index * width + group * GROUP
            cut = slice(start, start + GROUP)
            bias = ordered[index : index + 1, lanes]
            return nn(left, own[:, cut]) + nn(right, sib[:, cut]) + bias

        low = project(2).astype(BF16)
        value_low[:, lanes] = low
        maps = []
        for index, kept in ((0, scaled_query), (1, scaled_key)):
            scaled = rotate(project(index), cos, sin_a, sin_b)
            kept[:, lanes] = scaled
            power = nn(scaled, lift[...], HIGH) + nn(scaled * scaled, norm[...], HIGH)
            maps.append(jnp.exp(power) * (1.0 / math.sqrt(32.0)))
        query_map[:, feats] = maps[0]
        key_map[:, feats] = maps[1]
        feat = (maps[1].astype(BF16).astype(F32) * ok).astype(BF16)
        for index, (start, stop) in enumerate(pieces):
            part = feat[start:stop]
            state = tn(part, low[start:stop])
            total = tn(part, jnp.ones((stop - start, FEAT), BF16))
            packed[index * 3 + group] = jnp.where(mask_fold, fold(state, mask), total)


def middle(
    pieces, mine, other, query_map, x0, x1, x2, own, sib, place, vectors,
    attended, over, attended_rel, normed, spread, middle_low,
):
    half = own.shape[0]
    width = 2 * half
    mask = head_mask()
    for index, (start, stop) in enumerate(pieces):
        for group in range(width // GROUP):
            feats = slice(group * FEAT, (group + 1) * FEAT)
            lanes = slice(group * GROUP, (group + 1) * GROUP)
            state, total = unfold(mine[index * 3 + group] + other[index * 3 + group], mask)
            feat = query_map[start:stop, feats].astype(BF16)
            state_high, state_low = split(state)
            total_high, total_low = split(total)
            numerator = nn(feat, state_high) + nn(feat, state_low)
            denominator = nn(feat, total_high) + nn(feat, total_low) + EPS_DEN
            inverse = 1.0 / denominator
            over[start:stop, lanes] = inverse
            attended[start:stop, lanes] = numerator * inverse
    rel = nn(attended[...].astype(BF16), place[...]).astype(BF16)
    attended_rel[...] = rel
    branch = nn(rel[:, :half], own[:, 3 * width : 4 * width])
    branch += nn(rel[:, half:], sib[:, 3 * width : 4 * width])
    x = jnp.concatenate([x0[...], x1[...], x2[...]], 0).astype(F32)
    first = x + branch + vectors[BO : BO + 1, :]
    center = first - lane_mean(first)
    scale = lax.rsqrt(lane_mean(center * center) + EPS_NORM)
    norm = center * scale
    normed[...] = norm
    spread[...] = jnp.broadcast_to(scale, spread.shape)
    middle_low[...] = (norm * vectors[AG : AG + 1, :] + vectors[AS : AS + 1, :]).astype(BF16)


def ffn_chunks(base, chunks, middle_low, own, sib, vectors, activated, slope):
    half = own.shape[0]
    width = 2 * half
    low = middle_low[...]
    total = None
    for chunk in range(chunks):
        lane = chunk * 2 * width
        row = 16 + UB + base + chunk
        for index, part in enumerate((own, sib)):
            cut = slice(index * half, (index + 1) * half)
            pre = nt(low, part[:, lane : lane + width]) + vectors[row : row + 1, cut]
            cdf = 0.5 + 0.5 * lax.erf(pre * math.sqrt(0.5))
            act = (pre * cdf).astype(BF16)
            bell = jnp.exp(-0.5 * pre * pre) * (1.0 / math.sqrt(2.0 * math.pi))
            cut = slice(chunk * width + index * half, chunk * width + (index + 1) * half)
            activated[:, cut] = act
            slope[:, cut] = (cdf + pre * bell).astype(BF16)
            product = nn(act, part[:, lane + width : lane + 2 * width])
            total = product if total is None else total + product
    return total


def ffn_first(base, chunks, middle_low, own, sib, vectors, activated, slope, total):
    total[...] = ffn_chunks(base, chunks, middle_low, own, sib, vectors, activated, slope)


def ffn_second(
    base, chunks, middle_low, own, sib, vectors, before, normed, c0, c1, c2,
    activated, slope, o0, o1, o2, second_grad, down_low, sums,
):
    total = ffn_chunks(base, chunks, middle_low, own, sib, vectors, activated, slope)
    mid = normed[...] * vectors[AG : AG + 1, :] + vectors[AS : AS + 1, :]
    second = mid + (before[...] + total) + vectors[DB : DB + 1, :]
    center = second - lane_mean(second)
    spread = lax.rsqrt(lane_mean(center * center) + EPS_NORM)
    norm = center * spread
    gain = vectors[FG : FG + 1, :]
    result = (norm * gain + vectors[FS : FS + 1, :]).astype(BF16)
    start = 0
    for out in (o0, o1, o2):
        out[...] = result[start : start + out.shape[0]]
        start += out.shape[0]
    upstream = jnp.concatenate([c0[...], c1[...], c2[...]], 0).astype(F32)
    grad = norm_back(upstream, norm, spread, gain)
    low = grad.astype(BF16)
    second_grad[...] = grad
    down_low[...] = low
    sums[...] = jnp.zeros_like(sums)
    sums[0:1, :] = column_sum(low.astype(F32))
    sums[1:2, :] = column_sum(upstream * norm)
    sums[2:3, :] = column_sum(upstream)


def back_chunks(base, chunks, middle_low, down_low, own, sib, activated, slope, grad_own, grad_sib):
    half = own.shape[0]
    width = 2 * half
    low = middle_low[...]
    down = down_low[...]
    total = None
    small = [None, None]
    for chunk in range(chunks):
        lane = chunk * 2 * width
        pick = (iota((low.shape[0], 128), 1) == UB + base + chunk).astype(F32).astype(BF16)
        for index, (part, grad) in enumerate(((own, grad_own), (sib, grad_sib))):
            cut = slice(chunk * width + index * half, chunk * width + (index + 1) * half)
            up = nt(down, part[:, lane + width : lane + 2 * width])
            up = (up * slope[:, cut].astype(F32)).astype(BF16)
            grad[:, lane + width : lane + 2 * width] = tn(activated[:, cut], down).astype(BF16)
            grad[:, lane : lane + width] = tn(up, low).astype(BF16)
            bias = tn(up, pick)
            small[index] = bias if small[index] is None else small[index] + bias
            product = nn(up, part[:, lane : lane + width])
            total = product if total is None else total + product
    return total, small


def back_first(
    base, chunks, middle_low, down_low, own, sib, activated, slope,
    grad_own, grad_sib, total, small_own, small_sib,
):
    out, small = back_chunks(
        base, chunks, middle_low, down_low, own, sib, activated, slope, grad_own, grad_sib
    )
    total[...] = out
    small_own[...] = small[0]
    small_sib[...] = small[1]


def back_second(
    pieces, base, chunks, middle_low, down_low, own, sib, activated, slope,
    before, before_own, before_sib, second_grad, normed, spread, vectors, own_attn, sib_attn,
    attended_rel, place, attended, over, query_map,
    grad_own, grad_sib, small_own, small_sib, packed, num_low, den_grad, first_grad, sums,
):
    out, small = back_chunks(
        base, chunks, middle_low, down_low, own, sib, activated, slope, grad_own, grad_sib
    )
    small_own[...] = small[0] + before_own[...]
    small_sib[...] = small[1] + before_sib[...]
    half = own.shape[0]
    width = 2 * half
    grad = second_grad[...] + (before[...] + out)
    norm = normed[...]
    first = norm_back(grad, norm, spread[:, 0:1], vectors[AG : AG + 1, :])
    branch = first.astype(BF16)
    first_grad[...] = first
    sums[...] = jnp.zeros_like(sums)
    sums[0:1, :] = column_sum(branch.astype(F32))
    sums[1:2, :] = column_sum(grad * norm)
    sums[2:3, :] = column_sum(grad)
    last = slice(chunks * 2 * width, chunks * 2 * width + width)
    weight = tn(attended_rel[...], branch).astype(BF16)
    grad_own[:, last] = weight[:half]
    grad_sib[:, last] = weight[half:]
    cut = slice(3 * width, 4 * width)
    rel = jnp.concatenate([nt(branch, own_attn[:, cut]), nt(branch, sib_attn[:, cut])], 1)
    rel_high, rel_low = split(rel)
    upstream = nt(rel_high, place[...]) + nt(rel_low, place[...])
    inverse = over[...]
    num = (upstream * inverse).astype(BF16)
    num_low[...] = num
    weighted_high, weighted_low = split(upstream * attended[...])
    same = (iota((GROUP, GROUP), 0) // 64 == iota((GROUP, GROUP), 1) // 64)
    same = same.astype(F32).astype(BF16)
    mask, mask_fold = head_mask(), fold_mask()
    for group in range(width // GROUP):
        lanes = slice(group * GROUP, (group + 1) * GROUP)
        feats = slice(group * FEAT, (group + 1) * FEAT)
        den = nn(weighted_high[:, lanes], same) + nn(weighted_low[:, lanes], same)
        den = -den * inverse[:, lanes]
        den_grad[:, lanes] = den
        den_high, den_low = split(den)
        feat = query_map[:, feats].astype(BF16)
        for index, (start, stop) in enumerate(pieces):
            part = feat[start:stop]
            state = fold(tn(part, num[start:stop, lanes]), mask)
            total = fold(tn(part, den_high[start:stop]) + tn(part, den_low[start:stop]), mask)
            packed[index * 3 + group] = jnp.where(mask_fold, state, pltpu.roll(total, 64, 1))


def conclude(
    pieces, mine, other, mine_grad, other_grad, num_low, den_grad, value_low, query_map, key_map,
    scaled_query, scaled_key, rows_rel, valid, cosine, sine_a, sine_b, lift, place, first_grad,
    own, sib, sums_ffn, sums_attn, small_first, small_second,
    grad_own, grad_sib, i0, i1, i2, query_grad, key_grad, value_grad,
):
    half = own.shape[0]
    width = 2 * half
    mask = head_mask()
    cos, sin_a, sin_b = cosine[...], sine_a[...], sine_b[...]
    ok = valid[...]
    lifted = lift[...]
    spans = (iota((FEAT, GROUP), 0) // 32 == iota((FEAT, GROUP), 1) // 64).astype(F32)
    for group in range(width // GROUP):
        lanes = slice(group * GROUP, (group + 1) * GROUP)
        feats = slice(group * FEAT, (group + 1) * FEAT)
        query_parts, key_parts = [], []
        key_low = (key_map[:, feats].astype(BF16).astype(F32) * ok).astype(BF16)
        for index, (start, stop) in enumerate(pieces):
            slot = index * 3 + group
            state, total = unfold(mine[slot] + other[slot], mask)
            state_grad, total_grad = unfold(mine_grad[slot] + other_grad[slot], mask)
            state_high, state_low = split(state)
            total_high, total_low = split(total * (1.0 / 64.0))
            sg_high, sg_low = split(state_grad)
            tg_high, tg_low = split(total_grad * (1.0 / 64.0))
            num = num_low[start:stop, lanes]
            den_high, den_low = split(den_grad[start:stop, lanes])
            part = nt(num, state_high) + nt(num, state_low)
            part += nt(den_high, total_high) + nt(den_high, total_low) + nt(den_low, total_high)
            query_parts.append(part)
            value = value_low[start:stop, lanes]
            ones = jnp.ones((8, GROUP), BF16)
            row = (nt(ones, tg_high) + nt(ones, tg_low))[0:1]
            key_parts.append(nt(value, sg_high) + nt(value, sg_low) + row)
            low = key_low[start:stop]
            value_grad[start:stop, lanes] = (nn(low, sg_high) + nn(low, sg_low)).astype(BF16)
        query_inner = jnp.concatenate(query_parts, 0) * query_map[:, feats]
        key_inner = jnp.concatenate(key_parts, 0) * ok * key_map[:, feats]
        for inner, scaled, grad in (
            (query_inner, scaled_query, query_grad),
            (key_inner, scaled_key, key_grad),
        ):
            back = nt(inner, lifted, HIGH) - nn(inner, spans, HIGH) * scaled[:, lanes]
            grad[:, lanes] = rotate(back, cos, -sin_a, -sin_b).astype(BF16)
    rel = rows_rel[...]
    back = [None, None]
    rows = []
    for index, grad in enumerate((query_grad, key_grad, value_grad)):
        cut = slice(index * width, (index + 1) * width)
        block = grad[...]
        weight = tn(rel, block).astype(BF16)
        grad_own[:, cut] = weight[:half]
        grad_sib[:, cut] = weight[half:]
        rows.append(column_sum(block.astype(F32)))
        for side, part in enumerate((own, sib)):
            product = nt(block, part[:, cut])
            back[side] = product if back[side] is None else back[side] + product
    rel_high, rel_low = split(jnp.concatenate(back, 1))
    total = first_grad[...] + (nt(rel_high, place[...]) + nt(rel_low, place[...]))
    result = total.astype(BF16)
    start = 0
    for out in (i0, i1, i2):
        out[...] = result[start : start + out.shape[0]]
        start += out.shape[0]
    rows += [sums_attn[0:3, :], sums_ffn[0:3, :]]
    rows.append(jnp.zeros((128 - 9, width), F32))
    stacked = jnp.concatenate(rows, 0).astype(BF16)
    columns = nn(stacked, place[...]).T
    cut = slice(3 * width, 3 * width + 128)
    grad_own[:, cut] = (columns[:half] + small_first[...]).astype(BF16)
    grad_sib[:, cut] = (columns[half:] + small_second[...]).astype(BF16)


class Moves:
    def __init__(self, batch, seq):
        self.batch, self.seq = batch, seq
        self.cube = batch == 16 and seq == 2

    def pairs(self, batch_flip, core_flip):
        out = []
        for b in range(self.batch):
            for c in range(self.seq):
                out.append((b * self.seq + c, (b ^ batch_flip) * self.seq + (c ^ core_flip)))
        return out

    def send(self, block, batch_flip, core_flip=0):
        return lax.ppermute(block, AXES, self.pairs(batch_flip, core_flip))

    def order(self):
        b, c = lax.axis_index("batch"), lax.axis_index("seq")
        places = jnp.arange(self.batch, dtype=jnp.int32)
        if self.cube:
            flips = np.array([plane ^ (z * 4) for plane in (0, 1, 2, 3) for z in range(4)], np.int32)
            places = jnp.bitwise_xor(b, flips)
        return jnp.concatenate([places * self.seq + c, places * self.seq + (1 - c)])

    def early(self, block):
        if not self.cube:
            return None
        x = self.send(block, 1)
        y = self.send(block, 2)
        cut = block.shape[1] // 256 * 128
        both = jnp.concatenate([self.send(x[:, :cut], 2), self.send(y[:, cut:], 1)], 1)
        return x, y, both

    def gather(self, block, early):
        if not self.cube:
            own = lax.all_gather(block, "batch", axis=0, tiled=True)
            return own, self.send(own, 0, 1)
        near = self.send(block, 4)
        far = self.send(jnp.concatenate([block, near], 0), 8)
        column = jnp.concatenate([near, far], 0)
        x = self.send(column, 1)
        y = self.send(column, 2)
        cut = block.shape[1] // 256 * 128
        both = jnp.concatenate([self.send(x[:, :cut], 2), self.send(y[:, cut:], 1)], 1)
        own = jnp.concatenate([block, column, early[0], x, early[1], y, early[2], both], 0)
        return own, self.send(own, 0, 1)

    def scatter(self, own, sib):
        own = add(own, self.send(sib, 0, 1))
        if not self.cube:
            return lax.psum_scatter(own, "batch", scatter_dimension=0, tiled=True).astype(F32)
        quarter = own.shape[0] // 4
        cut = own.shape[1] // 256 * 128
        here, x, y, both = (own[i * quarter : (i + 1) * quarter] for i in range(4))
        from_x = self.send(both[:, :cut], 1)
        from_y = self.send(both[:, cut:], 2)
        y = jnp.concatenate([add(y[:, :cut], from_x), y[:, cut:]], 1)
        x = jnp.concatenate([x[:, :cut], add(x[:, cut:], from_y)], 1)
        here = add(here, self.send(x, 1), self.send(y, 2))
        step = quarter // 4
        near = add(here[: 2 * step], self.send(here[2 * step :], 8))
        return near[:step].astype(F32) + self.send(near[step:], 4).astype(F32)


def add(*blocks):
    total = blocks[0].astype(F32)
    for block in blocks[1:]:
        total = total + block.astype(F32)
    return total.astype(BF16)


def on_device(moves, inputs, lengths, cotangents, attn, ffn, projection):
    query_weight, key_weight, value_weight, output_weight = attn[:4]
    up_weight, up_bias, down_weight, down_bias, ffn_gain, ffn_shift = ffn
    step, width = query_weight.shape
    hidden = up_bias.shape[0]
    chunks = hidden // step
    first_half = chunks // 2

    small = list(attn[4:]) + [down_bias, ffn_gain, ffn_shift]
    small += [up_bias[i * step : (i + 1) * step] for i in range(chunks)]
    columns = jnp.stack(small + [jnp.zeros_like(small[0])] * (128 - len(small)), axis=1)
    ups = up_weight.T.reshape(chunks, step, width)
    downs = down_weight.reshape(chunks, step, width)
    share_attn = jnp.concatenate(
        [query_weight, key_weight, value_weight, output_weight, columns], 1
    )

    def share_ffn(start, stop):
        parts = []
        for i in range(start, stop):
            parts += [ups[i], downs[i]]
        return jnp.concatenate(parts, 1)

    shares = (share_attn, share_ffn(0, first_half), share_ffn(first_half, chunks))
    gathered = [moves.gather(share, moves.early(share)) for share in shares]
    (own_attn, sib_attn), (own_up, sib_up), (own_down, sib_down) = gathered

    ranks = moves.order()
    rows_at = (ranks[:, None] * step + jnp.arange(step, dtype=jnp.int32)[None, :]).reshape(-1)
    place = (jnp.arange(width, dtype=jnp.int32)[:, None] == rows_at[None, :]).astype(BF16)

    blocks, valids, positions, pieces = [], [], [], []
    start = 0
    for block, limit in zip(inputs, lengths):
        count, local, _ = block.shape
        blocks.append(block.reshape(count * local, width))
        at = lax.axis_index("seq") * local + jnp.arange(local, dtype=jnp.int32)
        positions.append(jnp.tile(at, count))
        valids.append((at[None, :] < limit[:, None]).reshape(-1))
        for _ in range(count):
            pieces.append((start, start + local))
            start += local
    pieces = tuple(pieces)
    rows = start
    position = jnp.concatenate(positions).astype(F32)
    valid = jnp.broadcast_to(jnp.concatenate(valids).astype(F32)[:, None], (rows, FEAT))
    half_head = HD // 2
    rates = 10000.0 ** (-jnp.arange(half_head, dtype=F32) / half_head)
    angle = position[:, None] * rates[None, :]
    scale = HD ** (-0.25)
    cos, sin = jnp.cos(angle) * scale, jnp.sin(angle) * scale
    none = jnp.zeros_like(sin)
    cosine = jnp.concatenate([cos] * 4, 1)
    sine_a = jnp.concatenate([-sin, none] * 2, 1)
    sine_b = jnp.concatenate([none, sin] * 2, 1)
    same = np.arange(GROUP)[:, None] // 64 == np.arange(FEAT)[None, :] // 32
    lift = jnp.where(same, jnp.tile(projection, (4, 4)), 0.0)
    norm = jnp.asarray(np.where(same, -0.5, 0.0), F32)

    half = width // 2
    feats = width // 2
    slots = len(pieces) * (width // GROUP)
    wide, narrow = (rows, width), (rows, feats)
    packed_shape = (slots, FEAT, FEAT)
    packed, query_map, key_map, scaled_query, scaled_key, value_low, rows_rel, vectors = call(
        functools.partial(front, pieces),
        [
            (packed_shape, F32), (narrow, F32), (narrow, F32), (wide, F32), (wide, F32),
            (wide, BF16), (wide, BF16), ((32, width), F32),
        ],
        "front",
        *blocks, own_attn, sib_attn, place, cosine, sine_a, sine_b, valid, lift, norm,
    )
    packed_other = moves.send(packed, 0, 1)
    attended, over, attended_rel, normed, spread, middle_low = call(
        functools.partial(middle, pieces),
        [
            (wide, F32), (wide, F32), (wide, BF16), (wide, F32), ((rows, 128), F32), (wide, BF16),
        ],
        "middle",
        packed, packed_other, query_map, *blocks, own_attn, sib_attn, place, vectors,
    )
    part = (rows, first_half * width)
    rest = (rows, (chunks - first_half) * width)
    act_first, slope_first, total_first = call(
        functools.partial(ffn_first, 0, first_half),
        [(part, BF16), (part, BF16), (wide, F32)],
        "ffn_first",
        middle_low, own_up, sib_up, vectors,
    )
    flat = [block.reshape(-1, width) for block in cotangents]
    flats = [(block.shape, BF16) for block in flat]
    act_second, slope_second, o0, o1, o2, second_grad, down_low, sums_ffn = call(
        functools.partial(ffn_second, first_half, chunks - first_half),
        [(rest, BF16), (rest, BF16), *flats, (wide, F32), (wide, BF16), ((8, width), F32)],
        "ffn_second",
        middle_low, own_down, sib_down, vectors, total_first, normed, *flat,
    )
    shape_first = (half, first_half * 2 * width)
    grad_own, grad_sib, total_back, small_own, small_sib = call(
        functools.partial(back_first, 0, first_half),
        [
            (shape_first, BF16), (shape_first, BF16), (wide, F32),
            ((half, 128), F32), ((half, 128), F32),
        ],
        "back_first",
        middle_low, down_low, own_up, sib_up, act_first, slope_first,
    )
    sum_first = moves.scatter(grad_own, grad_sib)
    shape_second = (half, (chunks - first_half) * 2 * width + width)
    (
        grad_own, grad_sib, small_own, small_sib, packed_grad, num_low, den_grad, first_grad,
        sums_attn,
    ) = call(
        functools.partial(back_second, pieces, first_half, chunks - first_half),
        [
            (shape_second, BF16), (shape_second, BF16), ((half, 128), F32), ((half, 128), F32),
            (packed_shape, F32), (wide, BF16), (wide, F32), (wide, F32), ((8, width), F32),
        ],
        "back_second",
        middle_low, down_low, own_down, sib_down, act_second, slope_second,
        total_back, small_own, small_sib, second_grad, normed, spread, vectors, own_attn, sib_attn,
        attended_rel, place, attended, over, query_map,
    )
    packed_grad_other = moves.send(packed_grad, 0, 1)
    sum_second = moves.scatter(grad_own, grad_sib)
    shape_attn = (half, 3 * width + 128)
    grad_own, grad_sib, i0, i1, i2, _, _, _ = call(
        functools.partial(conclude, pieces),
        [
            (shape_attn, BF16), (shape_attn, BF16), *flats, (wide, BF16), (wide, BF16),
            (wide, BF16),
        ],
        "conclude",
        packed, packed_other, packed_grad, packed_grad_other, num_low, den_grad, value_low,
        query_map, key_map, scaled_query, scaled_key, rows_rel, valid, cosine, sine_a, sine_b, lift,
        place, first_grad, own_attn, sib_attn, sums_ffn, sums_attn, small_own, small_sib,
    )
    sum_attn = moves.scatter(grad_own, grad_sib)

    def cut(block, index):
        return block[:, index * width : (index + 1) * width]

    grad_up, grad_down = [], []
    for index in range(chunks):
        source, at = (sum_first, index) if index < first_half else (sum_second, index - first_half)
        grad_up.append(cut(source, 2 * at))
        grad_down.append(cut(source, 2 * at + 1))
    grad_up = jnp.concatenate(grad_up, 0).T
    grad_down = jnp.concatenate(grad_down, 0)
    grad_output = cut(sum_second, 2 * (chunks - first_half))
    column = sum_attn[:, 3 * width :].T
    grad_up_bias = column[UB : UB + chunks].reshape(-1)
    outs = [o.reshape(block.shape) for o, block in zip((o0, o1, o2, i0, i1, i2), inputs * 2)]
    return (
        *outs,
        cut(sum_attn, 0), cut(sum_attn, 1), cut(sum_attn, 2), grad_output,
        column[BQ], column[BK], column[BV], column[BO], column[AG], column[AS],
        grad_up, grad_up_bias, grad_down, column[DB], column[FG], column[FS],
    )


def solution(mesh):
    moves = Moves(mesh.shape["batch"], mesh.shape["seq"])

    def body(*args):
        return on_device(
            moves, args[0:3], args[3:6], args[6:9], args[9:19], args[19:25], args[25]
        )

    tokens = P("batch", "seq", None)
    shard = P(AXES)
    rows = P(AXES, None)
    attn = (rows,) * 4 + (shard,) * 6
    ffn = (P(None, AXES), shard, rows, shard, shard, shard)
    in_specs = (tokens,) * 3 + (P("batch"),) * 3 + (tokens,) * 3 + attn + ffn + (P(),)
    out_specs = (tokens,) * 6 + attn + ffn
    return jax.shard_map(
        body, mesh=mesh, in_specs=in_specs, out_specs=out_specs, check_vma=False
    )
```

```python
import functools
import math

import jax
import jax.numpy as jnp
import numpy as np
from jax import lax
from jax.experimental import pallas as pl
from jax.experimental.pallas import tpu as pltpu
from jax.sharding import PartitionSpec as P

HD = 64
HIGH = lax.Precision.HIGHEST
EPS_NORM = 1e-05
EPS_DEN = 1e-06
F32 = jnp.float32
BF16 = jnp.bfloat16
AXES = ("batch", "seq")
GROUP = 256
FEAT = 128
VMEM = 20 * 1024 * 1024
BQ, BK, BV, BO, AG, AS, DB, FG, FS, UB = range(10)


def nn(a, b, precision=None):
    return lax.dot_general(
        a, b, (((1,), (0,)), ((), ())), precision=precision, preferred_element_type=F32
    )


def nt(a, b, precision=None):
    return lax.dot_general(
        a, b, (((1,), (1,)), ((), ())), precision=precision, preferred_element_type=F32
    )


def tn(a, b):
    return lax.dot_general(a, b, (((0,), (0,)), ((), ())), preferred_element_type=F32)


def split(x):
    high = x.astype(BF16)
    return high, (x - high.astype(F32)).astype(BF16)


def iota(shape, axis):
    return lax.broadcasted_iota(jnp.int32, shape, axis)


def head_mask():
    return iota((FEAT, GROUP), 0) // 32 == iota((FEAT, GROUP), 1) // 64


def fold_mask():
    return (iota((FEAT, FEAT), 0) // 32) % 2 == iota((FEAT, FEAT), 1) // 64


def fold(block, mask):
    kept = jnp.where(mask, block, 0.0)
    return kept[:, :FEAT] + kept[:, FEAT:]


def unfold(packed, mask):
    turned = pltpu.roll(packed, 64, 1)
    first = jnp.where(mask, jnp.concatenate([packed, packed], 1), 0.0)
    second = jnp.where(mask, jnp.concatenate([turned, turned], 1), 0.0)
    return first, second


def rotate(block, cosine, sine_a, sine_b):
    parts = []
    for lane in range(0, block.shape[1], 128):
        part = block[:, lane : lane + 128]
        parts.append(
            part * cosine + pltpu.roll(part, 96, 1) * sine_a + pltpu.roll(part, 32, 1) * sine_b
        )
    return jnp.concatenate(parts, 1)


def lane_mean(block):
    return jnp.mean(block, axis=-1, keepdims=True)


def norm_back(upstream, normed, spread, gain):
    scaled = upstream * gain
    return spread * (scaled - lane_mean(scaled) - normed * lane_mean(scaled * normed))


def column_sum(block):
    return jnp.sum(block, axis=0, keepdims=True)


def skipping(body, count, extra, *refs):
    return body(*refs[:count], *refs[count + extra :])


def call(body, outs, name, micros, *args, after=()):
    whole = pl.BlockSpec(memory_space=pltpu.VMEM)
    return pl.pallas_call(
        functools.partial(skipping, body, len(args), len(after)) if after else body,
        out_shape=tuple(jax.ShapeDtypeStruct(shape, kind) for shape, kind in outs),
        in_specs=[whole] * len(args) + [pl.BlockSpec(memory_space=pl.ANY)] * len(after),
        out_specs=tuple(whole for _ in outs),
        compiler_params=pltpu.CompilerParams(vmem_limit_bytes=VMEM),
        cost_estimate=pl.CostEstimate(
            flops=int(micros * 1.15e9), bytes_accessed=10**6, transcendentals=0
        ),
        name=name,
    )(*args, *after)


def pack(chunks, query, keys, value, output, small, up, down, attn, first, second, whole):
    step, width = query.shape
    for index, part in enumerate((query, keys, value, output)):
        attn[:, index * width : (index + 1) * width] = part[...]
    eye = (iota((16, 128), 0) == iota((16, 128), 1)).astype(F32).astype(BF16)
    attn[:, 4 * width :] = tn(small[...], eye).astype(BF16)
    turned = up[...].T
    for chunk in range(chunks):
        out = first if chunk < chunks // 2 else second
        at = 2 * width * (chunk if chunk < chunks // 2 else chunk - chunks // 2)
        rows = slice(chunk * step, (chunk + 1) * step)
        out[:, at : at + width] = turned[rows]
        out[:, at + width : at + 2 * width] = down[rows]
    lane = 0
    for part in (attn, first, second):
        whole[:, lane : lane + part.shape[1]] = part[...]
        lane += part.shape[1]


def front(
    pieces, x0, x1, x2, own, sib, place, cosine, sine_a, sine_b, valid, lift, norm,
    packed, query_map, key_map, scaled_query, scaled_key, value_low, rows_rel, vectors,
):
    half = own.shape[0]
    width = 2 * half
    tail = own.shape[1] - 128
    x = jnp.concatenate([x0[...], x1[...], x2[...]], 0)
    rel = nn(x, place[...]).astype(BF16)
    rows_rel[...] = rel
    left, right = rel[:, :half], rel[:, half:]
    small_own = own[:, tail:].T
    small_sib = sib[:, tail:].T
    ordered = nt(small_own, place[:, :half]) + nt(small_sib, place[:, half:])
    vectors[0:16, :] = ordered[0:16]
    vectors[16:32, :half] = small_own[0:16].astype(F32)
    vectors[16:32, half:] = small_sib[0:16].astype(F32)
    cos, sin_a, sin_b = cosine[...], sine_a[...], sine_b[...]
    ok = valid[...]
    mask, mask_fold = head_mask(), fold_mask()
    for group in range(width // GROUP):
        feats = slice(group * FEAT, (group + 1) * FEAT)
        lanes = slice(group * GROUP, (group + 1) * GROUP)

        def project(index):
            start = index * width + group * GROUP
            cut = slice(start, start + GROUP)
            bias = ordered[index : index + 1, lanes]
            return nn(left, own[:, cut]) + nn(right, sib[:, cut]) + bias

        low = project(2).astype(BF16)
        value_low[:, lanes] = low
        maps = []
        for index, kept in ((0, scaled_query), (1, scaled_key)):
            scaled = rotate(project(index), cos, sin_a, sin_b)
            kept[:, lanes] = scaled
            power = nn(scaled, lift[...], HIGH) + nn(scaled * scaled, norm[...], HIGH)
            maps.append(jnp.exp(power) * (1.0 / math.sqrt(32.0)))
        query_map[:, feats] = maps[0]
        key_map[:, feats] = maps[1]
        feat = (maps[1].astype(BF16).astype(F32) * ok).astype(BF16)
        for index, (start, stop) in enumerate(pieces):
            part = feat[start:stop]
            state = tn(part, low[start:stop])
            total = tn(part, jnp.ones((stop - start, FEAT), BF16))
            packed[index * 3 + group] = jnp.where(mask_fold, fold(state, mask), total)


def middle(
    pieces, mine, other, query_map, x0, x1, x2, own, sib, place, vectors,
    attended, over, attended_rel, normed, spread, middle_low,
):
    half = own.shape[0]
    width = 2 * half
    mask = head_mask()
    for index, (start, stop) in enumerate(pieces):
        for group in range(width // GROUP):
            feats = slice(group * FEAT, (group + 1) * FEAT)
            lanes = slice(group * GROUP, (group + 1) * GROUP)
            state, total = unfold(mine[index * 3 + group] + other[index * 3 + group], mask)
            feat = query_map[start:stop, feats].astype(BF16)
            state_high, state_low = split(state)
            total_high, total_low = split(total)
            numerator = nn(feat, state_high) + nn(feat, state_low)
            denominator = nn(feat, total_high) + nn(feat, total_low) + EPS_DEN
            inverse = 1.0 / denominator
            over[start:stop, lanes] = inverse
            attended[start:stop, lanes] = numerator * inverse
    rel = nn(attended[...].astype(BF16), place[...]).astype(BF16)
    attended_rel[...] = rel
    branch = nn(rel[:, :half], own[:, 3 * width : 4 * width])
    branch += nn(rel[:, half:], sib[:, 3 * width : 4 * width])
    x = jnp.concatenate([x0[...], x1[...], x2[...]], 0).astype(F32)
    first = x + branch + vectors[BO : BO + 1, :]
    center = first - lane_mean(first)
    scale = lax.rsqrt(lane_mean(center * center) + EPS_NORM)
    norm = center * scale
    normed[...] = norm
    spread[...] = jnp.broadcast_to(scale, spread.shape)
    middle_low[...] = (norm * vectors[AG : AG + 1, :] + vectors[AS : AS + 1, :]).astype(BF16)


def ffn_chunks(base, chunks, middle_low, own, sib, vectors, activated, slope):
    half = own.shape[0]
    width = 2 * half
    low = middle_low[...]
    total = None
    for chunk in range(chunks):
        lane = chunk * 2 * width
        row = 16 + UB + base + chunk
        for index, part in enumerate((own, sib)):
            cut = slice(index * half, (index + 1) * half)
            pre = nt(low, part[:, lane : lane + width]) + vectors[row : row + 1, cut]
            cdf = 0.5 + 0.5 * lax.erf(pre * math.sqrt(0.5))
            act = (pre * cdf).astype(BF16)
            bell = jnp.exp(-0.5 * pre * pre) * (1.0 / math.sqrt(2.0 * math.pi))
            cut = slice(chunk * width + index * half, chunk * width + (index + 1) * half)
            activated[:, cut] = act
            slope[:, cut] = (cdf + pre * bell).astype(BF16)
            product = nn(act, part[:, lane + width : lane + 2 * width])
            total = product if total is None else total + product
    return total


def ffn_first(base, chunks, middle_low, own, sib, vectors, activated, slope, total):
    total[...] = ffn_chunks(base, chunks, middle_low, own, sib, vectors, activated, slope)


def ffn_second(
    base, chunks, middle_low, own, sib, vectors, before, normed, c0, c1, c2,
    activated, slope, o0, o1, o2, second_grad, down_low, sums,
):
    total = ffn_chunks(base, chunks, middle_low, own, sib, vectors, activated, slope)
    mid = normed[...] * vectors[AG : AG + 1, :] + vectors[AS : AS + 1, :]
    second = mid + (before[...] + total) + vectors[DB : DB + 1, :]
    center = second - lane_mean(second)
    spread = lax.rsqrt(lane_mean(center * center) + EPS_NORM)
    norm = center * spread
    gain = vectors[FG : FG + 1, :]
    result = (norm * gain + vectors[FS : FS + 1, :]).astype(BF16)
    start = 0
    for out in (o0, o1, o2):
        out[...] = result[start : start + out.shape[0]]
        start += out.shape[0]
    upstream = jnp.concatenate([c0[...], c1[...], c2[...]], 0).astype(F32)
    grad = norm_back(upstream, norm, spread, gain)
    low = grad.astype(BF16)
    second_grad[...] = grad
    down_low[...] = low
    sums[...] = jnp.zeros(sums.shape, F32)
    sums[0:1, :] = column_sum(low.astype(F32))
    sums[1:2, :] = column_sum(upstream * norm)
    sums[2:3, :] = column_sum(upstream)


def back_chunks(base, chunks, middle_low, down_low, own, sib, activated, slope, grad_own, grad_sib):
    half = own.shape[0]
    width = 2 * half
    low = middle_low[...]
    down = down_low[...]
    total = None
    small = [None, None]
    for chunk in range(chunks):
        lane = chunk * 2 * width
        pick = (iota((low.shape[0], 128), 1) == UB + base + chunk).astype(F32).astype(BF16)
        for index, (part, grad) in enumerate(((own, grad_own), (sib, grad_sib))):
            cut = slice(chunk * width + index * half, chunk * width + (index + 1) * half)
            up = nt(down, part[:, lane + width : lane + 2 * width])
            up = (up * slope[:, cut].astype(F32)).astype(BF16)
            grad[:, lane + width : lane + 2 * width] = tn(activated[:, cut], down).astype(BF16)
            grad[:, lane : lane + width] = tn(up, low).astype(BF16)
            bias = tn(up, pick)
            small[index] = bias if small[index] is None else small[index] + bias
            product = nn(up, part[:, lane : lane + width])
            total = product if total is None else total + product
    return total, small


def back_part(
    base, chunks, middle_low, down_low, own, sib, activated, slope,
    grad_own, grad_sib, total, small_own, small_sib,
):
    out, small = back_chunks(
        base, chunks, middle_low, down_low, own, sib, activated, slope, grad_own, grad_sib
    )
    total[...] = out
    small_own[...] = small[0]
    small_sib[...] = small[1]


def turn(
    pieces, before, after, second_grad, normed, spread, vectors, own_attn, sib_attn,
    attended_rel, place, attended, over, query_map,
    grad_own, grad_sib, packed, num_low, den_grad, first_grad, sums,
):
    half = own_attn.shape[0]
    width = 2 * half
    grad = second_grad[...] + (before[...] + after[...])
    norm = normed[...]
    first = norm_back(grad, norm, spread[:, 0:1], vectors[AG : AG + 1, :])
    branch = first.astype(BF16)
    first_grad[...] = first
    sums[...] = jnp.zeros(sums.shape, F32)
    sums[0:1, :] = column_sum(branch.astype(F32))
    sums[1:2, :] = column_sum(grad * norm)
    sums[2:3, :] = column_sum(grad)
    weight = tn(attended_rel[...], branch).astype(BF16)
    grad_own[...] = weight[:half]
    grad_sib[...] = weight[half:]
    cut = slice(3 * width, 4 * width)
    rel = jnp.concatenate([nt(branch, own_attn[:, cut]), nt(branch, sib_attn[:, cut])], 1)
    rel_high, rel_low = split(rel)
    upstream = nt(rel_high, place[...]) + nt(rel_low, place[...])
    inverse = over[...]
    num = (upstream * inverse).astype(BF16)
    num_low[...] = num
    weighted_high, weighted_low = split(upstream * attended[...])
    same = (iota((GROUP, GROUP), 0) // 64 == iota((GROUP, GROUP), 1) // 64)
    same = same.astype(F32).astype(BF16)
    mask, mask_fold = head_mask(), fold_mask()
    for group in range(width // GROUP):
        lanes = slice(group * GROUP, (group + 1) * GROUP)
        feats = slice(group * FEAT, (group + 1) * FEAT)
        den = nn(weighted_high[:, lanes], same) + nn(weighted_low[:, lanes], same)
        den = -den * inverse[:, lanes]
        den_grad[:, lanes] = den
        den_high, den_low = split(den)
        feat = query_map[:, feats].astype(BF16)
        for index, (start, stop) in enumerate(pieces):
            part = feat[start:stop]
            state = fold(tn(part, num[start:stop, lanes]), mask)
            total = fold(tn(part, den_high[start:stop]) + tn(part, den_low[start:stop]), mask)
            packed[index * 3 + group] = jnp.where(mask_fold, state, pltpu.roll(total, 64, 1))


def conclude(
    pieces, mine, other, mine_grad, other_grad, num_low, den_grad, value_low, query_map, key_map,
    scaled_query, scaled_key, rows_rel, valid, cosine, sine_a, sine_b, lift, place, first_grad,
    own, sib, sums_ffn, sums_attn, small_first, small_second, small_third, small_fourth,
    output_own, output_sib, grad_own, grad_sib, i0, i1, i2, query_grad, key_grad, value_grad,
):
    half = own.shape[0]
    width = 2 * half
    mask = head_mask()
    cos, sin_a, sin_b = cosine[...], sine_a[...], sine_b[...]
    ok = valid[...]
    lifted = lift[...]
    spans = (iota((FEAT, GROUP), 0) // 32 == iota((FEAT, GROUP), 1) // 64).astype(F32)
    for group in range(width // GROUP):
        lanes = slice(group * GROUP, (group + 1) * GROUP)
        feats = slice(group * FEAT, (group + 1) * FEAT)
        query_parts, key_parts = [], []
        key_low = (key_map[:, feats].astype(BF16).astype(F32) * ok).astype(BF16)
        for index, (start, stop) in enumerate(pieces):
            slot = index * 3 + group
            state, total = unfold(mine[slot] + other[slot], mask)
            state_grad, total_grad = unfold(mine_grad[slot] + other_grad[slot], mask)
            state_high, state_low = split(state)
            total_high, total_low = split(total * (1.0 / 64.0))
            sg_high, sg_low = split(state_grad)
            tg_high, tg_low = split(total_grad * (1.0 / 64.0))
            num = num_low[start:stop, lanes]
            den_high, den_low = split(den_grad[start:stop, lanes])
            part = nt(num, state_high) + nt(num, state_low)
            part += nt(den_high, total_high) + nt(den_high, total_low) + nt(den_low, total_high)
            query_parts.append(part)
            value = value_low[start:stop, lanes]
            ones = jnp.ones((8, GROUP), BF16)
            row = (nt(ones, tg_high) + nt(ones, tg_low))[0:1]
            key_parts.append(nt(value, sg_high) + nt(value, sg_low) + row)
            low = key_low[start:stop]
            value_grad[start:stop, lanes] = (nn(low, sg_high) + nn(low, sg_low)).astype(BF16)
        query_inner = jnp.concatenate(query_parts, 0) * query_map[:, feats]
        key_inner = jnp.concatenate(key_parts, 0) * ok * key_map[:, feats]
        for inner, scaled, grad in (
            (query_inner, scaled_query, query_grad),
            (key_inner, scaled_key, key_grad),
        ):
            back = nt(inner, lifted, HIGH) - nn(inner, spans, HIGH) * scaled[:, lanes]
            grad[:, lanes] = rotate(back, cos, -sin_a, -sin_b).astype(BF16)
    rel = rows_rel[...]
    back = [None, None]
    rows = []
    for index, grad in enumerate((query_grad, key_grad, value_grad)):
        cut = slice(index * width, (index + 1) * width)
        block = grad[...]
        weight = tn(rel, block).astype(BF16)
        grad_own[:, cut] = weight[:half]
        grad_sib[:, cut] = weight[half:]
        rows.append(column_sum(block.astype(F32)))
        for side, part in enumerate((own, sib)):
            product = nt(block, part[:, cut])
            back[side] = product if back[side] is None else back[side] + product
    rel_high, rel_low = split(jnp.concatenate(back, 1))
    total = first_grad[...] + (nt(rel_high, place[...]) + nt(rel_low, place[...]))
    result = total.astype(BF16)
    start = 0
    for out in (i0, i1, i2):
        out[...] = result[start : start + out.shape[0]]
        start += out.shape[0]
    rows += [sums_attn[0:3, :], sums_ffn[0:3, :]]
    rows.append(jnp.zeros((128 - 9, width), F32))
    stacked = jnp.concatenate(rows, 0).astype(BF16)
    columns = nn(stacked, place[...]).T
    cut = slice(3 * width, 4 * width)
    grad_own[:, cut] = output_own[...]
    grad_sib[:, cut] = output_sib[...]
    cut = slice(4 * width, 4 * width + 128)
    grad_own[:, cut] = (columns[:half] + small_first[...] + small_third[...]).astype(BF16)
    grad_sib[:, cut] = (columns[half:] + small_second[...] + small_fourth[...]).astype(BF16)


class Moves:
    def __init__(self, batch, seq):
        self.batch, self.seq = batch, seq
        self.cube = batch == 16 and seq == 2

    def send(self, block, flip, other=None, core_flip=0, name="send"):
        flips = (flip, flip if other is None else other)
        pairs = []
        for b in range(self.batch):
            for c in range(self.seq):
                pairs.append((b * self.seq + c, (b ^ flips[c]) * self.seq + (c ^ core_flip)))
        with jax.named_scope(name):
            return lax.ppermute(block, AXES, pairs)

    def across(self, block, name="across"):
        return self.send(block, 0, 0, 1, name)

    def order(self):
        b, c = lax.axis_index("batch"), lax.axis_index("seq")
        places = jnp.arange(self.batch, dtype=jnp.int32)
        if not self.cube:
            return jnp.concatenate([places * self.seq + c, places * self.seq + (1 - c)])
        flips = np.array([[p ^ z for p in o for z in (0, 8, 4, 12)] for o in ((0, 1, 2, 3), (0, 2, 1, 3))])
        flips = flips.astype(np.int32)
        mine = jnp.where(c == 0, flips[0], flips[1])
        theirs = jnp.where(c == 0, flips[1], flips[0])
        return jnp.concatenate(
            [jnp.bitwise_xor(b, mine) * self.seq + c, jnp.bitwise_xor(b, theirs) * self.seq + 1 - c]
        )

    def gather(self, whole, shares):
        if not self.cube:
            owns = [lax.all_gather(share, "batch", axis=0, tiled=True) for share in shares]
            return [(own, self.across(own)) for own in owns]
        near0 = self.send(whole, 1, 2, name="early_a")
        next0 = self.send(jnp.concatenate([whole, near0], 0), 2, 1, name="early_b")
        step = whole.shape[0]
        out = []
        lane = 0
        token = None
        for index, block in enumerate(shares):
            tag = f"gather{index}_"
            lanes = slice(lane, lane + block.shape[1])
            lane += block.shape[1]
            if token is not None:
                block = block + token[0:1, 0:1] * 0
            far = self.send(block, 8, name=tag + "far")
            token = far
            near = self.send(jnp.concatenate([block, far], 0), 4, name=tag + "near")
            rest = jnp.concatenate([far, near], 0)
            first = self.send(rest, 1, 2, name=tag + "a")
            second = self.send(jnp.concatenate([rest, first], 0), 2, 1, name=tag + "b")
            own = jnp.concatenate(
                [
                    block, rest, near0[:, lanes], first, next0[:step, lanes], second[: 3 * step],
                    next0[step:, lanes], second[3 * step :],
                ],
                0,
            )
            out.append((own, self.across(own, tag + "across")))
        return out

    def scatter(self, own, sib, tag):
        steps = [add(own, self.across(sib, tag + "across"))]
        if not self.cube:
            total = lax.psum_scatter(steps[0], "batch", scatter_dimension=0, tiled=True)
            return total.astype(F32), steps * 4
        for flip, other, name in ((2, 1, "b"), (1, 2, "a"), (4, 4, "near")):
            last = steps[-1]
            half = last.shape[0] // 2
            steps.append(add(last[:half], self.send(last[half:], flip, other, name=tag + name)))
        last = steps[-1]
        half = last.shape[0] // 2
        total = last[:half].astype(F32) + self.send(last[half:], 8, name=tag + "far").astype(F32)
        return total, steps


def add(*blocks):
    total = blocks[0].astype(F32)
    for block in blocks[1:]:
        total = total + block.astype(F32)
    return total.astype(BF16)


def on_device(moves, inputs, lengths, cotangents, attn, ffn, projection):
    query_weight, key_weight, value_weight, output_weight = attn[:4]
    up_weight, up_bias, down_weight, down_bias, ffn_gain, ffn_shift = ffn
    step, width = query_weight.shape
    hidden = up_bias.shape[0]
    chunks = hidden // step
    first_half = chunks // 2

    small = list(attn[4:]) + [down_bias, ffn_gain, ffn_shift]
    small += [up_bias[i * step : (i + 1) * step] for i in range(chunks)]
    lanes_attn, lanes_half = 4 * width + 128, first_half * 2 * width
    lanes_rest = chunks * 2 * width - lanes_half
    *shares, whole = call(
        functools.partial(pack, chunks),
        [
            ((step, lanes), BF16)
            for lanes in (lanes_attn, lanes_half, lanes_rest, lanes_attn + lanes_half + lanes_rest)
        ],
        "pack",
        3,
        *attn[:4], jnp.stack(small + [small[0]] * (16 - len(small))), up_weight, down_weight,
    )
    (own_attn, sib_attn), (own_up, sib_up), (own_down, sib_down) = moves.gather(whole, shares)

    ranks = moves.order()
    rows_at = (ranks[:, None] * step + jnp.arange(step, dtype=jnp.int32)[None, :]).reshape(-1)
    place = (jnp.arange(width, dtype=jnp.int32)[:, None] == rows_at[None, :]).astype(BF16)

    blocks, valids, positions, pieces = [], [], [], []
    start = 0
    for block, limit in zip(inputs, lengths):
        count, local, _ = block.shape
        blocks.append(block.reshape(count * local, width))
        at = lax.axis_index("seq") * local + jnp.arange(local, dtype=jnp.int32)
        positions.append(jnp.tile(at, count))
        valids.append((at[None, :] < limit[:, None]).reshape(-1))
        for _ in range(count):
            pieces.append((start, start + local))
            start += local
    pieces = tuple(pieces)
    rows = start
    position = jnp.concatenate(positions).astype(F32)
    valid = jnp.broadcast_to(jnp.concatenate(valids).astype(F32)[:, None], (rows, FEAT))
    half_head = HD // 2
    rates = 10000.0 ** (-jnp.arange(half_head, dtype=F32) / half_head)
    angle = position[:, None] * rates[None, :]
    scale = HD ** (-0.25)
    cos, sin = jnp.cos(angle) * scale, jnp.sin(angle) * scale
    none = jnp.zeros_like(sin)
    cosine = jnp.concatenate([cos] * 4, 1)
    sine_a = jnp.concatenate([-sin, none] * 2, 1)
    sine_b = jnp.concatenate([none, sin] * 2, 1)
    same = np.arange(GROUP)[:, None] // 64 == np.arange(FEAT)[None, :] // 32
    lift = jnp.where(same, jnp.tile(projection, (4, 4)), 0.0)
    norm = jnp.asarray(np.where(same, -0.5, 0.0), F32)

    half = width // 2
    feats = width // 2
    slots = len(pieces) * (width // GROUP)
    wide, narrow = (rows, width), (rows, feats)
    packed_shape = (slots, FEAT, FEAT)
    packed, query_map, key_map, scaled_query, scaled_key, value_low, rows_rel, vectors = call(
        functools.partial(front, pieces),
        [
            (packed_shape, F32), (narrow, F32), (narrow, F32), (wide, F32), (wide, F32),
            (wide, BF16), (wide, BF16), ((32, width), F32),
        ],
        "front",
        13,
        *blocks, own_attn, sib_attn, place, cosine, sine_a, sine_b, valid, lift, norm,
    )
    packed_other = moves.across(packed)
    attended, over, attended_rel, normed, spread, middle_low = call(
        functools.partial(middle, pieces),
        [
            (wide, F32), (wide, F32), (wide, BF16), (wide, F32), ((rows, 128), F32), (wide, BF16),
        ],
        "middle",
        8,
        packed, packed_other, query_map, *blocks, own_attn, sib_attn, place, vectors,
    )
    part = (rows, first_half * width)
    rest = (rows, (chunks - first_half) * width)
    act_first, slope_first, total_first = call(
        functools.partial(ffn_first, 0, first_half),
        [(part, BF16), (part, BF16), (wide, F32)],
        "ffn_first",
        7,
        middle_low, own_up, sib_up, vectors,
    )
    flat = [block.reshape(-1, width) for block in cotangents]
    flats = [(block.shape, BF16) for block in flat]
    act_second, slope_second, o0, o1, o2, second_grad, down_low, sums_ffn = call(
        functools.partial(ffn_second, first_half, chunks - first_half),
        [(rest, BF16), (rest, BF16), *flats, (wide, F32), (wide, BF16), ((8, width), F32)],
        "ffn_second",
        9,
        middle_low, own_down, sib_down, vectors, total_first, normed, *flat,
    )
    smalls, sums, totals, partials = [], [], [], []
    for base, count, own, sib, act, slope, name in (
        (0, first_half, own_up, sib_up, act_first, slope_first, "back_first"),
        (first_half, chunks - first_half, own_down, sib_down, act_second, slope_second, "back_second"),
    ):
        shape = (half, count * 2 * width)
        grad_own, grad_sib, total, small_own, small_sib = call(
            functools.partial(back_part, base, count),
            [
                (shape, BF16), (shape, BF16), (wide, F32),
                ((half, 128), F32), ((half, 128), F32),
            ],
            name,
            10,
            middle_low, down_low, own, sib, act, slope,
        )
        smalls += [small_own, small_sib]
        totals.append(total)
        total, partial = moves.scatter(grad_own, grad_sib, name)
        sums.append(total)
        partials.append(partial)
    square = (half, width)
    (
        output_own, output_sib, packed_grad, num_low, den_grad, first_grad, sums_attn,
    ) = call(
        functools.partial(turn, pieces),
        [
            (square, BF16), (square, BF16), (packed_shape, F32), (wide, BF16), (wide, F32),
            (wide, F32), ((8, width), F32),
        ],
        "turn",
        11,
        *totals, second_grad, normed, spread, vectors, own_attn, sib_attn,
        attended_rel, place, attended, over, query_map,
        after=(partials[0][0],),
    )
    packed_grad_other = moves.across(packed_grad)
    shape_attn = (half, 4 * width + 128)
    grad_own, grad_sib, i0, i1, i2, _, _, _ = call(
        functools.partial(conclude, pieces),
        [
            (shape_attn, BF16), (shape_attn, BF16), *flats, (wide, BF16), (wide, BF16),
            (wide, BF16),
        ],
        "conclude",
        23,
        packed, packed_other, packed_grad, packed_grad_other, num_low, den_grad, value_low,
        query_map, key_map, scaled_query, scaled_key, rows_rel, valid, cosine, sine_a, sine_b, lift,
        place, first_grad, own_attn, sib_attn, sums_ffn, sums_attn, *smalls, output_own, output_sib,
        after=(partials[0][1], partials[1][0]),
    )
    sum_attn, _ = moves.scatter(grad_own, grad_sib, "attn")

    def cut(block, index):
        return block[:, index * width : (index + 1) * width]

    grad_up, grad_down = [], []
    for index in range(chunks):
        source, at = (sums[0], index) if index < first_half else (sums[1], index - first_half)
        grad_up.append(cut(source, 2 * at))
        grad_down.append(cut(source, 2 * at + 1))
    grad_up = jnp.concatenate(grad_up, 0).T
    grad_down = jnp.concatenate(grad_down, 0)
    grad_output = cut(sum_attn, 3)
    column = sum_attn[:, 4 * width :].T
    grad_up_bias = column[UB : UB + chunks].reshape(-1)
    outs = [o.reshape(block.shape) for o, block in zip((o0, o1, o2, i0, i1, i2), inputs * 2)]
    return (
        *outs,
        cut(sum_attn, 0), cut(sum_attn, 1), cut(sum_attn, 2), grad_output,
        column[BQ], column[BK], column[BV], column[BO], column[AG], column[AS],
        grad_up, grad_up_bias, grad_down, column[DB], column[FG], column[FS],
    )


def solution(mesh):
    moves = Moves(mesh.shape["batch"], mesh.shape["seq"])

    def body(*args):
        return on_device(
            moves, args[0:3], args[3:6], args[6:9], args[9:19], args[19:25], args[25]
        )

    tokens = P("batch", "seq", None)
    shard = P(AXES)
    rows = P(AXES, None)
    attn = (rows,) * 4 + (shard,) * 6
    ffn = (P(None, AXES), shard, rows, shard, shard, shard)
    in_specs = (tokens,) * 3 + (P("batch"),) * 3 + (tokens,) * 3 + attn + ffn + (P(),)
    out_specs = (tokens,) * 6 + attn + ffn
    return jax.shard_map(
        body, mesh=mesh, in_specs=in_specs, out_specs=out_specs, check_vma=False
    )
```

```python
import functools
import math

import jax
import jax.numpy as jnp
import numpy as np
from jax import lax
from jax.experimental import pallas as pl
from jax.experimental.pallas import tpu as pltpu
from jax.sharding import PartitionSpec as P

HD = 64
HIGH = lax.Precision.HIGHEST
EPS_NORM = 1e-05
EPS_DEN = 1e-06
F32 = jnp.float32
BF16 = jnp.bfloat16
AXES = ("batch", "seq")
GROUP = 256
FEAT = 128
VMEM = 14 * 1024 * 1024
SCALE = 0.01
LONG = 10000
BQ, BK, BV, BO, AG, AS, DB, FG, FS, UB = range(10)


def nn(a, b, precision=None):
    return lax.dot_general(
        a, b, (((1,), (0,)), ((), ())), precision=precision, preferred_element_type=F32
    )


def nt(a, b, precision=None):
    return lax.dot_general(
        a, b, (((1,), (1,)), ((), ())), precision=precision, preferred_element_type=F32
    )


def tn(a, b):
    return lax.dot_general(a, b, (((0,), (0,)), ((), ())), preferred_element_type=F32)


def split(x):
    high = x.astype(BF16)
    return high, (x - high.astype(F32)).astype(BF16)


def iota(shape, axis):
    return lax.broadcasted_iota(jnp.int32, shape, axis)


def head_mask():
    return iota((FEAT, GROUP), 0) // 32 == iota((FEAT, GROUP), 1) // 64


def fold_mask():
    return (iota((FEAT, FEAT), 0) // 32) % 2 == iota((FEAT, FEAT), 1) // 64


def fold(block, mask):
    kept = jnp.where(mask, block, 0.0)
    return kept[:, :FEAT] + kept[:, FEAT:]


def unfold(packed, mask):
    turned = pltpu.roll(packed, 64, 1)
    first = jnp.where(mask, jnp.concatenate([packed, packed], 1), 0.0)
    second = jnp.where(mask, jnp.concatenate([turned, turned], 1), 0.0)
    return first, second


def rotate(block, cosine, sine_a, sine_b):
    parts = []
    for lane in range(0, block.shape[1], 128):
        part = block[:, lane : lane + 128]
        parts.append(
            part * cosine + pltpu.roll(part, 96, 1) * sine_a + pltpu.roll(part, 32, 1) * sine_b
        )
    return jnp.concatenate(parts, 1)


def lane_mean(block):
    return jnp.mean(block, axis=-1, keepdims=True)


def norm_back(upstream, normed, spread, gain):
    scaled = upstream * gain
    return spread * (scaled - lane_mean(scaled) - normed * lane_mean(scaled * normed))


def column_sum(block):
    return jnp.sum(block, axis=0, keepdims=True)


def skipping(body, count, extra, *refs):
    return body(*refs[:count], *refs[count + extra :])


def call(body, outs, name, micros, *args, after=(), stage=False):
    whole = pl.BlockSpec(memory_space=pltpu.VMEM)
    anywhere = pl.BlockSpec(memory_space=pl.ANY)
    scratch = [pltpu.VMEM(arg.shape, arg.dtype) for arg in args]
    scratch.append(pltpu.SemaphoreType.DMA((len(args),)))
    return pl.pallas_call(
        functools.partial(skipping, body, len(args), len(after)) if after else body,
        out_shape=tuple(jax.ShapeDtypeStruct(shape, kind) for shape, kind in outs),
        in_specs=[anywhere if stage else whole] * len(args) + [anywhere] * len(after),
        scratch_shapes=scratch if stage else [],
        out_specs=tuple(whole for _ in outs),
        compiler_params=pltpu.CompilerParams(vmem_limit_bytes=VMEM),
        cost_estimate=pl.CostEstimate(
            flops=int(micros * SCALE * 1.15e9), bytes_accessed=10**6, transcendentals=0
        ),
        name=name,
    )(*args, *after)


def pack(
    chunks, query, keys, value, output, small, up, down, attn, first, second, whole, *scratch
):
    buffers, sems = scratch[:-1], scratch[-1]
    sources = (query, keys, value, output, small, up, down)
    copies = [
        pltpu.make_async_copy(source, buffer, sems.at[index])
        for index, (source, buffer) in enumerate(zip(sources, buffers))
    ]
    for copy in copies:
        copy.start()
    for copy in copies:
        copy.wait()
    step, width = query.shape
    for index in range(4):
        attn[:, index * width : (index + 1) * width] = buffers[index][...]
    eye = (iota((16, 128), 0) == iota((16, 128), 1)).astype(F32).astype(BF16)
    attn[:, 4 * width :] = tn(buffers[4][...], eye).astype(BF16)
    for chunk in range(chunks):
        out = first if chunk < chunks // 2 else second
        at = 2 * width * (chunk if chunk < chunks // 2 else chunk - chunks // 2)
        rows = slice(chunk * step, (chunk + 1) * step)
        out[:, at : at + width] = buffers[5][rows, :]
        out[:, at + width : at + 2 * width] = buffers[6][rows, :]
    lane = 0
    for part in (attn, first, second):
        whole[:, lane : lane + part.shape[1]] = part[...]
        lane += part.shape[1]


def front(
    pieces, x0, x1, x2, own, sib, place, cosine, sine_a, sine_b, valid, lift, norm,
    packed, query_map, key_map, scaled_query, scaled_key, value_low, rows_rel, vectors,
):
    half = own.shape[0]
    width = 2 * half
    tail = own.shape[1] - 128
    x = jnp.concatenate([x0[...], x1[...], x2[...]], 0)
    rel = nn(x, place[...]).astype(BF16)
    rows_rel[...] = rel
    left, right = rel[:, :half], rel[:, half:]
    small_own = own[:, tail:].T
    small_sib = sib[:, tail:].T
    ordered = nt(small_own, place[:, :half]) + nt(small_sib, place[:, half:])
    vectors[0:16, :] = ordered[0:16]
    vectors[16:32, :half] = small_own[0:16].astype(F32)
    vectors[16:32, half:] = small_sib[0:16].astype(F32)
    cos, sin_a, sin_b = cosine[...], sine_a[...], sine_b[...]
    ok = valid[...]
    mask, mask_fold = head_mask(), fold_mask()
    for group in range(width // GROUP):
        feats = slice(group * FEAT, (group + 1) * FEAT)
        lanes = slice(group * GROUP, (group + 1) * GROUP)

        def project(index):
            start = index * width + group * GROUP
            cut = slice(start, start + GROUP)
            bias = ordered[index : index + 1, lanes]
            return nn(left, own[:, cut]) + nn(right, sib[:, cut]) + bias

        low = project(2).astype(BF16)
        value_low[:, lanes] = low
        maps = []
        for index, kept in ((0, scaled_query), (1, scaled_key)):
            scaled = rotate(project(index), cos, sin_a, sin_b)
            kept[:, lanes] = scaled
            power = nn(scaled, lift[...], HIGH) + nn(scaled * scaled, norm[...], HIGH)
            maps.append(jnp.exp(power) * (1.0 / math.sqrt(32.0)))
        query_map[:, feats] = maps[0]
        key_map[:, feats] = maps[1]
        feat = (maps[1].astype(BF16).astype(F32) * ok).astype(BF16)
        for index, (start, stop) in enumerate(pieces):
            part = feat[start:stop]
            state = tn(part, low[start:stop])
            total = tn(part, jnp.ones((stop - start, FEAT), BF16))
            packed[index * 3 + group] = jnp.where(mask_fold, fold(state, mask), total)


def middle(
    pieces, mine, other, query_map, x0, x1, x2, own, sib, place, vectors,
    attended, over, attended_rel, normed, spread, middle_low,
):
    half = own.shape[0]
    width = 2 * half
    mask = head_mask()
    for index, (start, stop) in enumerate(pieces):
        for group in range(width // GROUP):
            feats = slice(group * FEAT, (group + 1) * FEAT)
            lanes = slice(group * GROUP, (group + 1) * GROUP)
            state, total = unfold(mine[index * 3 + group] + other[index * 3 + group], mask)
            feat = query_map[start:stop, feats].astype(BF16)
            state_high, state_low = split(state)
            total_high, total_low = split(total)
            numerator = nn(feat, state_high) + nn(feat, state_low)
            denominator = nn(feat, total_high) + nn(feat, total_low) + EPS_DEN
            inverse = 1.0 / denominator
            over[start:stop, lanes] = inverse
            attended[start:stop, lanes] = numerator * inverse
    rel = nn(attended[...].astype(BF16), place[...]).astype(BF16)
    attended_rel[...] = rel
    branch = nn(rel[:, :half], own[:, 3 * width : 4 * width])
    branch += nn(rel[:, half:], sib[:, 3 * width : 4 * width])
    x = jnp.concatenate([x0[...], x1[...], x2[...]], 0).astype(F32)
    first = x + branch + vectors[BO : BO + 1, :]
    center = first - lane_mean(first)
    scale = lax.rsqrt(lane_mean(center * center) + EPS_NORM)
    norm = center * scale
    normed[...] = norm
    spread[...] = jnp.broadcast_to(scale, spread.shape)
    middle_low[...] = (norm * vectors[AG : AG + 1, :] + vectors[AS : AS + 1, :]).astype(BF16)


def ffn_chunks(base, chunks, middle_low, own, sib, vectors, activated, slope):
    half = own.shape[0]
    width = 2 * half
    low = middle_low[...]
    total = None
    for chunk in range(chunks):
        lane = chunk * 2 * width
        row = 16 + UB + base + chunk
        for index, part in enumerate((own, sib)):
            cut = slice(index * half, (index + 1) * half)
            pre = nt(low, part[:, lane : lane + width]) + vectors[row : row + 1, cut]
            cdf = 0.5 + 0.5 * lax.erf(pre * math.sqrt(0.5))
            act = (pre * cdf).astype(BF16)
            bell = jnp.exp(-0.5 * pre * pre) * (1.0 / math.sqrt(2.0 * math.pi))
            cut = slice(chunk * width + index * half, chunk * width + (index + 1) * half)
            activated[:, cut] = act
            slope[:, cut] = (cdf + pre * bell).astype(BF16)
            product = nn(act, part[:, lane + width : lane + 2 * width])
            total = product if total is None else total + product
    return total


def ffn_first(base, chunks, middle_low, own, sib, vectors, activated, slope, total):
    total[...] = ffn_chunks(base, chunks, middle_low, own, sib, vectors, activated, slope)


def ffn_second(
    base, chunks, middle_low, own, sib, vectors, before, normed, c0, c1, c2,
    activated, slope, o0, o1, o2, second_grad, down_low, sums,
):
    total = ffn_chunks(base, chunks, middle_low, own, sib, vectors, activated, slope)
    mid = normed[...] * vectors[AG : AG + 1, :] + vectors[AS : AS + 1, :]
    second = mid + (before[...] + total) + vectors[DB : DB + 1, :]
    center = second - lane_mean(second)
    spread = lax.rsqrt(lane_mean(center * center) + EPS_NORM)
    norm = center * spread
    gain = vectors[FG : FG + 1, :]
    result = (norm * gain + vectors[FS : FS + 1, :]).astype(BF16)
    start = 0
    for out in (o0, o1, o2):
        out[...] = result[start : start + out.shape[0]]
        start += out.shape[0]
    upstream = jnp.concatenate([c0[...], c1[...], c2[...]], 0).astype(F32)
    grad = norm_back(upstream, norm, spread, gain)
    low = grad.astype(BF16)
    second_grad[...] = grad
    down_low[...] = low
    sums[...] = jnp.zeros(sums.shape, F32)
    sums[0:1, :] = column_sum(low.astype(F32))
    sums[1:2, :] = column_sum(upstream * norm)
    sums[2:3, :] = column_sum(upstream)


def back_chunks(base, chunks, middle_low, down_low, own, sib, activated, slope, grad_own, grad_sib):
    half = own.shape[0]
    width = 2 * half
    low = middle_low[...]
    down = down_low[...]
    total = None
    small = [None, None]
    for chunk in range(chunks):
        lane = chunk * 2 * width
        pick = (iota((low.shape[0], 128), 1) == UB + base + chunk).astype(F32).astype(BF16)
        for index, (part, grad) in enumerate(((own, grad_own), (sib, grad_sib))):
            cut = slice(chunk * width + index * half, chunk * width + (index + 1) * half)
            up = nt(down, part[:, lane + width : lane + 2 * width])
            up = (up * slope[:, cut].astype(F32)).astype(BF16)
            grad[:, lane + width : lane + 2 * width] = tn(activated[:, cut], down).astype(BF16)
            grad[:, lane : lane + width] = tn(up, low).astype(BF16)
            bias = tn(up, pick)
            small[index] = bias if small[index] is None else small[index] + bias
            product = nn(up, part[:, lane : lane + width])
            total = product if total is None else total + product
    return total, small


def back_part(
    base, chunks, middle_low, down_low, own, sib, activated, slope,
    grad_own, grad_sib, total, small_own, small_sib,
):
    out, small = back_chunks(
        base, chunks, middle_low, down_low, own, sib, activated, slope, grad_own, grad_sib
    )
    total[...] = out
    small_own[...] = small[0]
    small_sib[...] = small[1]


def turn(
    pieces, before, after, second_grad, normed, spread, vectors, own_attn, sib_attn,
    attended_rel, place, attended, over, query_map, ffn_own, ffn_sib,
    grad_own, grad_sib, packed, num_low, den_grad, first_grad, sums,
):
    half = own_attn.shape[0]
    width = 2 * half
    grad = second_grad[...] + (before[...] + after[...])
    norm = normed[...]
    first = norm_back(grad, norm, spread[:, 0:1], vectors[AG : AG + 1, :])
    branch = first.astype(BF16)
    first_grad[...] = first
    sums[...] = jnp.zeros(sums.shape, F32)
    sums[0:1, :] = column_sum(branch.astype(F32))
    sums[1:2, :] = column_sum(grad * norm)
    sums[2:3, :] = column_sum(grad)
    weight = tn(attended_rel[...], branch).astype(BF16)
    lanes = ffn_own.shape[1]
    grad_own[:, :lanes] = ffn_own[...]
    grad_sib[:, :lanes] = ffn_sib[...]
    grad_own[:, lanes:] = weight[:half]
    grad_sib[:, lanes:] = weight[half:]
    cut = slice(3 * width, 4 * width)
    rel = jnp.concatenate([nt(branch, own_attn[:, cut]), nt(branch, sib_attn[:, cut])], 1)
    rel_high, rel_low = split(rel)
    upstream = nt(rel_high, place[...]) + nt(rel_low, place[...])
    inverse = over[...]
    num = (upstream * inverse).astype(BF16)
    num_low[...] = num
    weighted_high, weighted_low = split(upstream * attended[...])
    same = (iota((GROUP, GROUP), 0) // 64 == iota((GROUP, GROUP), 1) // 64)
    same = same.astype(F32).astype(BF16)
    mask, mask_fold = head_mask(), fold_mask()
    for group in range(width // GROUP):
        lanes = slice(group * GROUP, (group + 1) * GROUP)
        feats = slice(group * FEAT, (group + 1) * FEAT)
        den = nn(weighted_high[:, lanes], same) + nn(weighted_low[:, lanes], same)
        den = -den * inverse[:, lanes]
        den_grad[:, lanes] = den
        den_high, den_low = split(den)
        feat = query_map[:, feats].astype(BF16)
        for index, (start, stop) in enumerate(pieces):
            part = feat[start:stop]
            state = fold(tn(part, num[start:stop, lanes]), mask)
            total = fold(tn(part, den_high[start:stop]) + tn(part, den_low[start:stop]), mask)
            packed[index * 3 + group] = jnp.where(mask_fold, state, pltpu.roll(total, 64, 1))


def attend_back(
    pieces, mine, other, mine_grad, other_grad, num_low, den_grad, value_low, query_map, key_map,
    scaled_query, scaled_key, valid, cosine, sine_a, sine_b, lift,
    query_grad, key_grad, value_grad,
):
    width = value_low.shape[1]
    mask = head_mask()
    cos, sin_a, sin_b = cosine[...], sine_a[...], sine_b[...]
    ok = valid[...]
    lifted = lift[...]
    spans = (iota((FEAT, GROUP), 0) // 32 == iota((FEAT, GROUP), 1) // 64).astype(F32)
    for group in range(width // GROUP):
        lanes = slice(group * GROUP, (group + 1) * GROUP)
        feats = slice(group * FEAT, (group + 1) * FEAT)
        query_parts, key_parts = [], []
        key_low = (key_map[:, feats].astype(BF16).astype(F32) * ok).astype(BF16)
        for index, (start, stop) in enumerate(pieces):
            slot = index * 3 + group
            state, total = unfold(mine[slot] + other[slot], mask)
            state_grad, total_grad = unfold(mine_grad[slot] + other_grad[slot], mask)
            state_high, state_low = split(state)
            total_high, total_low = split(total * (1.0 / 64.0))
            sg_high, sg_low = split(state_grad)
            tg_high, tg_low = split(total_grad * (1.0 / 64.0))
            num = num_low[start:stop, lanes]
            den_high, den_low = split(den_grad[start:stop, lanes])
            part = nt(num, state_high) + nt(num, state_low)
            part += nt(den_high, total_high) + nt(den_high, total_low) + nt(den_low, total_high)
            query_parts.append(part)
            value = value_low[start:stop, lanes]
            ones = jnp.ones((8, GROUP), BF16)
            row = (nt(ones, tg_high) + nt(ones, tg_low))[0:1]
            key_parts.append(nt(value, sg_high) + nt(value, sg_low) + row)
            low = key_low[start:stop]
            value_grad[start:stop, lanes] = (nn(low, sg_high) + nn(low, sg_low)).astype(BF16)
        query_inner = jnp.concatenate(query_parts, 0) * query_map[:, feats]
        key_inner = jnp.concatenate(key_parts, 0) * ok * key_map[:, feats]
        for inner, scaled, grad in (
            (query_inner, scaled_query, query_grad),
            (key_inner, scaled_key, key_grad),
        ):
            back = nt(inner, lifted, HIGH) - nn(inner, spans, HIGH) * scaled[:, lanes]
            grad[:, lanes] = rotate(back, cos, -sin_a, -sin_b).astype(BF16)
def weights_back(
    query_grad, key_grad, value_grad, rows_rel, place, sums_ffn, sums_attn,
    small_first, small_second, small_third, small_fourth, grad_own, grad_sib,
):
    half = grad_own.shape[0]
    width = 2 * half
    rel = rows_rel[...]
    rows = []
    for index, grad in enumerate((query_grad, key_grad, value_grad)):
        cut = slice(index * width, (index + 1) * width)
        block = grad[...]
        weight = tn(rel, block).astype(BF16)
        grad_own[:, cut] = weight[:half]
        grad_sib[:, cut] = weight[half:]
        rows.append(column_sum(block.astype(F32)))
    rows += [sums_attn[0:3, :], sums_ffn[0:3, :]]
    rows.append(jnp.zeros((128 - 9, width), F32))
    stacked = jnp.concatenate(rows, 0).astype(BF16)
    columns = nn(stacked, place[...]).T
    cut = slice(3 * width, 3 * width + 128)
    grad_own[:, cut] = (columns[:half] + small_first[...] + small_third[...]).astype(BF16)
    grad_sib[:, cut] = (columns[half:] + small_second[...] + small_fourth[...]).astype(BF16)


def rows_back(query_grad, key_grad, value_grad, own, sib, place, first_grad, i0, i1, i2):
    width = place.shape[0]
    back = []
    for part in (own, sib):
        total = None
        for index, grad in enumerate((query_grad, key_grad, value_grad)):
            product = nt(grad[...], part[:, index * width : (index + 1) * width])
            total = product if total is None else total + product
        back.append(total)
    rel_high, rel_low = split(jnp.concatenate(back, 1))
    total = first_grad[...] + (nt(rel_high, place[...]) + nt(rel_low, place[...]))
    result = total.astype(BF16)
    start = 0
    for out in (i0, i1, i2):
        out[...] = result[start : start + out.shape[0]]
        start += out.shape[0]


class Moves:
    def __init__(self, batch, seq):
        self.batch, self.seq = batch, seq
        self.cube = batch == 16 and seq == 2

    def send(self, block, flip, other=None, core_flip=0, name="send"):
        flips = (flip, flip if other is None else other)
        pairs = []
        for b in range(self.batch):
            for c in range(self.seq):
                pairs.append((b * self.seq + c, (b ^ flips[c]) * self.seq + (c ^ core_flip)))
        with jax.named_scope(name):
            return lax.ppermute(block, AXES, pairs)

    def across(self, block, name="across"):
        return self.send(block, 0, 0, 1, name)

    def order(self):
        b, c = lax.axis_index("batch"), lax.axis_index("seq")
        places = jnp.arange(self.batch, dtype=jnp.int32)
        if not self.cube:
            return jnp.concatenate([places * self.seq + c, places * self.seq + (1 - c)])
        flips = np.array([[p ^ z for p in o for z in (0, 8, 4, 12)] for o in ((0, 1, 2, 3), (0, 2, 1, 3))])
        flips = flips.astype(np.int32)
        mine = jnp.where(c == 0, flips[0], flips[1])
        theirs = jnp.where(c == 0, flips[1], flips[0])
        return jnp.concatenate(
            [jnp.bitwise_xor(b, mine) * self.seq + c, jnp.bitwise_xor(b, theirs) * self.seq + 1 - c]
        )

    def gather(self, whole, shares, ready, use_first, use_second, use_third):
        if not self.cube:
            owns = [lax.all_gather(share, "batch", axis=0, tiled=True) for share in shares]
            out = [(own, self.across(own)) for own in owns]
            kept = use_first(*out[0], ())
            more = use_second(kept, *out[0], ())
            return out, kept, more, use_third(kept, more, *out[1])
        step = whole.shape[0]
        early_a = self.send(whole, 1, 2, name="early_a")
        early_b = self.send(join([whole, early_a]), 2, 1, name="early_b")
        lanes, lane = [], 0
        for share in shares:
            lanes.append((lane, lane + share.shape[1]))
            lane += share.shape[1]

        def far(index, *after):
            block = join([shares[index]], after) if after else shares[index]
            return self.send(block, 8, name=f"gather{index}_far")

        def near(index, far, *after):
            return self.send(join([shares[index], far], after), 4, name=f"gather{index}_near")

        def plane_a(index, *parts, after=()):
            block = join(parts, after)
            return block, self.send(block, 1, 2, name=f"gather{index}_a")

        def plane_b(index, *parts, after=()):
            block = join(parts, after)
            return block, self.send(block, 2, 1, name=f"gather{index}_b")

        def finish(index, far, near, first, second, *after, micros=0):
            cut = lanes[index]
            parts = [
                shares[index], far, near, (early_a, 0, step, *cut), first,
                (early_b, 0, step, *cut), (second, 0, 3 * step, 0, second.shape[1]),
                (early_b, step, 2 * step, *cut), (second, 3 * step, 6 * step, 0, second.shape[1]),
            ]
            own = join(parts, after, micros)
            return own, self.across(own, f"gather{index}_across")

        far_0 = far(0)
        near_0 = near(0, far_0, early_a)
        far_1 = far(1, far_0)
        _, a_0 = plane_a(0, far_0, near_0, after=(far_1, *ready))
        near_1 = near(1, far_1, near_0)
        far_2 = far(2, near_0)
        _, b_0 = plane_b(0, far_0, near_0, a_0, after=(near_1, early_b))
        _, a_1 = plane_a(1, far_1, near_1, after=(a_0,))
        near_2 = near(2, far_2, a_0)
        out_0 = finish(0, far_0, near_0, a_0, b_0, a_1, near_2)
        sent, b_1 = plane_b(1, far_1, near_1, a_1, after=(out_0[0],))
        sent, a_2 = plane_a(2, far_2, near_2, after=(sent,))
        kept = use_first(*out_0, (sent,))
        sent, b_2 = plane_b(2, far_2, near_2, a_2, after=(kept[0],))
        out_1 = finish(1, far_1, near_1, a_1, b_1, sent, micros=LONG)
        more = use_second(kept, *out_0, (out_1[0],))
        token = use_third(kept, more, *out_1)
        out_2 = finish(2, far_2, near_2, a_2, b_2, token[0])
        return [out_0, out_1, out_2], kept, more, token


class Scatter:
    def __init__(self, moves, own, sib, tag):
        self.moves, self.tag, self.kept, self.stage = moves, tag, own, 0
        self.coming = moves.across(sib, tag + "_across")

    def step(self, *after, micros=0):
        if not self.moves.cube:
            if self.stage == 0:
                self.kept = add(self.kept, self.coming)
                self.stage = 1
            return self.kept
        rows, lanes = self.kept.shape
        half = (rows // 2, lanes)

        def body(kept, coming, low, high):
            total = (kept[...].astype(F32) + coming[...].astype(F32)).astype(BF16)
            low[...] = total[: half[0]]
            high[...] = total[half[0] :]

        name = f"{self.tag}_add{self.stage}"
        self.kept, out = call(
            body, [(half, BF16), (half, BF16)], name, micros, self.kept, self.coming, after=after
        )
        flips = ((2, 1), (1, 2), (4, 4), (8, 8))[self.stage]
        self.coming = self.moves.send(out, *flips, name=f"{self.tag}_{self.stage}")
        self.stage += 1
        return self.kept

    def total(self):
        if not self.moves.cube:
            total = lax.psum_scatter(self.kept, "batch", scatter_dimension=0, tiled=True)
            return total.astype(F32)
        return self.kept.astype(F32) + self.coming.astype(F32)


def join(parts, after=(), micros=0):
    parts = [part if isinstance(part, tuple) else (part, 0, part.shape[0], 0, part.shape[1]) for part in parts]

    def body(*refs):
        row = 0
        for ref, (_, start, stop, left, right) in zip(refs, parts):
            refs[-1][row : row + stop - start, :] = ref[start:stop, left:right]
            row += stop - start

    rows = sum(stop - start for _, start, stop, _, _ in parts)
    shape = (rows, parts[0][4] - parts[0][3])
    arrays = [part[0] for part in parts]
    return call(body, [(shape, arrays[0].dtype)], "join", micros, *arrays, after=after)[0]


def add(*blocks):
    total = blocks[0].astype(F32)
    for block in blocks[1:]:
        total = total + block.astype(F32)
    return total.astype(BF16)


def on_device(moves, inputs, lengths, cotangents, attn, ffn, projection):
    query_weight, key_weight, value_weight, output_weight = attn[:4]
    up_weight, up_bias, down_weight, down_bias, ffn_gain, ffn_shift = ffn
    step, width = query_weight.shape
    hidden = up_bias.shape[0]
    chunks = hidden // step
    first_half = chunks // 2

    small = [*attn[4:], down_bias, ffn_gain, ffn_shift]
    small += [up_bias[i * step : (i + 1) * step] for i in range(chunks)]
    at = jnp.arange(16, dtype=jnp.int32)[:, None]
    small = sum(jnp.where(at == index, one[None, :], 0).astype(BF16) for index, one in enumerate(small))
    lanes_attn, lanes_half = 4 * width + 128, first_half * 2 * width
    lanes_rest = chunks * 2 * width - lanes_half
    sources = (*attn[:4], small, up_weight.T, down_weight)
    sources = [pltpu.with_memory_space_constraint(one, pltpu.HBM) for one in sources]
    *shares, whole = call(
        functools.partial(pack, chunks),
        [
            ((step, lanes), BF16)
            for lanes in (lanes_attn, lanes_half, lanes_rest, lanes_attn + lanes_half + lanes_rest)
        ],
        "pack",
        3,
        *sources,
        stage=True,
    )

    ranks = moves.order()
    rows_at = (ranks[:, None] * step + jnp.arange(step, dtype=jnp.int32)[None, :]).reshape(-1)
    place = (jnp.arange(width, dtype=jnp.int32)[:, None] == rows_at[None, :]).astype(BF16)

    blocks, valids, positions, pieces = [], [], [], []
    start = 0
    for block, limit in zip(inputs, lengths):
        count, local, _ = block.shape
        blocks.append(block.reshape(count * local, width))
        at = lax.axis_index("seq") * local + jnp.arange(local, dtype=jnp.int32)
        positions.append(jnp.tile(at, count))
        valids.append((at[None, :] < limit[:, None]).reshape(-1))
        for _ in range(count):
            pieces.append((start, start + local))
            start += local
    pieces = tuple(pieces)
    rows = start
    position = jnp.concatenate(positions).astype(F32)
    valid = jnp.broadcast_to(jnp.concatenate(valids).astype(F32)[:, None], (rows, FEAT))
    half_head = HD // 2
    rates = 10000.0 ** (-jnp.arange(half_head, dtype=F32) / half_head)
    angle = position[:, None] * rates[None, :]
    scale = HD ** (-0.25)
    cos, sin = jnp.cos(angle) * scale, jnp.sin(angle) * scale
    none = jnp.zeros_like(sin)
    cosine = jnp.concatenate([cos] * 4, 1)
    sine_a = jnp.concatenate([-sin, none] * 2, 1)
    sine_b = jnp.concatenate([none, sin] * 2, 1)
    same = np.arange(GROUP)[:, None] // 64 == np.arange(FEAT)[None, :] // 32
    lift = jnp.where(same, jnp.tile(projection, (4, 4)), 0.0)
    norm = jnp.asarray(np.where(same, -0.5, 0.0), F32)

    half = width // 2
    feats = width // 2
    slots = len(pieces) * (width // GROUP)
    wide, narrow = (rows, width), (rows, feats)
    packed_shape = (slots, FEAT, FEAT)
    def use_first(own, sib, after):
        return call(
            functools.partial(front, pieces),
            [
                (packed_shape, F32), (narrow, F32), (narrow, F32), (wide, F32), (wide, F32),
                (wide, BF16), (wide, BF16), ((32, width), F32),
            ],
            "front",
            9,
            *blocks, own, sib, place, cosine, sine_a, sine_b, valid, lift, norm,
            after=after,
        )

    def use_second(kept, own, sib, after):
        other = moves.across(kept[0])
        more = call(
            functools.partial(middle, pieces),
            [
                (wide, F32), (wide, F32), (wide, BF16), (wide, F32), ((rows, 128), F32),
                (wide, BF16),
            ],
            "middle",
            3,
            kept[0], other, kept[1], *blocks, own, sib, place, kept[-1],
            after=after,
        )
        return other, *more

    part = (rows, first_half * width)

    def use_third(kept, more, own, sib):
        return call(
            functools.partial(ffn_first, 0, first_half),
            [(part, BF16), (part, BF16), (wide, F32)],
            "ffn_first",
            4,
            more[-1], own, sib, kept[-1],
        )

    tables = (place, cosine, sine_a, sine_b, valid, lift, norm)
    gathered, kept, more, token = moves.gather(
        whole, shares, tables, use_first, use_second, use_third
    )
    (own_attn, sib_attn), (own_up, sib_up), (own_down, sib_down) = gathered
    packed, query_map, key_map, scaled_query, scaled_key, value_low, rows_rel, vectors = kept
    packed_other, attended, over, attended_rel, normed, spread, middle_low = more
    act_first, slope_first, total_first = token
    rest = (rows, (chunks - first_half) * width)
    flat = [block.reshape(-1, width) for block in cotangents]
    flats = [(block.shape, BF16) for block in flat]
    act_second, slope_second, o0, o1, o2, second_grad, down_low, sums_ffn = call(
        functools.partial(ffn_second, first_half, chunks - first_half),
        [(rest, BF16), (rest, BF16), *flats, (wide, F32), (wide, BF16), ((8, width), F32)],
        "ffn_second",
        5,
        middle_low, own_down, sib_down, vectors, total_first, normed, *flat,
    )
    smalls, totals, grads = [], [], []
    for base, count, own, sib, act, slope, name in (
        (first_half, chunks - first_half, own_down, sib_down, act_second, slope_second, "back_second"),
        (0, first_half, own_up, sib_up, act_first, slope_first, "back_first"),
    ):
        shape = (half, count * 2 * width)
        *grad, total, small_own, small_sib = call(
            functools.partial(back_part, base, count),
            [
                (shape, BF16), (shape, BF16), (wide, F32),
                ((half, 128), F32), ((half, 128), F32),
            ],
            name,
            6,
            middle_low, down_low, own, sib, act, slope,
            after=totals,
        )
        smalls += [small_own, small_sib]
        totals.append(total)
        grads.append(grad)
    second = Scatter(moves, *grads[0], "second")
    shape = (half, (first_half * 2 + 1) * width)
    *grad, packed_grad, num_low, den_grad, first_grad, sums_attn = call(
        functools.partial(turn, pieces),
        [
            (shape, BF16), (shape, BF16), (packed_shape, F32), (wide, BF16), (wide, F32),
            (wide, F32), ((8, width), F32),
        ],
        "turn",
        5,
        totals[1], totals[0], second_grad, normed, spread, vectors, own_attn, sib_attn,
        attended_rel, place, attended, over, query_map, *grads[1],
        after=(second.step(totals[1], micros=LONG),),
    )
    packed_grad_other = moves.across(packed_grad)
    first = Scatter(moves, *grad, "first")
    token = second.step(first_grad, micros=LONG)
    token = first.step(token, micros=LONG)
    row_grads = call(
        functools.partial(attend_back, pieces),
        [(wide, BF16)] * 3,
        "attend_back",
        9,
        packed, packed_other, packed_grad, packed_grad_other, num_low, den_grad, value_low,
        query_map, key_map, scaled_query, scaled_key, valid, cosine, sine_a, sine_b, lift,
        after=(token,),
    )
    shape = (half, 3 * width + 128)
    grad = call(
        weights_back,
        [(shape, BF16), (shape, BF16)],
        "weights_back",
        3,
        *row_grads, rows_rel, place, sums_ffn, sums_attn, *smalls,
    )
    third = Scatter(moves, *grad, "third")
    token = second.step(grad[0], micros=LONG)
    token = third.step(token, micros=LONG)
    token = second.step(token)
    token = first.step(token)
    i0, i1, i2 = call(
        rows_back, flats, "rows_back", 4, *row_grads, own_attn, sib_attn, place, first_grad,
        after=(token,),
    )
    token = third.step(i0, micros=LONG)
    token = first.step(token, micros=LONG)
    token = third.step(token, micros=LONG)
    token = first.step(token, micros=LONG)
    token = third.step(token, micros=LONG)
    sum_first, sum_second, sum_attn = first.total(), second.total(), third.total()

    def cut(block, index):
        return block[:, index * width : (index + 1) * width]

    grad_up, grad_down = [], []
    for index in range(chunks):
        source, at = (sum_first, index) if index < first_half else (sum_second, index - first_half)
        grad_up.append(cut(source, 2 * at))
        grad_down.append(cut(source, 2 * at + 1))
    grad_up = jnp.concatenate(grad_up, 0).T
    grad_down = jnp.concatenate(grad_down, 0)
    grad_output = cut(sum_first, 2 * first_half)
    column = sum_attn[:, 3 * width :].T
    grad_up_bias = column[UB : UB + chunks].reshape(-1)
    outs = [o.reshape(block.shape) for o, block in zip((o0, o1, o2, i0, i1, i2), inputs * 2)]
    return (
        *outs,
        cut(sum_attn, 0), cut(sum_attn, 1), cut(sum_attn, 2), grad_output,
        column[BQ], column[BK], column[BV], column[BO], column[AG], column[AS],
        grad_up, grad_up_bias, grad_down, column[DB], column[FG], column[FS],
    )


def solution(mesh):
    moves = Moves(mesh.shape["batch"], mesh.shape["seq"])

    def body(*args):
        return on_device(
            moves, args[0:3], args[3:6], args[6:9], args[9:19], args[19:25], args[25]
        )

    tokens = P("batch", "seq", None)
    shard = P(AXES)
    rows = P(AXES, None)
    attn = (rows,) * 4 + (shard,) * 6
    ffn = (P(None, AXES), shard, rows, shard, shard, shard)
    in_specs = (tokens,) * 3 + (P("batch"),) * 3 + (tokens,) * 3 + attn + ffn + (P(),)
    out_specs = (tokens,) * 6 + attn + ffn
    return jax.shard_map(
        body, mesh=mesh, in_specs=in_specs, out_specs=out_specs, check_vma=False
    )
```

```python
import functools
import math

import jax
import jax.numpy as jnp
import numpy as np
from jax import lax
from jax.experimental import pallas as pl
from jax.experimental.pallas import tpu as pltpu
from jax.sharding import PartitionSpec as P

HD = 64
HIGH = lax.Precision.HIGHEST
EPS_NORM = 1e-05
EPS_DEN = 1e-06
F32 = jnp.float32
BF16 = jnp.bfloat16
AXES = ("batch", "seq")
GROUP = 256
FEAT = 128
VMEM = 14 * 1024 * 1024
LONG = 100
BQ, BK, BV, BO, AG, AS, DB, FG, FS, UB = range(10)


def nn(a, b, precision=None):
    return lax.dot_general(
        a, b, (((1,), (0,)), ((), ())), precision=precision, preferred_element_type=F32
    )


def nt(a, b, precision=None):
    return lax.dot_general(
        a, b, (((1,), (1,)), ((), ())), precision=precision, preferred_element_type=F32
    )


def tn(a, b):
    return lax.dot_general(a, b, (((0,), (0,)), ((), ())), preferred_element_type=F32)


def split(x):
    high = x.astype(BF16)
    return high, (x - high.astype(F32)).astype(BF16)


def iota(shape, axis):
    return lax.broadcasted_iota(jnp.int32, shape, axis)


def head_mask():
    return iota((FEAT, GROUP), 0) // 32 == iota((FEAT, GROUP), 1) // 64


def spread_mask(rows, row_size, lanes, lane_size):
    same = iota((rows, lanes), 0) // row_size == iota((rows, lanes), 1) // lane_size
    return same.astype(F32).astype(BF16)


def compact(block, mask):
    kept = jnp.where(mask, block, 0.0)
    kept = kept[:, :FEAT] + kept[:, FEAT:]
    return jnp.concatenate([kept[0:32] + kept[32:64], kept[64:96] + kept[96:128]], 0)


def expand(block, mask):
    top, bottom = block[0:32], block[32:64]
    rows = jnp.concatenate([top, top, bottom, bottom], 0)
    return jnp.where(mask, jnp.concatenate([rows, rows], 1), 0.0)


def both(mine, other, start, count):
    return mine[start : start + count, :] + other[start : start + count, :]


def exact(x, ones):
    high, low = split(x)
    return nn(high, ones) + nn(low, ones)


def rotate(block, cosine, sine_a, sine_b):
    parts = []
    for lane in range(0, block.shape[1], 128):
        part = block[:, lane : lane + 128]
        parts.append(
            part * cosine + pltpu.roll(part, 96, 1) * sine_a + pltpu.roll(part, 32, 1) * sine_b
        )
    return jnp.concatenate(parts, 1)


def lane_mean(block):
    return jnp.mean(block, axis=-1, keepdims=True)


def norm_back(upstream, normed, spread, gain):
    scaled = upstream * gain
    return spread * (scaled - lane_mean(scaled) - normed * lane_mean(scaled * normed))


def column_sum(block):
    return jnp.sum(block, axis=0, keepdims=True)


def skipping(body, count, extra, *refs):
    return body(*refs[:count], *refs[count + extra :])


def call(body, outs, name, micros, *args, after=(), stage=False):
    whole = pl.BlockSpec(memory_space=pltpu.VMEM)
    anywhere = pl.BlockSpec(memory_space=pl.ANY)
    scratch = [pltpu.VMEM(arg.shape, arg.dtype) for arg in args]
    scratch.append(pltpu.SemaphoreType.DMA((len(args),)))
    return pl.pallas_call(
        functools.partial(skipping, body, len(args), len(after)) if after else body,
        out_shape=tuple(jax.ShapeDtypeStruct(shape, kind) for shape, kind in outs),
        in_specs=[anywhere if stage else whole] * len(args) + [anywhere] * len(after),
        scratch_shapes=scratch if stage else [],
        out_specs=tuple(whole for _ in outs),
        compiler_params=pltpu.CompilerParams(vmem_limit_bytes=VMEM),
        cost_estimate=pl.CostEstimate(
            flops=int(micros * 1.15e9), bytes_accessed=10**6, transcendentals=0
        ),
        name=name,
    )(*args, *after)


def pack(
    chunks, query, keys, value, output, small, up, down, attn, first, second, whole, *scratch
):
    buffers, sems = scratch[:-1], scratch[-1]
    sources = (query, keys, value, output, small, up, down)
    copies = [
        pltpu.make_async_copy(source, buffer, sems.at[index])
        for index, (source, buffer) in enumerate(zip(sources, buffers))
    ]
    for copy in copies:
        copy.start()
    for copy in copies:
        copy.wait()
    step, width = query.shape
    for index in range(4):
        attn[:, index * width : (index + 1) * width] = buffers[index][...]
    eye = (iota((16, 128), 0) == iota((16, 128), 1)).astype(F32).astype(BF16)
    attn[:, 4 * width :] = tn(buffers[4][...], eye).astype(BF16)
    for chunk in range(chunks):
        out = first if chunk < chunks // 2 else second
        at = 2 * width * (chunk if chunk < chunks // 2 else chunk - chunks // 2)
        rows = slice(chunk * step, (chunk + 1) * step)
        out[:, at : at + width] = buffers[5][rows, :]
        out[:, at + width : at + 2 * width] = buffers[6][rows, :]
    lane = 0
    for part in (attn, first, second):
        whole[:, lane : lane + part.shape[1]] = part[...]
        lane += part.shape[1]


def front(
    pieces, x0, x1, x2, own, sib, place, cosine, sine_a, sine_b, valid, lift, norm,
    packed, query_map, key_map, scaled_query, scaled_key, value_low, rows_rel, vectors,
):
    half = own.shape[0]
    width = 2 * half
    tail = own.shape[1] - 128
    x = jnp.concatenate([x0[...], x1[...], x2[...]], 0)
    rel = nn(x, place[...]).astype(BF16)
    rows_rel[...] = rel
    left, right = rel[:, :half], rel[:, half:]
    small_own = own[:, tail:].T
    small_sib = sib[:, tail:].T
    ordered = nt(small_own, place[:, :half]) + nt(small_sib, place[:, half:])
    vectors[0:16, :] = ordered[0:16]
    vectors[16:32, :half] = small_own[0:16].astype(F32)
    vectors[16:32, half:] = small_sib[0:16].astype(F32)
    cos, sin_a, sin_b = cosine[...], sine_a[...], sine_b[...]
    ok = valid[...]
    mask = head_mask()
    lift_high, lift_low = split(lift[...])
    halves = norm[...].astype(BF16)
    totals = len(pieces) * (width // GROUP) * 64
    for group in range(width // GROUP):
        feats = slice(group * FEAT, (group + 1) * FEAT)
        lanes = slice(group * GROUP, (group + 1) * GROUP)

        def project(index):
            start = index * width + group * GROUP
            cut = slice(start, start + GROUP)
            bias = ordered[index : index + 1, lanes]
            return nn(left, own[:, cut]) + nn(right, sib[:, cut]) + bias

        low = project(2).astype(BF16)
        value_low[:, lanes] = low
        maps = []
        for index, kept in ((0, scaled_query), (1, scaled_key)):
            scaled = rotate(project(index), cos, sin_a, sin_b)
            kept[:, lanes] = scaled
            high, low_part = split(scaled)
            power = nn(high, lift_high) + (nn(high, lift_low) + nn(low_part, lift_high))
            power += exact(scaled * scaled, halves)
            maps.append(jnp.exp(power) * (1.0 / math.sqrt(32.0)))
        query_map[:, feats] = maps[0]
        key_map[:, feats] = maps[1]
        feat = maps[1].astype(BF16).astype(F32) * ok
        for index, (start, stop) in enumerate(pieces):
            slot = index * (width // GROUP) + group
            state = tn(feat[start:stop].astype(BF16), low[start:stop])
            packed[slot * 64 : (slot + 1) * 64, :] = compact(state, mask)
            packed[totals + slot : totals + slot + 1, :] = column_sum(feat[start:stop])


def middle(
    pieces, mine, other, query_map, x0, x1, x2, own, sib, place, vectors,
    attended, over, over_feat, attended_rel, normed, spread, middle_low,
):
    half = own.shape[0]
    width = 2 * half
    mask = head_mask()
    wide = spread_mask(FEAT, 32, GROUP, 64)
    narrow = spread_mask(FEAT, 32, FEAT, 32)
    totals = len(pieces) * (width // GROUP) * 64
    for group in range(width // GROUP):
        feats = slice(group * FEAT, (group + 1) * FEAT)
        lanes = slice(group * GROUP, (group + 1) * GROUP)
        feat = query_map[:, feats].astype(BF16)
        tops, bottoms = [], []
        for index, (start, stop) in enumerate(pieces):
            slot = index * (width // GROUP) + group
            state_high, state_low = split(expand(both(mine, other, slot * 64, 64), mask))
            part = feat[start:stop]
            tops.append(nn(part, state_high) + nn(part, state_low))
            bottoms.append(part.astype(F32) * both(mine, other, totals + slot, 1))
        high, low = split(jnp.concatenate(bottoms, 0))
        inverse = 1.0 / (nn(high, wide) + nn(low, wide) + EPS_DEN)
        over[:, lanes] = inverse
        over_feat[:, feats] = 1.0 / (nn(high, narrow) + nn(low, narrow) + EPS_DEN)
        attended[:, lanes] = jnp.concatenate(tops, 0) * inverse
    rel = nn(attended[...].astype(BF16), place[...]).astype(BF16)
    attended_rel[...] = rel
    branch = nn(rel[:, :half], own[:, 3 * width : 4 * width])
    branch += nn(rel[:, half:], sib[:, 3 * width : 4 * width])
    x = jnp.concatenate([x0[...], x1[...], x2[...]], 0).astype(F32)
    first = x + branch + vectors[BO : BO + 1, :]
    center = first - lane_mean(first)
    scale = lax.rsqrt(lane_mean(center * center) + EPS_NORM)
    norm = center * scale
    normed[...] = norm
    spread[...] = jnp.broadcast_to(scale, spread.shape)
    middle_low[...] = (norm * vectors[AG : AG + 1, :] + vectors[AS : AS + 1, :]).astype(BF16)


def ffn_chunks(base, chunks, middle_low, own, sib, vectors, activated, slope):
    half = own.shape[0]
    width = 2 * half
    low = middle_low[...]
    total = None
    for chunk in range(chunks):
        lane = chunk * 2 * width
        row = 16 + UB + base + chunk
        for index, part in enumerate((own, sib)):
            cut = slice(index * half, (index + 1) * half)
            pre = nt(low, part[:, lane : lane + width]) + vectors[row : row + 1, cut]
            cdf = 0.5 + 0.5 * lax.erf(pre * math.sqrt(0.5))
            act = (pre * cdf).astype(BF16)
            bell = jnp.exp(-0.5 * pre * pre) * (1.0 / math.sqrt(2.0 * math.pi))
            cut = slice(chunk * width + index * half, chunk * width + (index + 1) * half)
            activated[:, cut] = act
            slope[:, cut] = (cdf + pre * bell).astype(BF16)
            product = nn(act, part[:, lane + width : lane + 2 * width])
            total = product if total is None else total + product
    return total


def ffn_first(base, chunks, middle_low, own, sib, vectors, activated, slope, total):
    total[...] = ffn_chunks(base, chunks, middle_low, own, sib, vectors, activated, slope)


def ffn_second(
    base, chunks, middle_low, own, sib, vectors, before, normed, c0, c1, c2,
    activated, slope, o0, o1, o2, second_grad, down_low, sums,
):
    total = ffn_chunks(base, chunks, middle_low, own, sib, vectors, activated, slope)
    mid = normed[...] * vectors[AG : AG + 1, :] + vectors[AS : AS + 1, :]
    second = mid + (before[...] + total) + vectors[DB : DB + 1, :]
    center = second - lane_mean(second)
    spread = lax.rsqrt(lane_mean(center * center) + EPS_NORM)
    norm = center * spread
    gain = vectors[FG : FG + 1, :]
    result = (norm * gain + vectors[FS : FS + 1, :]).astype(BF16)
    start = 0
    for out in (o0, o1, o2):
        out[...] = result[start : start + out.shape[0]]
        start += out.shape[0]
    upstream = jnp.concatenate([c0[...], c1[...], c2[...]], 0).astype(F32)
    grad = norm_back(upstream, norm, spread, gain)
    low = grad.astype(BF16)
    second_grad[...] = grad
    down_low[...] = low
    sums[...] = jnp.zeros(sums.shape, F32)
    sums[0:1, :] = column_sum(low.astype(F32))
    sums[1:2, :] = column_sum(upstream * norm)
    sums[2:3, :] = column_sum(upstream)


def back_down(first, second, down_low, grad_own, grad_sib):
    half, lanes = grad_own.shape
    width = 2 * half
    down = down_low[...]
    early = first.shape[1] // width
    for chunk in range(lanes // width):
        part, at = (first, chunk) if chunk < early else (second, chunk - early)
        cut = slice(chunk * width, (chunk + 1) * width)
        grad_own[:, cut] = tn(part[:, at * width : at * width + half], down).astype(BF16)
        grad_sib[:, cut] = tn(part[:, at * width + half : (at + 1) * width], down).astype(BF16)


def back_up(base, count, middle_low, down_low, own, sib, slope, total, small_own, small_sib, *grads):
    half = own.shape[0]
    width = 2 * half
    low = middle_low[...]
    down = down_low[...]
    result = None
    small = [None, None]
    for chunk in range(count):
        lane = chunk * 2 * width
        at = slice(chunk * width, (chunk + 1) * width)
        pick = (iota((low.shape[0], 128), 1) == UB + base + chunk).astype(F32).astype(BF16)
        for index, part in enumerate((own, sib)):
            cut = slice(chunk * width + index * half, chunk * width + (index + 1) * half)
            up = nt(down, part[:, lane + width : lane + 2 * width])
            up = (up * slope[:, cut].astype(F32)).astype(BF16)
            weight = tn(up, low).astype(BF16)
            row = 0
            for grad in grads[:1] if index == 0 else grads[1:]:
                grad[:, at] = weight[row : row + grad.shape[0]]
                row += grad.shape[0]
            bias = tn(up, pick)
            small[index] = bias if small[index] is None else small[index] + bias
            product = nn(up, part[:, lane : lane + width])
            result = product if result is None else result + product
    total[...] = result
    small_own[...] = small[0]
    small_sib[...] = small[1]


def turn(
    pieces, before, after, second_grad, normed, spread, vectors, own_attn, sib_attn,
    attended_rel, place, attended, over, over_feat, query_map,
    grad_own, grad_sib, packed, num_low, den_grad, first_grad, sums,
):
    half = own_attn.shape[0]
    width = 2 * half
    grad = second_grad[...] + (before[...] + after[...])
    norm = normed[...]
    first = norm_back(grad, norm, spread[:, 0:1], vectors[AG : AG + 1, :])
    branch = first.astype(BF16)
    first_grad[...] = first
    sums[...] = jnp.zeros(sums.shape, F32)
    sums[0:1, :] = column_sum(branch.astype(F32))
    sums[1:2, :] = column_sum(grad * norm)
    sums[2:3, :] = column_sum(grad)
    weight = tn(attended_rel[...], branch).astype(BF16)
    grad_own[...] = weight[:half]
    grad_sib[...] = weight[half:]
    cut = slice(3 * width, 4 * width)
    rel = jnp.concatenate([nt(branch, own_attn[:, cut]), nt(branch, sib_attn[:, cut])], 1)
    rel_high, rel_low = split(rel)
    upstream = nt(rel_high, place[...]) + nt(rel_low, place[...])
    inverse = over[...]
    num = (upstream * inverse).astype(BF16)
    num_low[...] = num
    weighted_high, weighted_low = split(upstream * attended[...])
    mask = head_mask()
    narrow = spread_mask(GROUP, 64, FEAT, 32)
    totals = len(pieces) * (width // GROUP) * 64
    for group in range(width // GROUP):
        lanes = slice(group * GROUP, (group + 1) * GROUP)
        feats = slice(group * FEAT, (group + 1) * FEAT)
        den = nn(weighted_high[:, lanes], narrow) + nn(weighted_low[:, lanes], narrow)
        den = -den * over_feat[:, feats]
        den_grad[:, feats] = den
        feat = query_map[:, feats].astype(BF16)
        den = den * feat.astype(F32)
        for index, (start, stop) in enumerate(pieces):
            slot = index * (width // GROUP) + group
            state = tn(feat[start:stop], num[start:stop, lanes])
            packed[slot * 64 : (slot + 1) * 64, :] = compact(state, mask)
            packed[totals + slot : totals + slot + 1, :] = column_sum(den[start:stop])


def attend_back(
    pieces, mine, other, mine_grad, other_grad, num_low, den_grad, value_low, query_map, key_map,
    scaled_query, scaled_key, valid, cosine, sine_a, sine_b, lift,
    query_grad, key_grad, value_grad,
):
    width = value_low.shape[1]
    mask = head_mask()
    cos, sin_a, sin_b = cosine[...], sine_a[...], sine_b[...]
    ok = valid[...]
    lift_high, lift_low = split(lift[...])
    wide = spread_mask(FEAT, 32, GROUP, 64)
    totals = len(pieces) * (width // GROUP) * 64
    for group in range(width // GROUP):
        lanes = slice(group * GROUP, (group + 1) * GROUP)
        feats = slice(group * FEAT, (group + 1) * FEAT)
        query_parts, key_parts = [], []
        key_low = (key_map[:, feats].astype(BF16).astype(F32) * ok).astype(BF16)
        for index, (start, stop) in enumerate(pieces):
            slot = index * (width // GROUP) + group
            state_high, state_low = split(expand(both(mine, other, slot * 64, 64), mask))
            grads = expand(both(mine_grad, other_grad, slot * 64, 64), mask)
            sg_high, sg_low = split(grads)
            num = num_low[start:stop, lanes]
            part = den_grad[start:stop, feats] * both(mine, other, totals + slot, 1)
            query_parts.append(part + (nt(num, state_high) + nt(num, state_low)))
            value = value_low[start:stop, lanes]
            row = both(mine_grad, other_grad, totals + slot, 1)
            key_parts.append(row + (nt(value, sg_high) + nt(value, sg_low)))
            low = key_low[start:stop]
            value_grad[start:stop, lanes] = (nn(low, sg_high) + nn(low, sg_low)).astype(BF16)
        query_inner = jnp.concatenate(query_parts, 0) * query_map[:, feats]
        key_inner = jnp.concatenate(key_parts, 0) * ok * key_map[:, feats]
        for inner, scaled, grad in (
            (query_inner, scaled_query, query_grad),
            (key_inner, scaled_key, key_grad),
        ):
            high, low = split(inner)
            back = nt(high, lift_high) + (nt(high, lift_low) + nt(low, lift_high))
            back -= (nn(high, wide) + nn(low, wide)) * scaled[:, lanes]
            grad[:, lanes] = rotate(back, cos, -sin_a, -sin_b).astype(BF16)


def weights_back(
    query_grad, key_grad, value_grad, rows_rel, place, sums_ffn, sums_attn,
    small_0, small_1, small_2, small_3, grad_own, grad_sib, grad_rest,
):
    half = grad_own.shape[0]
    width = 2 * half
    part = half // 2
    rel = rows_rel[...]
    rows = []

    def keep(cut, block):
        grad_own[:, cut] = block[:half]
        grad_sib[:, cut] = block[half : half + part]
        grad_rest[:, cut] = block[half + part :]

    for index, grad in enumerate((query_grad, key_grad, value_grad)):
        block = grad[...]
        keep(slice(index * width, (index + 1) * width), tn(rel, block).astype(BF16))
        rows.append(column_sum(block.astype(F32)))
    rows += [sums_attn[0:3, :], sums_ffn[0:3, :]]
    rows.append(jnp.zeros((128 - 9, width), F32))
    columns = nn(jnp.concatenate(rows, 0).astype(BF16), place[...]).T
    left = columns[:half] + small_0[...] + small_2[...]
    right = columns[half:] + small_1[...] + small_3[...]
    total = jnp.concatenate([left, right], 0).astype(BF16)
    keep(slice(3 * width, 3 * width + 128), total)


def rows_back(query_grad, key_grad, value_grad, own, sib, place, first_grad, i0, i1, i2):
    width = place.shape[0]
    back = []
    for part in (own, sib):
        total = None
        for index, grad in enumerate((query_grad, key_grad, value_grad)):
            product = nt(grad[...], part[:, index * width : (index + 1) * width])
            total = product if total is None else total + product
        back.append(total)
    rel_high, rel_low = split(jnp.concatenate(back, 1))
    total = first_grad[...] + (nt(rel_high, place[...]) + nt(rel_low, place[...]))
    result = total.astype(BF16)
    start = 0
    for out in (i0, i1, i2):
        out[...] = result[start : start + out.shape[0]]
        start += out.shape[0]


def finish_ffn(down_low, down_high, up_low, up_high, up, down):
    step = down_low.shape[0]
    width = up.shape[1]
    for low, high, out in ((up_low, up_high, up), (down_low, down_high, down)):
        total = low[...].astype(F32) + high[...].astype(F32)
        for chunk in range(total.shape[1] // width):
            out[chunk * step : (chunk + 1) * step, :] = total[:, chunk * width : (chunk + 1) * width]


def finish_attn(low, high, output_low, output_high, query, keys, value, output, small):
    step, width = query.shape
    for index, out in enumerate((query, keys, value)):
        cut = slice(index * width, (index + 1) * width)
        out[...] = low[:, cut].astype(F32) + high[:, cut].astype(F32)
    output[...] = output_low[...].astype(F32) + output_high[...].astype(F32)
    cut = slice(3 * width, 3 * width + 128)
    eye = (iota((step, step), 0) == iota((step, step), 1)).astype(F32).astype(BF16)
    small[...] = (tn(low[:, cut], eye) + tn(high[:, cut], eye))[0:16]


class Moves:
    def __init__(self, batch, seq):
        self.batch, self.seq = batch, seq
        self.cube = batch == 16 and seq == 2

    def send(self, block, flip, other=None, core_flip=0, name="send"):
        flips = (flip, flip if other is None else other)
        pairs = []
        for b in range(self.batch):
            for c in range(self.seq):
                pairs.append((b * self.seq + c, (b ^ flips[c]) * self.seq + (c ^ core_flip)))
        with jax.named_scope(name):
            return lax.ppermute(block, AXES, pairs)

    def across(self, block, name="across"):
        return self.send(block, 0, 0, 1, name)

    def order(self):
        b, c = lax.axis_index("batch"), lax.axis_index("seq")
        places = jnp.arange(self.batch, dtype=jnp.int32)
        if not self.cube:
            return jnp.concatenate([places * self.seq + c, places * self.seq + (1 - c)])
        flips = np.array([[p ^ z for p in o for z in (0, 8, 4, 12)] for o in ((0, 1, 2, 3), (0, 2, 1, 3))])
        flips = flips.astype(np.int32)
        mine = jnp.where(c == 0, flips[0], flips[1])
        theirs = jnp.where(c == 0, flips[1], flips[0])
        return jnp.concatenate(
            [jnp.bitwise_xor(b, mine) * self.seq + c, jnp.bitwise_xor(b, theirs) * self.seq + 1 - c]
        )

    def gather(self, whole, shares, ready, use_first, use_second, use_third):
        if not self.cube:
            owns = [lax.all_gather(share, "batch", axis=0, tiled=True) for share in shares]
            out = [(own, self.across(own)) for own in owns]
            kept = use_first(*out[0], ())
            more = use_second(kept, *out[0], ())
            return out, kept, more, use_third(kept, more, *out[1])
        step = whole.shape[0]
        early_a = self.send(whole, 1, 2, name="early_a")
        early_b = self.send(join([whole, early_a]), 2, 1, name="early_b")
        lanes, lane = [], 0
        for share in shares:
            lanes.append((lane, lane + share.shape[1]))
            lane += share.shape[1]

        def far(index, *after):
            block = join([shares[index]], after) if after else shares[index]
            return self.send(block, 8, name=f"gather{index}_far")

        def near(index, far, *after):
            return self.send(join([shares[index], far], after), 4, name=f"gather{index}_near")

        def plane_a(index, *parts, after=()):
            block = join(parts, after)
            return block, self.send(block, 1, 2, name=f"gather{index}_a")

        def plane_b(index, *parts, after=()):
            block = join(parts, after)
            return block, self.send(block, 2, 1, name=f"gather{index}_b")

        def finish(index, far, near, first, second, *after, micros=0):
            cut = lanes[index]
            parts = [
                shares[index], far, near, (early_a, 0, step, *cut), first,
                (early_b, 0, step, *cut), (second, 0, 3 * step, 0, second.shape[1]),
                (early_b, step, 2 * step, *cut), (second, 3 * step, 6 * step, 0, second.shape[1]),
            ]
            own = join(parts, after, micros)
            return own, self.across(own, f"gather{index}_across")

        far_0 = far(0)
        near_0 = near(0, far_0, early_a)
        far_1 = far(1, far_0)
        _, a_0 = plane_a(0, far_0, near_0, after=(far_1, *ready))
        near_1 = near(1, far_1, near_0)
        far_2 = far(2, near_0)
        _, b_0 = plane_b(0, far_0, near_0, a_0, after=(near_1, early_b))
        _, a_1 = plane_a(1, far_1, near_1, after=(a_0,))
        near_2 = near(2, far_2, a_0)
        out_0 = finish(0, far_0, near_0, a_0, b_0, a_1, near_2)
        sent, b_1 = plane_b(1, far_1, near_1, a_1, after=(out_0[0],))
        sent, a_2 = plane_a(2, far_2, near_2, after=(sent,))
        kept = use_first(*out_0, (sent,))
        sent, b_2 = plane_b(2, far_2, near_2, a_2, after=(kept[0],))
        out_1 = finish(1, far_1, near_1, a_1, b_1, sent, micros=LONG)
        more = use_second(kept, *out_0, (out_1[0],))
        token = use_third(kept, more, *out_1)
        out_2 = finish(2, far_2, near_2, a_2, b_2, token[0])
        return [out_0, out_1, out_2], kept, more, token


class Scatter:
    def __init__(self, moves, own, sib, tag, z_first=False):
        self.moves, self.tag, self.kept, self.stage = moves, tag, own, 0
        self.coming = [[moves.across(part, tag + "_across") for part in parts] for parts in sib]
        plane = [((2, 1), 1), ((1, 2), 1)]
        self.plan = plane + [((4, 4), 1), ((8, 8), 1)]
        if z_first:
            self.plan = [((4, 4), 4), ((8, 8), 4)] + plane

    def step(self, *after, micros=0):
        if not self.moves.cube:
            if self.stage == 0:
                coming = [jnp.concatenate(parts, 0) for parts in self.coming]
                self.kept = [add(jnp.concatenate(self.kept, 1), jnp.concatenate(coming, 1))]
                self.stage = 1
            return self.kept[0]
        flips, runs = self.plan[self.stage]
        rows, lanes = self.kept[0].shape[0], sum(part.shape[1] for part in self.kept)
        half, run = (rows // 2, lanes), rows // runs
        kept, coming = self.kept, self.coming

        def body(*refs):
            low, high = refs[-2:]
            lane, at = 0, len(kept)
            for ref, parts in zip(refs, coming):
                cut = slice(lane, lane + ref.shape[1])
                lane += ref.shape[1]
                block = jnp.concatenate([one[...] for one in refs[at : at + len(parts)]], 0)
                at += len(parts)
                total = (ref[...].astype(F32) + block.astype(F32)).astype(BF16)
                for index in range(runs):
                    out, start = slice(index * run // 2, (index + 1) * run // 2), index * run
                    low[out, cut] = total[start : start + run // 2]
                    high[out, cut] = total[start + run // 2 : start + run]

        name = f"{self.tag}_add{self.stage}"
        arrays = list(kept) + [part for parts in coming for part in parts]
        keep, out = call(body, [(half, BF16), (half, BF16)], name, micros, *arrays, after=after)
        self.kept = [keep]
        self.coming = [[self.moves.send(out, *flips, name=f"{self.tag}_{self.stage}")]]
        self.stage += 1
        return keep

    def total(self):
        if not self.moves.cube:
            total = lax.psum_scatter(self.kept[0], "batch", scatter_dimension=0, tiled=True)
            return total, jnp.zeros_like(total)
        return self.kept[0], self.coming[0][0]


def join(parts, after=(), micros=0):
    parts = [part if isinstance(part, tuple) else (part, 0, part.shape[0], 0, part.shape[1]) for part in parts]

    def body(*refs):
        row = 0
        for ref, (_, start, stop, left, right) in zip(refs, parts):
            refs[-1][row : row + stop - start, :] = ref[start:stop, left:right]
            row += stop - start

    rows = sum(stop - start for _, start, stop, _, _ in parts)
    shape = (rows, parts[0][4] - parts[0][3])
    arrays = [part[0] for part in parts]
    return call(body, [(shape, arrays[0].dtype)], "join", micros, *arrays, after=after)[0]


def add(*blocks):
    total = blocks[0].astype(F32)
    for block in blocks[1:]:
        total = total + block.astype(F32)
    return total.astype(BF16)


def on_device(moves, inputs, lengths, cotangents, attn, ffn, projection):
    query_weight, key_weight, value_weight, output_weight = attn[:4]
    up_weight, up_bias, down_weight, down_bias, ffn_gain, ffn_shift = ffn
    step, width = query_weight.shape
    hidden = up_bias.shape[0]
    chunks = hidden // step
    first_half = chunks // 2

    small = [*attn[4:], down_bias, ffn_gain, ffn_shift]
    small += [up_bias[i * step : (i + 1) * step] for i in range(chunks)]
    at = jnp.arange(16, dtype=jnp.int32)[:, None]
    small = sum(jnp.where(at == index, one[None, :], 0).astype(BF16) for index, one in enumerate(small))
    lanes_attn, lanes_half = 4 * width + 128, first_half * 2 * width
    lanes_rest = chunks * 2 * width - lanes_half
    sources = (*attn[:4], small, up_weight.T, down_weight)
    sources = [pltpu.with_memory_space_constraint(one, pltpu.HBM) for one in sources]
    *shares, whole = call(
        functools.partial(pack, chunks),
        [
            ((step, lanes), BF16)
            for lanes in (lanes_attn, lanes_half, lanes_rest, lanes_attn + lanes_half + lanes_rest)
        ],
        "pack",
        0,
        *sources,
        stage=True,
    )

    ranks = moves.order()
    rows_at = (ranks[:, None] * step + jnp.arange(step, dtype=jnp.int32)[None, :]).reshape(-1)
    place = (jnp.arange(width, dtype=jnp.int32)[:, None] == rows_at[None, :]).astype(BF16)

    blocks, valids, positions, pieces = [], [], [], []
    start = 0
    for block, limit in zip(inputs, lengths):
        count, local, _ = block.shape
        blocks.append(block.reshape(count * local, width))
        at = lax.axis_index("seq") * local + jnp.arange(local, dtype=jnp.int32)
        positions.append(jnp.tile(at, count))
        valids.append((at[None, :] < limit[:, None]).reshape(-1))
        for _ in range(count):
            pieces.append((start, start + local))
            start += local
    pieces = tuple(pieces)
    rows = start
    position = jnp.concatenate(positions).astype(F32)
    valid = jnp.broadcast_to(jnp.concatenate(valids).astype(F32)[:, None], (rows, FEAT))
    half_head = HD // 2
    rates = 10000.0 ** (-jnp.arange(half_head, dtype=F32) / half_head)
    angle = position[:, None] * rates[None, :]
    scale = HD ** (-0.25)
    cos, sin = jnp.cos(angle) * scale, jnp.sin(angle) * scale
    none = jnp.zeros_like(sin)
    cosine = jnp.concatenate([cos] * 4, 1)
    sine_a = jnp.concatenate([-sin, none] * 2, 1)
    sine_b = jnp.concatenate([none, sin] * 2, 1)
    same = np.arange(GROUP)[:, None] // 64 == np.arange(FEAT)[None, :] // 32
    lift = jnp.where(same, jnp.tile(projection, (4, 4)), 0.0)
    norm = jnp.asarray(np.where(same, -0.5, 0.0), F32)

    half = width // 2
    feats = width // 2
    slots = len(pieces) * (width // GROUP)
    wide, narrow = (rows, width), (rows, feats)
    packed_shape = (slots * 64 + -(-slots // 8) * 8, FEAT)
    def use_first(own, sib, after):
        return call(
            functools.partial(front, pieces),
            [
                (packed_shape, F32), (narrow, F32), (narrow, F32), (wide, F32), (wide, F32),
                (wide, BF16), (wide, BF16), ((32, width), F32),
            ],
            "front",
            0,
            *blocks, own, sib, place, cosine, sine_a, sine_b, valid, lift, norm,
            after=after,
        )

    def use_second(kept, own, sib, after):
        other = moves.across(kept[0])
        more = call(
            functools.partial(middle, pieces),
            [
                (wide, F32), (wide, F32), (narrow, F32), (wide, BF16), (wide, F32),
                ((rows, 128), F32), (wide, BF16),
            ],
            "middle",
            0,
            kept[0], other, kept[1], *blocks, own, sib, place, kept[-1],
            after=after,
        )
        return other, *more

    part = (rows, first_half * width)

    def use_third(kept, more, own, sib):
        return call(
            functools.partial(ffn_first, 0, first_half),
            [(part, BF16), (part, BF16), (wide, F32)],
            "ffn_first",
            0,
            more[-1], own, sib, kept[-1],
        )

    tables = (place, cosine, sine_a, sine_b, valid, lift, norm)
    gathered, kept, more, token = moves.gather(
        whole, shares, tables, use_first, use_second, use_third
    )
    (own_attn, sib_attn), (own_up, sib_up), (own_down, sib_down) = gathered
    packed, query_map, key_map, scaled_query, scaled_key, value_low, rows_rel, vectors = kept
    packed_other, attended, over, over_feat, attended_rel, normed, spread, middle_low = more
    act_first, slope_first, total_first = token
    rest = (rows, (chunks - first_half) * width)
    flat = [block.reshape(-1, width) for block in cotangents]
    flats = [(block.shape, BF16) for block in flat]
    act_second, slope_second, o0, o1, o2, second_grad, down_low, sums_ffn = call(
        functools.partial(ffn_second, first_half, chunks - first_half),
        [(rest, BF16), (rest, BF16), *flats, (wide, F32), (wide, BF16), ((8, width), F32)],
        "ffn_second",
        0,
        middle_low, own_down, sib_down, vectors, total_first, normed, *flat,
    )
    shape = (half, chunks * width)
    own, sib = call(
        back_down, [(shape, BF16)] * 2, "back_down", 0, act_first, act_second, down_low
    )
    down = Scatter(moves, [own], [[sib]], "down")

    def back(name, base, count, own, sib, slope, parts, *after):
        return call(
            functools.partial(back_up, base, count),
            [(wide, F32), ((half, 128), F32), ((half, 128), F32)]
            + [((part, count * width), BF16) for part in parts],
            name,
            0,
            middle_low, down_low, own, sib, slope,
            after=after,
        )

    total_second, small_0, small_1, own_second, sib_second = back(
        "back_second", first_half, chunks - first_half, own_down, sib_down, slope_second,
        (half, half), own,
    )
    token = down.step(total_second)
    total_first, small_2, small_3, own_first, *sib_first = back(
        "back_first", 0, first_half, own_up, sib_up, slope_first, (half, half // 2, half // 2), token
    )
    up = Scatter(moves, [own_first, own_second], [sib_first, [sib_second]], "up")
    square = (half, width)
    own, sib, packed_grad, num_low, den_grad, first_grad, sums_attn = call(
        functools.partial(turn, pieces),
        [
            (square, BF16), (square, BF16), (packed_shape, F32), (wide, BF16), (narrow, F32),
            (wide, F32), ((8, width), F32),
        ],
        "turn",
        0,
        total_first, total_second, second_grad, normed, spread, vectors, own_attn, sib_attn,
        attended_rel, place, attended, over, over_feat, query_map,
    )
    packed_grad_other = moves.across(packed_grad)
    output = Scatter(moves, [own], [[sib]], "output", z_first=True)
    token = up.step(first_grad)
    row_grads = call(
        functools.partial(attend_back, pieces),
        [(wide, BF16)] * 3,
        "attend_back",
        0,
        packed, packed_other, packed_grad, packed_grad_other, num_low, den_grad, value_low,
        query_map, key_map, scaled_query, scaled_key, valid, cosine, sine_a, sine_b, lift,
        after=(token,),
    )
    token = output.step(row_grads[0])
    token = down.step(token, micros=1)
    lanes = 3 * width + 128
    own, *sib = call(
        weights_back,
        [((half, lanes), BF16), ((half // 2, lanes), BF16), ((half // 2, lanes), BF16)],
        "weights_back",
        0,
        *row_grads, rows_rel, place, sums_ffn, sums_attn, small_0, small_1, small_2, small_3,
        after=(token,),
    )
    third = Scatter(moves, [own], [sib], "third")
    token = down.step(own)
    token = up.step(token)
    token = third.step(token)
    token = output.step(token, micros=LONG)
    i0, i1, i2 = call(
        rows_back, flats, "rows_back", 0, *row_grads, own_attn, sib_attn, place, first_grad,
        after=(token,),
    )
    token = down.step(i0, micros=LONG)
    token = up.step(token)
    token = output.step(token)
    token = third.step(token, micros=LONG)
    token = up.step(token, micros=LONG)
    token = output.step(token)
    token = third.step(token)
    grad_up, grad_down = call(
        finish_ffn,
        [((hidden, width), F32)] * 2,
        "finish_ffn",
        LONG,
        *down.total(), *up.total(),
        after=(token,),
    )
    third.step(grad_up)
    grad_query, grad_key, grad_value, grad_output, column = call(
        finish_attn, [((step, width), F32)] * 4 + [((16, step), F32)], "finish_attn", 0,
        *third.total(), *output.total(),
    )
    grad_up_bias = column[UB : UB + chunks].reshape(-1)
    outs = [o.reshape(block.shape) for o, block in zip((o0, o1, o2, i0, i1, i2), inputs * 2)]
    return (
        *outs,
        grad_query, grad_key, grad_value, grad_output,
        column[BQ], column[BK], column[BV], column[BO], column[AG], column[AS],
        grad_up.T, grad_up_bias, grad_down, column[DB], column[FG], column[FS],
    )


def solution(mesh):
    moves = Moves(mesh.shape["batch"], mesh.shape["seq"])

    def body(*args):
        return on_device(
            moves, args[0:3], args[3:6], args[6:9], args[9:19], args[19:25], args[25]
        )

    tokens = P("batch", "seq", None)
    shard = P(AXES)
    rows = P(AXES, None)
    attn = (rows,) * 4 + (shard,) * 6
    ffn = (P(None, AXES), shard, rows, shard, shard, shard)
    in_specs = (tokens,) * 3 + (P("batch"),) * 3 + (tokens,) * 3 + attn + ffn + (P(),)
    out_specs = (tokens,) * 6 + attn + ffn
    return jax.shard_map(
        body, mesh=mesh, in_specs=in_specs, out_specs=out_specs, check_vma=False
    )
```

```python
import functools
import math

import jax
import jax.numpy as jnp
import numpy as np
from jax import lax
from jax.experimental import pallas as pl
from jax.experimental.pallas import tpu as pltpu
from jax.sharding import PartitionSpec as P

HD = 64
HIGH = lax.Precision.HIGHEST
EPS_NORM = 1e-05
EPS_DEN = 1e-06
F32 = jnp.float32
BF16 = jnp.bfloat16
AXES = ("batch", "seq")
GROUP = 256
FEAT = 128
VMEM = 14 * 1024 * 1024
PLAN = (
    "n0:ea", "eb:ea", "f1:n0.", "a0:tables", "n1:n0", "f2:n0", "b0:n1,eb=1", "a1:f0,n1.",
    "fo:n1", "n2:a0", "w0:a1,n2", "no:n2", "b1:a1.", "a2", "fr:n2.", "b2:w0", "w1=100",
    "wo:w1.", "mi:w0", "g1", "w2:mi.", "g2", "bd", "be", "k2", "d0", "k1", "tu:k1.,bd.", "u0",
    "ab", "o0", "d1=1", "wb", "d2", "u1=100", "t0", "o1=100", "rb", "d3=1", "o2", "u2",
    "t1=100", "u3=100", "o3", "t2:o3.", "ff=100", "t3",
)
PIECES = (1, 2, 2)
BQ, BK, BV, BO, AG, AS, DB, FG, FS, UB = range(10)


def nn(a, b, precision=None):
    return lax.dot_general(
        a, b, (((1,), (0,)), ((), ())), precision=precision, preferred_element_type=F32
    )


def nt(a, b, precision=None):
    return lax.dot_general(
        a, b, (((1,), (1,)), ((), ())), precision=precision, preferred_element_type=F32
    )


def tn(a, b):
    return lax.dot_general(a, b, (((0,), (0,)), ((), ())), preferred_element_type=F32)


def split(x):
    high = x.astype(BF16)
    return high, (x - high.astype(F32)).astype(BF16)


def iota(shape, axis):
    return lax.broadcasted_iota(jnp.int32, shape, axis)


def head_mask():
    return iota((FEAT, GROUP), 0) // 32 == iota((FEAT, GROUP), 1) // 64


def spread_mask(rows, row_size, lanes, lane_size):
    same = iota((rows, lanes), 0) // row_size == iota((rows, lanes), 1) // lane_size
    return same.astype(F32).astype(BF16)


def compact(block, mask):
    kept = jnp.where(mask, block, 0.0)
    kept = kept[:, :FEAT] + kept[:, FEAT:]
    return jnp.concatenate([kept[0:32] + kept[32:64], kept[64:96] + kept[96:128]], 0)


def expand(block, mask):
    top, bottom = block[0:32], block[32:64]
    rows = jnp.concatenate([top, top, bottom, bottom], 0)
    return jnp.where(mask, jnp.concatenate([rows, rows], 1), 0.0)


def both(mine, other, start, count):
    return mine[start : start + count, :] + other[start : start + count, :]


def exact(x, ones):
    high, low = split(x)
    return nn(high, ones) + nn(low, ones)


def rotate(block, cosine, sine_a, sine_b):
    parts = []
    for lane in range(0, block.shape[1], 128):
        part = block[:, lane : lane + 128]
        parts.append(
            part * cosine + pltpu.roll(part, 96, 1) * sine_a + pltpu.roll(part, 32, 1) * sine_b
        )
    return jnp.concatenate(parts, 1)


def lane_mean(block):
    return jnp.mean(block, axis=-1, keepdims=True)


def norm_back(upstream, normed, spread, gain):
    scaled = upstream * gain
    return spread * (scaled - lane_mean(scaled) - normed * lane_mean(scaled * normed))


def column_sum(block):
    return jnp.sum(block, axis=0, keepdims=True)


def skipping(body, count, extra, *refs):
    return body(*refs[:count], *refs[count + extra :])


def call(body, outs, name, micros, *args, after=(), stage=False):
    whole = pl.BlockSpec(memory_space=pltpu.VMEM)
    anywhere = pl.BlockSpec(memory_space=pl.ANY)
    scratch = [pltpu.VMEM(arg.shape, arg.dtype) for arg in args]
    scratch.append(pltpu.SemaphoreType.DMA((len(args),)))
    return pl.pallas_call(
        functools.partial(skipping, body, len(args), len(after)) if after else body,
        out_shape=tuple(jax.ShapeDtypeStruct(shape, kind) for shape, kind in outs),
        in_specs=[anywhere if stage else whole] * len(args) + [anywhere] * len(after),
        scratch_shapes=scratch if stage else [],
        out_specs=tuple(whole for _ in outs),
        compiler_params=pltpu.CompilerParams(vmem_limit_bytes=VMEM),
        cost_estimate=pl.CostEstimate(
            flops=int(micros * 1.15e9), bytes_accessed=10**6, transcendentals=0
        ),
        name=name,
    )(*args, *after)


def pack(
    chunks, early, query, keys, value, output, small, up, down,
    attn, out, first, second, whole, *scratch
):
    buffers, sems = scratch[:-1], scratch[-1]
    sources = (query, keys, value, output, small, up, down)
    copies = [
        pltpu.make_async_copy(source, buffer, sems.at[index])
        for index, (source, buffer) in enumerate(zip(sources, buffers))
    ]
    for copy in copies:
        copy.start()
    for copy in copies:
        copy.wait()
    step, width = query.shape
    for index in range(3):
        attn[:, index * width : (index + 1) * width] = buffers[index][...]
    out[...] = buffers[3][...]
    eye = (iota((16, 128), 0) == iota((16, 128), 1)).astype(F32).astype(BF16)
    attn[:, 3 * width :] = tn(buffers[4][...], eye).astype(BF16)
    for chunk in range(chunks):
        part = first if chunk < early else second
        at = 2 * width * (chunk if chunk < early else chunk - early)
        rows = slice(chunk * step, (chunk + 1) * step)
        part[:, at : at + width] = buffers[5][rows, :]
        part[:, at + width : at + 2 * width] = buffers[6][rows, :]
    lane = 0
    for part in (attn, out, first, second):
        whole[:, lane : lane + part.shape[1]] = part[...]
        lane += part.shape[1]


def front(
    pieces, x0, x1, x2, own, sib, place, cosine, sine_a, sine_b, valid, lift, norm,
    packed, query_map, key_map, scaled_query, scaled_key, value_low, rows_rel, vectors,
):
    half = own.shape[0]
    width = 2 * half
    tail = own.shape[1] - 128
    x = jnp.concatenate([x0[...], x1[...], x2[...]], 0)
    rel = nn(x, place[...]).astype(BF16)
    rows_rel[...] = rel
    left, right = rel[:, :half], rel[:, half:]
    small_own = own[:, tail:].T
    small_sib = sib[:, tail:].T
    ordered = nt(small_own, place[:, :half]) + nt(small_sib, place[:, half:])
    vectors[0:16, :] = ordered[0:16]
    vectors[16:32, :half] = small_own[0:16].astype(F32)
    vectors[16:32, half:] = small_sib[0:16].astype(F32)
    cos, sin_a, sin_b = cosine[...], sine_a[...], sine_b[...]
    ok = valid[...]
    mask = head_mask()
    lift_high, lift_low = split(lift[...])
    halves = norm[...].astype(BF16)
    totals = len(pieces) * (width // GROUP) * 64
    for group in range(width // GROUP):
        feats = slice(group * FEAT, (group + 1) * FEAT)
        lanes = slice(group * GROUP, (group + 1) * GROUP)

        def project(index):
            start = index * width + group * GROUP
            cut = slice(start, start + GROUP)
            bias = ordered[index : index + 1, lanes]
            return nn(left, own[:, cut]) + nn(right, sib[:, cut]) + bias

        low = project(2).astype(BF16)
        value_low[:, lanes] = low
        maps = []
        for index, kept in ((0, scaled_query), (1, scaled_key)):
            scaled = rotate(project(index), cos, sin_a, sin_b)
            kept[:, lanes] = scaled
            high, low_part = split(scaled)
            power = nn(high, lift_high) + (nn(high, lift_low) + nn(low_part, lift_high))
            power += exact(scaled * scaled, halves)
            maps.append(jnp.exp(power) * (1.0 / math.sqrt(32.0)))
        query_map[:, feats] = maps[0]
        key_map[:, feats] = maps[1]
        feat = maps[1].astype(BF16).astype(F32) * ok
        for index, (start, stop) in enumerate(pieces):
            slot = index * (width // GROUP) + group
            state = tn(feat[start:stop].astype(BF16), low[start:stop])
            packed[slot * 64 : (slot + 1) * 64, :] = compact(state, mask)
            packed[totals + slot : totals + slot + 1, :] = column_sum(feat[start:stop])


def middle(
    pieces, mine, other, query_map, x0, x1, x2, own, sib, place, vectors,
    attended, over, over_feat, attended_rel, normed, spread, middle_low,
):
    half = own.shape[0]
    width = 2 * half
    mask = head_mask()
    wide = spread_mask(FEAT, 32, GROUP, 64)
    narrow = spread_mask(FEAT, 32, FEAT, 32)
    totals = len(pieces) * (width // GROUP) * 64
    for group in range(width // GROUP):
        feats = slice(group * FEAT, (group + 1) * FEAT)
        lanes = slice(group * GROUP, (group + 1) * GROUP)
        feat = query_map[:, feats].astype(BF16)
        tops, bottoms = [], []
        for index, (start, stop) in enumerate(pieces):
            slot = index * (width // GROUP) + group
            state_high, state_low = split(expand(both(mine, other, slot * 64, 64), mask))
            part = feat[start:stop]
            tops.append(nn(part, state_high) + nn(part, state_low))
            bottoms.append(part.astype(F32) * both(mine, other, totals + slot, 1))
        high, low = split(jnp.concatenate(bottoms, 0))
        inverse = 1.0 / (nn(high, wide) + nn(low, wide) + EPS_DEN)
        over[:, lanes] = inverse
        over_feat[:, feats] = 1.0 / (nn(high, narrow) + nn(low, narrow) + EPS_DEN)
        attended[:, lanes] = jnp.concatenate(tops, 0) * inverse
    rel = nn(attended[...].astype(BF16), place[...]).astype(BF16)
    attended_rel[...] = rel
    branch = nn(rel[:, :half], own[...])
    branch += nn(rel[:, half:], sib[...])
    x = jnp.concatenate([x0[...], x1[...], x2[...]], 0).astype(F32)
    first = x + branch + vectors[BO : BO + 1, :]
    center = first - lane_mean(first)
    scale = lax.rsqrt(lane_mean(center * center) + EPS_NORM)
    norm = center * scale
    normed[...] = norm
    spread[...] = jnp.broadcast_to(scale, spread.shape)
    middle_low[...] = (norm * vectors[AG : AG + 1, :] + vectors[AS : AS + 1, :]).astype(BF16)


def ffn_chunks(base, chunks, middle_low, own, sib, vectors, activated, slope):
    half = own.shape[0]
    width = 2 * half
    low = middle_low[...]
    total = None
    for chunk in range(chunks):
        lane = chunk * 2 * width
        row = 16 + UB + base + chunk
        for index, part in enumerate((own, sib)):
            cut = slice(index * half, (index + 1) * half)
            pre = nt(low, part[:, lane : lane + width]) + vectors[row : row + 1, cut]
            cdf = 0.5 + 0.5 * lax.erf(pre * math.sqrt(0.5))
            act = (pre * cdf).astype(BF16)
            bell = jnp.exp(-0.5 * pre * pre) * (1.0 / math.sqrt(2.0 * math.pi))
            cut = slice(chunk * width + index * half, chunk * width + (index + 1) * half)
            activated[:, cut] = act
            slope[:, cut] = (cdf + pre * bell).astype(BF16)
            product = nn(act, part[:, lane + width : lane + 2 * width])
            total = product if total is None else total + product
    return total


def ffn_first(base, chunks, middle_low, own, sib, vectors, activated, slope, total):
    total[...] = ffn_chunks(base, chunks, middle_low, own, sib, vectors, activated, slope)


def ffn_second(
    base, chunks, middle_low, own, sib, vectors, before, normed, c0, c1, c2,
    activated, slope, o0, o1, o2, second_grad, down_low, sums,
):
    total = ffn_chunks(base, chunks, middle_low, own, sib, vectors, activated, slope)
    mid = normed[...] * vectors[AG : AG + 1, :] + vectors[AS : AS + 1, :]
    second = mid + (before[...] + total) + vectors[DB : DB + 1, :]
    center = second - lane_mean(second)
    spread = lax.rsqrt(lane_mean(center * center) + EPS_NORM)
    norm = center * spread
    gain = vectors[FG : FG + 1, :]
    result = (norm * gain + vectors[FS : FS + 1, :]).astype(BF16)
    start = 0
    for out in (o0, o1, o2):
        out[...] = result[start : start + out.shape[0]]
        start += out.shape[0]
    upstream = jnp.concatenate([c0[...], c1[...], c2[...]], 0).astype(F32)
    grad = norm_back(upstream, norm, spread, gain)
    low = grad.astype(BF16)
    second_grad[...] = grad
    down_low[...] = low
    sums[...] = jnp.zeros(sums.shape, F32)
    sums[0:1, :] = column_sum(low.astype(F32))
    sums[1:2, :] = column_sum(upstream * norm)
    sums[2:3, :] = column_sum(upstream)


def back_down(activated, down_low, grad_own, grad_sib):
    half, lanes = grad_own.shape
    width = 2 * half
    down = down_low[...]
    for chunk in range(lanes // width):
        cut = slice(chunk * width, (chunk + 1) * width)
        middle_lane = chunk * width + half
        grad_own[:, cut] = tn(activated[:, chunk * width : middle_lane], down).astype(BF16)
        grad_sib[:, cut] = tn(activated[:, middle_lane : (chunk + 1) * width], down).astype(BF16)


def back_up(base, count, middle_low, down_low, own, sib, slope, total, small_own, small_sib, *grads):
    half = own.shape[0]
    width = 2 * half
    low = middle_low[...]
    down = down_low[...]
    result = None
    small = [None, None]
    for chunk in range(count):
        lane = chunk * 2 * width
        at = slice(chunk * width, (chunk + 1) * width)
        pick = (iota((low.shape[0], 128), 1) == UB + base + chunk).astype(F32).astype(BF16)
        for index, part in enumerate((own, sib)):
            cut = slice(chunk * width + index * half, chunk * width + (index + 1) * half)
            up = nt(down, part[:, lane + width : lane + 2 * width])
            up = (up * slope[:, cut].astype(F32)).astype(BF16)
            weight = tn(up, low).astype(BF16)
            row = 0
            for grad in grads[:1] if index == 0 else grads[1:]:
                grad[:, at] = weight[row : row + grad.shape[0]]
                row += grad.shape[0]
            bias = tn(up, pick)
            small[index] = bias if small[index] is None else small[index] + bias
            product = nn(up, part[:, lane : lane + width])
            result = product if result is None else result + product
    total[...] = result
    small_own[...] = small[0]
    small_sib[...] = small[1]


def turn(
    pieces, before, after, second_grad, normed, spread, vectors, own_attn, sib_attn,
    attended_rel, place, attended, over, over_feat, query_map,
    grad_own, grad_sib, packed, num_low, den_grad, first_grad, sums,
):
    half = own_attn.shape[0]
    width = 2 * half
    grad = second_grad[...] + (before[...] + after[...])
    norm = normed[...]
    first = norm_back(grad, norm, spread[:, 0:1], vectors[AG : AG + 1, :])
    branch = first.astype(BF16)
    first_grad[...] = first
    sums[...] = jnp.zeros(sums.shape, F32)
    sums[0:1, :] = column_sum(branch.astype(F32))
    sums[1:2, :] = column_sum(grad * norm)
    sums[2:3, :] = column_sum(grad)
    weight = tn(attended_rel[...], branch).astype(BF16)
    grad_own[...] = weight[:half]
    grad_sib[...] = weight[half:]
    rel = jnp.concatenate([nt(branch, own_attn[...]), nt(branch, sib_attn[...])], 1)
    rel_high, rel_low = split(rel)
    upstream = nt(rel_high, place[...]) + nt(rel_low, place[...])
    inverse = over[...]
    num = (upstream * inverse).astype(BF16)
    num_low[...] = num
    weighted_high, weighted_low = split(upstream * attended[...])
    mask = head_mask()
    narrow = spread_mask(GROUP, 64, FEAT, 32)
    totals = len(pieces) * (width // GROUP) * 64
    for group in range(width // GROUP):
        lanes = slice(group * GROUP, (group + 1) * GROUP)
        feats = slice(group * FEAT, (group + 1) * FEAT)
        den = nn(weighted_high[:, lanes], narrow) + nn(weighted_low[:, lanes], narrow)
        den = -den * over_feat[:, feats]
        den_grad[:, feats] = den
        feat = query_map[:, feats].astype(BF16)
        den = den * feat.astype(F32)
        for index, (start, stop) in enumerate(pieces):
            slot = index * (width // GROUP) + group
            state = tn(feat[start:stop], num[start:stop, lanes])
            packed[slot * 64 : (slot + 1) * 64, :] = compact(state, mask)
            packed[totals + slot : totals + slot + 1, :] = column_sum(den[start:stop])


def attend_back(
    pieces, mine, other, mine_grad, other_grad, num_low, den_grad, value_low, query_map, key_map,
    scaled_query, scaled_key, valid, cosine, sine_a, sine_b, lift,
    query_grad, key_grad, value_grad,
):
    width = value_low.shape[1]
    mask = head_mask()
    cos, sin_a, sin_b = cosine[...], sine_a[...], sine_b[...]
    ok = valid[...]
    lift_high, lift_low = split(lift[...])
    wide = spread_mask(FEAT, 32, GROUP, 64)
    totals = len(pieces) * (width // GROUP) * 64
    for group in range(width // GROUP):
        lanes = slice(group * GROUP, (group + 1) * GROUP)
        feats = slice(group * FEAT, (group + 1) * FEAT)
        query_parts, key_parts = [], []
        key_low = (key_map[:, feats].astype(BF16).astype(F32) * ok).astype(BF16)
        for index, (start, stop) in enumerate(pieces):
            slot = index * (width // GROUP) + group
            state_high, state_low = split(expand(both(mine, other, slot * 64, 64), mask))
            grads = expand(both(mine_grad, other_grad, slot * 64, 64), mask)
            sg_high, sg_low = split(grads)
            num = num_low[start:stop, lanes]
            part = den_grad[start:stop, feats] * both(mine, other, totals + slot, 1)
            query_parts.append(part + (nt(num, state_high) + nt(num, state_low)))
            value = value_low[start:stop, lanes]
            row = both(mine_grad, other_grad, totals + slot, 1)
            key_parts.append(row + (nt(value, sg_high) + nt(value, sg_low)))
            low = key_low[start:stop]
            value_grad[start:stop, lanes] = (nn(low, sg_high) + nn(low, sg_low)).astype(BF16)
        query_inner = jnp.concatenate(query_parts, 0) * query_map[:, feats]
        key_inner = jnp.concatenate(key_parts, 0) * ok * key_map[:, feats]
        for inner, scaled, grad in (
            (query_inner, scaled_query, query_grad),
            (key_inner, scaled_key, key_grad),
        ):
            high, low = split(inner)
            back = nt(high, lift_high) + (nt(high, lift_low) + nt(low, lift_high))
            back -= (nn(high, wide) + nn(low, wide)) * scaled[:, lanes]
            grad[:, lanes] = rotate(back, cos, -sin_a, -sin_b).astype(BF16)


def weights_back(
    query_grad, key_grad, value_grad, rows_rel, place, sums_ffn, sums_attn,
    small_0, small_1, small_2, small_3, grad_own, *grad_sib,
):
    half = grad_own.shape[0]
    width = 2 * half
    part = half // len(grad_sib)
    rel = rows_rel[...]
    rows = []

    def keep(cut, block):
        grad_own[:, cut] = block[:half]
        for index, grad in enumerate(grad_sib):
            grad[:, cut] = block[half + index * part : half + (index + 1) * part]

    for index, grad in enumerate((query_grad, key_grad, value_grad)):
        block = grad[...]
        keep(slice(index * width, (index + 1) * width), tn(rel, block).astype(BF16))
        rows.append(column_sum(block.astype(F32)))
    rows += [sums_attn[0:3, :], sums_ffn[0:3, :]]
    rows.append(jnp.zeros((128 - 9, width), F32))
    columns = nn(jnp.concatenate(rows, 0).astype(BF16), place[...]).T
    left = columns[:half] + small_0[...] + small_2[...]
    right = columns[half:] + small_1[...] + small_3[...]
    total = jnp.concatenate([left, right], 0).astype(BF16)
    keep(slice(3 * width, 3 * width + 128), total)


def rows_back(query_grad, key_grad, value_grad, own, sib, place, first_grad, i0, i1, i2):
    width = place.shape[0]
    back = []
    for part in (own, sib):
        total = None
        for index, grad in enumerate((query_grad, key_grad, value_grad)):
            product = nt(grad[...], part[:, index * width : (index + 1) * width])
            total = product if total is None else total + product
        back.append(total)
    rel_high, rel_low = split(jnp.concatenate(back, 1))
    total = first_grad[...] + (nt(rel_high, place[...]) + nt(rel_low, place[...]))
    result = total.astype(BF16)
    start = 0
    for out in (i0, i1, i2):
        out[...] = result[start : start + out.shape[0]]
        start += out.shape[0]


def finish_ffn(down_low, down_high, up_low, up_high, up, down):
    step = down_low.shape[0]
    width = up.shape[1]
    for low, high, out in ((up_low, up_high, up), (down_low, down_high, down)):
        total = low[...].astype(F32) + high[...].astype(F32)
        for chunk in range(total.shape[1] // width):
            out[chunk * step : (chunk + 1) * step, :] = total[:, chunk * width : (chunk + 1) * width]


def finish_attn(low, high, output_low, output_high, query, keys, value, output, small):
    step, width = query.shape
    for index, out in enumerate((query, keys, value)):
        cut = slice(index * width, (index + 1) * width)
        out[...] = low[:, cut].astype(F32) + high[:, cut].astype(F32)
    output[...] = output_low[...].astype(F32) + output_high[...].astype(F32)
    cut = slice(3 * width, 3 * width + 128)
    eye = (iota((step, step), 0) == iota((step, step), 1)).astype(F32).astype(BF16)
    small[...] = (tn(low[:, cut], eye) + tn(high[:, cut], eye))[0:16]


class Moves:
    def __init__(self, batch, seq):
        self.batch, self.seq = batch, seq
        self.cube = batch == 16 and seq == 2

    def send(self, block, flip, other=None, core_flip=0, name="send"):
        flips = (flip, flip if other is None else other)
        pairs = []
        for b in range(self.batch):
            for c in range(self.seq):
                pairs.append((b * self.seq + c, (b ^ flips[c]) * self.seq + (c ^ core_flip)))
        with jax.named_scope(name):
            return lax.ppermute(block, AXES, pairs)

    def across(self, block, name="across"):
        return self.send(block, 0, 0, 1, name)

    def order(self):
        b, c = lax.axis_index("batch"), lax.axis_index("seq")
        places = jnp.arange(self.batch, dtype=jnp.int32)
        if not self.cube:
            return jnp.concatenate([places * self.seq + c, places * self.seq + (1 - c)])
        flips = np.array([[p ^ z for p in o for z in (0, 8, 4, 12)] for o in ((0, 1, 2, 3), (0, 2, 1, 3))])
        flips = flips.astype(np.int32)
        mine = jnp.where(c == 0, flips[0], flips[1])
        theirs = jnp.where(c == 0, flips[1], flips[0])
        return jnp.concatenate(
            [jnp.bitwise_xor(b, mine) * self.seq + c, jnp.bitwise_xor(b, theirs) * self.seq + 1 - c]
        )

    def gather(self, whole, shares):
        if not self.cube:
            return None
        step = whole.shape[0]
        lanes, lane = [], 0
        for share in shares:
            lanes.append((lane, lane + share.shape[1]))
            lane += share.shape[1]
        got = {"ea": self.send(whole, 1, 2, name="early_a"), "f0": self.send(shares[0], 8, name="f0")}

        def move(name, flips, *parts):
            def run(after, micros):
                block = join([got[one] if isinstance(one, str) else one for one in parts], after, micros)
                got[name] = self.send(block, *flips, name=name)
                return block

            return run

        def finish(index):
            cut, key = lanes[index], "0-12"[index]

            def run(after, micros):
                first, second, early_b = got["a" + key], got["b" + key], got["eb"]
                parts = [
                    shares[index], got["f" + key], got["n" + key], (got["ea"], 0, step, *cut), first,
                    (early_b, 0, step, *cut), (second, 0, 3 * step, 0, second.shape[1]),
                    (early_b, step, 2 * step, *cut),
                    (second, 3 * step, 6 * step, 0, second.shape[1]),
                ]
                own = join(parts, after, micros)
                got["w" + key] = (own, self.across(own, "w" + key))
                return own

            return run

        steps = {"eb": move("eb", (2, 1), whole, "ea")}
        out_cut = lanes[1]

        def out_far(after, micros):
            early_a, early_b = got["ea"], got["eb"]
            parts = [shares[1], (early_a, 0, step, *out_cut), (early_b, 0, 2 * step, *out_cut)]
            got["plane"] = join(parts, after, micros)
            got["fo"] = self.send(got["plane"], 8, name="fo")
            return got["plane"]

        def out_finish(after, micros):
            parts = []
            for plane in range(4):
                cut = (plane * step, (plane + 1) * step, 0, out_cut[1] - out_cut[0])
                last = ((4 + plane) * step, (5 + plane) * step, *cut[2:])
                parts += [(got["plane"], *cut), (got["fo"], *cut), (got["no"], *cut), (got["no"], *last)]
            own = join(parts, after, micros)
            got["wo"] = (own, self.across(own, "wo"))
            return own

        steps.update(fo=out_far, no=move("no", (4,), "plane", "fo"), wo=out_finish)
        for index, share in enumerate(shares):
            if index == 1:
                continue
            key = "0-12"[index]
            steps["f" + key] = move("f" + key, (8,), share)
            steps["n" + key] = move("n" + key, (4,), share, "f" + key)
            steps["a" + key] = move("a" + key, (1, 2), "f" + key, "n" + key)
            steps["b" + key] = move("b" + key, (2, 1), "f" + key, "n" + key, "a" + key)
            steps["w" + key] = finish(index)
        return steps, got


class Scatter:
    def __init__(self, moves, own, sib, tag, z_first=False):
        self.moves, self.tag, self.kept, self.stage = moves, tag, own, 0
        self.coming = [[moves.across(part, tag + "_across") for part in parts] for parts in sib]
        plane = [((2, 1), 1), ((1, 2), 1)]
        self.plan = plane + [((4, 4), 1), ((8, 8), 1)]
        if z_first:
            self.plan = [((4, 4), 4), ((8, 8), 4)] + plane

    def step(self, after, micros=0):
        if not self.moves.cube:
            if self.stage == 0:
                coming = [jnp.concatenate(parts, 0) for parts in self.coming]
                self.kept = [add(jnp.concatenate(self.kept, 1), jnp.concatenate(coming, 1))]
                self.stage = 1
            return self.kept[0]
        flips, runs = self.plan[self.stage]
        rows, lanes = self.kept[0].shape[0], sum(part.shape[1] for part in self.kept)
        half, run = (rows // 2, lanes), rows // runs
        kept, coming = self.kept, self.coming

        def body(*refs):
            low, high = refs[-2:]
            lane, at = 0, len(kept)
            for ref, parts in zip(refs, coming):
                cut = slice(lane, lane + ref.shape[1])
                lane += ref.shape[1]
                block = jnp.concatenate([one[...] for one in refs[at : at + len(parts)]], 0)
                at += len(parts)
                total = (ref[...].astype(F32) + block.astype(F32)).astype(BF16)
                for index in range(runs):
                    out, start = slice(index * run // 2, (index + 1) * run // 2), index * run
                    low[out, cut] = total[start : start + run // 2]
                    high[out, cut] = total[start + run // 2 : start + run]

        name = f"{self.tag}_add{self.stage}"
        arrays = list(kept) + [part for parts in coming for part in parts]
        keep, out = call(body, [(half, BF16), (half, BF16)], name, micros, *arrays, after=after)
        self.kept = [keep]
        self.coming = [[self.moves.send(out, *flips, name=f"{self.tag}_{self.stage}")]]
        self.stage += 1
        return keep

    def total(self):
        if not self.moves.cube:
            total = lax.psum_scatter(self.kept[0], "batch", scatter_dimension=0, tiled=True)
            return total, jnp.zeros_like(total)
        return self.kept[0], self.coming[0][0]


def join(parts, after, micros):
    parts = [part if isinstance(part, tuple) else (part, 0, part.shape[0], 0, part.shape[1]) for part in parts]

    def body(*refs):
        row = 0
        for ref, (_, start, stop, left, right) in zip(refs, parts):
            refs[-1][row : row + stop - start, :] = ref[start:stop, left:right]
            row += stop - start

    rows = sum(stop - start for _, start, stop, _, _ in parts)
    shape = (rows, parts[0][4] - parts[0][3])
    arrays = [part[0] for part in parts]
    return call(body, [(shape, arrays[0].dtype)], "join", micros, *arrays, after=after)[0]


def add(*blocks):
    total = blocks[0].astype(F32)
    for block in blocks[1:]:
        total = total + block.astype(F32)
    return total.astype(BF16)


def on_device(moves, inputs, lengths, cotangents, attn, ffn, projection):
    query_weight, key_weight, value_weight, output_weight = attn[:4]
    up_weight, up_bias, down_weight, down_bias, ffn_gain, ffn_shift = ffn
    step, width = query_weight.shape
    hidden = up_bias.shape[0]
    chunks = hidden // step
    first_half = chunks // 2

    small = [*attn[4:], down_bias, ffn_gain, ffn_shift]
    small += [up_bias[i * step : (i + 1) * step] for i in range(chunks)]
    at = jnp.arange(16, dtype=jnp.int32)[:, None]
    small = sum(jnp.where(at == index, one[None, :], 0).astype(BF16) for index, one in enumerate(small))
    sizes = [3 * width + 128, width, first_half * 2 * width, (chunks - first_half) * 2 * width]
    sources = (*attn[:4], small, up_weight.T, down_weight)
    sources = [pltpu.with_memory_space_constraint(one, pltpu.HBM) for one in sources]
    *shares, whole = call(
        functools.partial(pack, chunks, first_half),
        [((step, lanes), BF16) for lanes in (*sizes, sum(sizes))],
        "pack",
        0,
        *sources,
        stage=True,
    )

    ranks = moves.order()
    rows_at = (ranks[:, None] * step + jnp.arange(step, dtype=jnp.int32)[None, :]).reshape(-1)
    place = (jnp.arange(width, dtype=jnp.int32)[:, None] == rows_at[None, :]).astype(BF16)

    blocks, valids, positions, pieces = [], [], [], []
    start = 0
    for block, limit in zip(inputs, lengths):
        count, local, _ = block.shape
        blocks.append(block.reshape(count * local, width))
        at = lax.axis_index("seq") * local + jnp.arange(local, dtype=jnp.int32)
        positions.append(jnp.tile(at, count))
        valids.append((at[None, :] < limit[:, None]).reshape(-1))
        for _ in range(count):
            pieces.append((start, start + local))
            start += local
    pieces = tuple(pieces)
    rows = start
    position = jnp.concatenate(positions).astype(F32)
    valid = jnp.broadcast_to(jnp.concatenate(valids).astype(F32)[:, None], (rows, FEAT))
    half_head = HD // 2
    rates = 10000.0 ** (-jnp.arange(half_head, dtype=F32) / half_head)
    angle = position[:, None] * rates[None, :]
    scale = HD ** (-0.25)
    cos, sin = jnp.cos(angle) * scale, jnp.sin(angle) * scale
    none = jnp.zeros_like(sin)
    cosine = jnp.concatenate([cos] * 4, 1)
    sine_a = jnp.concatenate([-sin, none] * 2, 1)
    sine_b = jnp.concatenate([none, sin] * 2, 1)
    same = np.arange(GROUP)[:, None] // 64 == np.arange(FEAT)[None, :] // 32
    lift = jnp.where(same, jnp.tile(projection, (4, 4)), 0.0)
    norm = jnp.asarray(np.where(same, -0.5, 0.0), F32)

    half = width // 2
    feats = width // 2
    slots = len(pieces) * (width // GROUP)
    wide, narrow = (rows, width), (rows, feats)
    packed_shape = (slots * 64 + -(-slots // 8) * 8, FEAT)
    tables = (place, cosine, sine_a, sine_b, valid, lift, norm)
    part = (rows, first_half * width)
    rest = (rows, (chunks - first_half) * width)
    square = (half, width)
    flat = [block.reshape(-1, width) for block in cotangents]
    flats = [(block.shape, BF16) for block in flat]
    planned = moves.gather(whole, shares)
    if planned is None:
        owns = [lax.all_gather(share, "batch", axis=0, tiled=True) for share in shares]
        steps, got = {}, {"w" + key: (own, moves.across(own)) for key, own in zip("0o12", owns)}
    else:
        steps, got = planned

    def kernel(name, body, outs, *args):
        def run(after, micros):
            got[name] = call(body, outs, name, micros, *args, after=after)
            return got[name][0]

        return run

    def front_run(after, micros):
        token = kernel(
            "front",
            functools.partial(front, pieces),
            [
                (packed_shape, F32), (narrow, F32), (narrow, F32), (wide, F32), (wide, F32),
                (wide, BF16), (wide, BF16), ((32, width), F32),
            ],
            *blocks, *got["w0"], *tables,
        )(after, micros)
        got["e1"] = moves.across(token, "e1")
        return token

    def middle_run(after, micros):
        kept = got["front"]
        return kernel(
            "middle",
            functools.partial(middle, pieces),
            [
                (wide, F32), (wide, F32), (narrow, F32), (wide, BF16), (wide, F32),
                ((rows, 128), F32), (wide, BF16),
            ],
            kept[0], got["e1"], kept[1], *blocks, *got["wo"], place, kept[-1],
        )(after, micros)

    def ffn_first_run(after, micros):
        return kernel(
            "ffn_first",
            functools.partial(ffn_first, 0, first_half),
            [(part, BF16), (part, BF16), (wide, F32)],
            got["middle"][-1], *got["w1"], got["front"][-1],
        )(after, micros)

    def ffn_second_run(after, micros):
        return kernel(
            "ffn_second",
            functools.partial(ffn_second, first_half, chunks - first_half),
            [(rest, BF16), (rest, BF16), *flats, (wide, F32), (wide, BF16), ((8, width), F32)],
            got["middle"][-1], *got["w2"], got["front"][-1], got["ffn_first"][2],
            got["middle"][4], *flat,
        )(after, micros)

    def scatter_run(name):
        return lambda after, micros: got[name].step(after, micros)

    def down_run(name, source, count):
        def run(after, micros):
            shape = (half, count * width)
            return kernel(
                name, back_down, [(shape, BF16)] * 2, got[source][0], got["ffn_second"][6]
            )(after, micros)

        return run

    down_first_run = down_run("down_first", "ffn_first", first_half)
    down_second_run = down_run("down_second", "ffn_second", chunks - first_half)

    def down_last_run(after, micros):
        token = down_second_run(after, micros)
        one, two = got["down_first"], got["down_second"]
        got["d"] = Scatter(moves, [one[0], two[0]], [one[1:], two[1:]], "d")
        return token

    def back_run(name, base, count, weights, slope, parts):
        def run(after, micros):
            return kernel(
                name,
                functools.partial(back_up, base, count),
                [(wide, F32), ((half, 128), F32), ((half, 128), F32)]
                + [((half // part, count * width), BF16) for part in parts],
                got["middle"][-1], got["ffn_second"][6], *got[weights], got[slope][1],
            )(after, micros)

        return run

    back_second_run = back_run(
        "back_second", first_half, chunks - first_half, "w2", "ffn_second",
        (1,) + (PIECES[0],) * PIECES[0],
    )
    back_first_only = back_run(
        "back_first", 0, first_half, "w1", "ffn_first", (1,) + (PIECES[1],) * PIECES[1]
    )

    def back_first_run(after, micros):
        token = back_first_only(after, micros)
        one, two = got["back_first"][3:], got["back_second"][3:]
        got["u"] = Scatter(moves, [one[0], two[0]], [one[1:], two[1:]], "u")
        return token

    def turn_run(after, micros):
        kept, more = got["front"], got["middle"]
        token = kernel(
            "turn",
            functools.partial(turn, pieces),
            [
                (square, BF16), (square, BF16), (packed_shape, F32), (wide, BF16), (narrow, F32),
                (wide, F32), ((8, width), F32),
            ],
            got["back_first"][0], got["back_second"][0], got["ffn_second"][5], more[4], more[5],
            kept[-1], *got["wo"], more[3], place, more[0], more[1], more[2], kept[1],
        )(after, micros)
        got["e2"] = moves.across(got["turn"][2], "e2")
        got["o"] = Scatter(moves, [token], [[got["turn"][1]]], "o", z_first=True)
        return token

    def attend_run(after, micros):
        kept, turned = got["front"], got["turn"]
        return kernel(
            "attend_back",
            functools.partial(attend_back, pieces),
            [(wide, BF16)] * 3,
            kept[0], got["e1"], turned[2], got["e2"], turned[3], turned[4], kept[5], kept[1],
            kept[2], kept[3], kept[4], valid, cosine, sine_a, sine_b, lift,
        )(after, micros)

    def weights_run(after, micros):
        lanes, count = 3 * width + 128, PIECES[2]
        token = kernel(
            "weights_back",
            weights_back,
            [((half, lanes), BF16)] + [((half // count, lanes), BF16)] * count,
            *got["attend_back"], got["front"][6], place, got["ffn_second"][-1], got["turn"][-1],
            *got["back_second"][1:3], *got["back_first"][1:3],
        )(after, micros)
        got["t"] = Scatter(moves, [token], [got["weights_back"][1:]], "t")
        return token

    def rows_run(after, micros):
        return kernel(
            "rows_back", rows_back, flats, *got["attend_back"], *got["w0"], place, got["turn"][5]
        )(after, micros)

    def finish_run(after, micros):
        return kernel(
            "finish_ffn", finish_ffn, [((hidden, width), F32)] * 2, *got["d"].total(), *got["u"].total()
        )(after, micros)

    steps.update(
        fr=front_run, mi=middle_run, g1=ffn_first_run, g2=ffn_second_run, bd=down_first_run, be=down_last_run,
        k2=back_second_run, k1=back_first_run, tu=turn_run, ab=attend_run, wb=weights_run,
        rb=rows_run, ff=finish_run,
        **{name + str(index): scatter_run(name) for name in "duot" for index in range(4)},
    )
    token, done = None, {}

    def found(name):
        if name == "tables":
            return tables
        if name[-1] == ".":
            return (done[name[:-1]],)
        return (got[name][-1] if isinstance(got[name], tuple) else got[name],)

    for name in PLAN:
        name, _, cost = name.partition("=")
        name, _, before = name.partition(":")
        if name in steps:
            after = () if token is None or (before and planned) else (token,)
            if before and planned:
                after = sum((found(one) for one in before.split(",")), ())
            token = done[name] = steps[name](after, int(cost or 0))
    grad_up, grad_down = got["finish_ffn"]
    i0, i1, i2 = got["rows_back"]
    o0, o1, o2 = got["ffn_second"][2:5]
    grad_query, grad_key, grad_value, grad_output, column = call(
        finish_attn, [((step, width), F32)] * 4 + [((16, step), F32)], "finish_attn", 0,
        *got["t"].total(), *got["o"].total(),
    )
    grad_up_bias = column[UB : UB + chunks].reshape(-1)
    outs = [o.reshape(block.shape) for o, block in zip((o0, o1, o2, i0, i1, i2), inputs * 2)]
    return (
        *outs,
        grad_query, grad_key, grad_value, grad_output,
        column[BQ], column[BK], column[BV], column[BO], column[AG], column[AS],
        grad_up.T, grad_up_bias, grad_down, column[DB], column[FG], column[FS],
    )


def solution(mesh):
    moves = Moves(mesh.shape["batch"], mesh.shape["seq"])

    def body(*args):
        return on_device(
            moves, args[0:3], args[3:6], args[6:9], args[9:19], args[19:25], args[25]
        )

    tokens = P("batch", "seq", None)
    shard = P(AXES)
    rows = P(AXES, None)
    attn = (rows,) * 4 + (shard,) * 6
    ffn = (P(None, AXES), shard, rows, shard, shard, shard)
    in_specs = (tokens,) * 3 + (P("batch"),) * 3 + (tokens,) * 3 + attn + ffn + (P(),)
    out_specs = (tokens,) * 6 + attn + ffn
    return jax.shard_map(
        body, mesh=mesh, in_specs=in_specs, out_specs=out_specs, check_vma=False
    )
```

```python
import functools
import math

import jax
import jax.numpy as jnp
import numpy as np
from jax import lax
from jax.experimental import pallas as pl
from jax.experimental.pallas import tpu as pltpu
from jax.sharding import PartitionSpec as P

HD = 64
HIGH = lax.Precision.HIGHEST
EPS_NORM = 1e-05
EPS_DEN = 1e-06
F32 = jnp.float32
BF16 = jnp.bfloat16
AXES = ("batch", "seq")
GROUP = 256
FEAT = 128
VMEM = 14 * 1024 * 1024
PLAN = ("n0:ea", "eb:ea", "f1:n0.", "a0:tables", "n1:n0", "f2:n0", "b0:n1,eb=1", "a1:f0,n1.", "fo:n1", "n2:a0", "w0:a1,n2,a0", "b1:a1.", "a2", "fr:a2.", "no:fr.", "b2:fr.,w0", "w1=100", "wo:w1.", "mi:wo,e1", "g1", "w2:mi.", "g2", "bd", "be", "k2", "d0", "k1", "tu:k1.,bd.", "u0", "d1=1", "ab", "o0", "wb", "d2", "u1=100", "t0", "o1=100", "rb", "d3=3", "o2", "u2", "t1=100", "u3=100", "o3", "t2:o3.", "ff=3", "t3",)
PIECES = (1, 2, 2)
BQ, BK, BV, BO, AG, AS, DB, FG, FS, UB = range(10)


def nn(a, b, precision=None):
    return lax.dot_general(
        a, b, (((1,), (0,)), ((), ())), precision=precision, preferred_element_type=F32
    )


def nt(a, b, precision=None):
    return lax.dot_general(
        a, b, (((1,), (1,)), ((), ())), precision=precision, preferred_element_type=F32
    )


def tn(a, b):
    return lax.dot_general(a, b, (((0,), (0,)), ((), ())), preferred_element_type=F32)


def split(x):
    high = x.astype(BF16)
    return high, (x - high.astype(F32)).astype(BF16)


def iota(shape, axis):
    return lax.broadcasted_iota(jnp.int32, shape, axis)


def head_mask():
    return iota((FEAT, GROUP), 0) // 32 == iota((FEAT, GROUP), 1) // 64


def spread_mask(rows, row_size, lanes, lane_size):
    same = iota((rows, lanes), 0) // row_size == iota((rows, lanes), 1) // lane_size
    return same.astype(F32).astype(BF16)


def compact(block, mask):
    kept = jnp.where(mask, block, 0.0)
    kept = kept[:, :FEAT] + kept[:, FEAT:]
    return jnp.concatenate([kept[0:32] + kept[32:64], kept[64:96] + kept[96:128]], 0)


def expand(block, mask):
    top, bottom = block[0:32], block[32:64]
    rows = jnp.concatenate([top, top, bottom, bottom], 0)
    return jnp.where(mask, jnp.concatenate([rows, rows], 1), 0.0)


def both(mine, other, start, count):
    return mine[start : start + count, :] + other[start : start + count, :]


def exact(x, ones):
    high, low = split(x)
    return nn(high, ones) + nn(low, ones)


def rotate(block, cosine, sine_a, sine_b):
    parts = []
    for lane in range(0, block.shape[1], 128):
        part = block[:, lane : lane + 128]
        parts.append(
            part * cosine + pltpu.roll(part, 96, 1) * sine_a + pltpu.roll(part, 32, 1) * sine_b
        )
    return jnp.concatenate(parts, 1)


def lane_mean(block):
    return jnp.mean(block, axis=-1, keepdims=True)


def norm_back(upstream, normed, spread, gain):
    scaled = upstream * gain
    return spread * (scaled - lane_mean(scaled) - normed * lane_mean(scaled * normed))


def column_sum(block):
    return jnp.sum(block, axis=0, keepdims=True)


def skipping(body, count, extra, *refs):
    return body(*refs[:count], *refs[count + extra :])


def call(body, outs, name, micros, *args, after=(), stage=False):
    whole = pl.BlockSpec(memory_space=pltpu.VMEM)
    anywhere = pl.BlockSpec(memory_space=pl.ANY)
    scratch = [pltpu.VMEM(arg.shape, arg.dtype) for arg in args]
    scratch.append(pltpu.SemaphoreType.DMA((len(args),)))
    return pl.pallas_call(
        functools.partial(skipping, body, len(args), len(after)) if after else body,
        out_shape=tuple(jax.ShapeDtypeStruct(shape, kind) for shape, kind in outs),
        in_specs=[anywhere if stage else whole] * len(args) + [anywhere] * len(after),
        scratch_shapes=scratch if stage else [],
        out_specs=tuple(whole for _ in outs),
        compiler_params=pltpu.CompilerParams(vmem_limit_bytes=VMEM),
        cost_estimate=pl.CostEstimate(
            flops=int(micros * 1.15e9), bytes_accessed=10**6, transcendentals=0
        ),
        name=name,
    )(*args, *after)


def pack(
    chunks, early, query, keys, value, output, small, up, down,
    attn, out, first, second, whole, *scratch
):
    buffers, sems = scratch[:-1], scratch[-1]
    sources = (query, keys, value, output, small, up, down)
    copies = [
        pltpu.make_async_copy(source, buffer, sems.at[index])
        for index, (source, buffer) in enumerate(zip(sources, buffers))
    ]
    for copy in copies:
        copy.start()
    for copy in copies:
        copy.wait()
    step, width = query.shape
    for index in range(3):
        attn[:, index * width : (index + 1) * width] = buffers[index][...]
    out[...] = buffers[3][...]
    eye = (iota((16, 128), 0) == iota((16, 128), 1)).astype(F32).astype(BF16)
    attn[:, 3 * width :] = tn(buffers[4][...], eye).astype(BF16)
    for chunk in range(chunks):
        part = first if chunk < early else second
        at = 2 * width * (chunk if chunk < early else chunk - early)
        rows = slice(chunk * step, (chunk + 1) * step)
        part[:, at : at + width] = buffers[5][rows, :]
        part[:, at + width : at + 2 * width] = buffers[6][rows, :]
    lane = 0
    for part in (attn, out, first, second):
        whole[:, lane : lane + part.shape[1]] = part[...]
        lane += part.shape[1]


def front(
    pieces, x0, x1, x2, own, sib, place, cosine, sine_a, sine_b, valid, lift, norm,
    packed, query_map, key_map, scaled_query, scaled_key, value_low, rows_rel, vectors,
):
    half = own.shape[0]
    width = 2 * half
    tail = own.shape[1] - 128
    x = jnp.concatenate([x0[...], x1[...], x2[...]], 0)
    rel = nn(x, place[...]).astype(BF16)
    rows_rel[...] = rel
    left, right = rel[:, :half], rel[:, half:]
    small_own = own[:, tail:].T
    small_sib = sib[:, tail:].T
    ordered = nt(small_own, place[:, :half]) + nt(small_sib, place[:, half:])
    vectors[0:16, :] = ordered[0:16]
    vectors[16:32, :half] = small_own[0:16].astype(F32)
    vectors[16:32, half:] = small_sib[0:16].astype(F32)
    cos, sin_a, sin_b = cosine[...], sine_a[...], sine_b[...]
    ok = valid[...]
    mask = head_mask()
    lift_high, lift_low = split(lift[...])
    halves = norm[...].astype(BF16)
    totals = len(pieces) * (width // GROUP) * 64
    for group in range(width // GROUP):
        feats = slice(group * FEAT, (group + 1) * FEAT)
        lanes = slice(group * GROUP, (group + 1) * GROUP)

        def project(index):
            start = index * width + group * GROUP
            cut = slice(start, start + GROUP)
            bias = ordered[index : index + 1, lanes]
            return nn(left, own[:, cut]) + nn(right, sib[:, cut]) + bias

        low = project(2).astype(BF16)
        value_low[:, lanes] = low
        maps = []
        for index, kept in ((0, scaled_query), (1, scaled_key)):
            scaled = rotate(project(index), cos, sin_a, sin_b)
            kept[:, lanes] = scaled
            high, low_part = split(scaled)
            power = nn(high, lift_high) + (nn(high, lift_low) + nn(low_part, lift_high))
            power += exact(scaled * scaled, halves)
            maps.append(jnp.exp(power) * (1.0 / math.sqrt(32.0)))
        query_map[:, feats] = maps[0]
        key_map[:, feats] = maps[1]
        feat = maps[1].astype(BF16).astype(F32) * ok
        for index, (start, stop) in enumerate(pieces):
            slot = index * (width // GROUP) + group
            state = tn(feat[start:stop].astype(BF16), low[start:stop])
            packed[slot * 64 : (slot + 1) * 64, :] = compact(state, mask)
            packed[totals + slot : totals + slot + 1, :] = column_sum(feat[start:stop])


def middle(
    pieces, mine, other, query_map, x0, x1, x2, own, sib, place, vectors,
    attended, over, over_feat, attended_rel, normed, spread, middle_low,
):
    half = own.shape[0]
    width = 2 * half
    mask = head_mask()
    wide = spread_mask(FEAT, 32, GROUP, 64)
    narrow = spread_mask(FEAT, 32, FEAT, 32)
    totals = len(pieces) * (width // GROUP) * 64
    for group in range(width // GROUP):
        feats = slice(group * FEAT, (group + 1) * FEAT)
        lanes = slice(group * GROUP, (group + 1) * GROUP)
        feat = query_map[:, feats].astype(BF16)
        tops, bottoms = [], []
        for index, (start, stop) in enumerate(pieces):
            slot = index * (width // GROUP) + group
            state_high, state_low = split(expand(both(mine, other, slot * 64, 64), mask))
            part = feat[start:stop]
            tops.append(nn(part, state_high) + nn(part, state_low))
            bottoms.append(part.astype(F32) * both(mine, other, totals + slot, 1))
        high, low = split(jnp.concatenate(bottoms, 0))
        inverse = 1.0 / (nn(high, wide) + nn(low, wide) + EPS_DEN)
        over[:, lanes] = inverse
        over_feat[:, feats] = 1.0 / (nn(high, narrow) + nn(low, narrow) + EPS_DEN)
        attended[:, lanes] = jnp.concatenate(tops, 0) * inverse
    rel = nn(attended[...].astype(BF16), place[...]).astype(BF16)
    attended_rel[...] = rel
    branch = nn(rel[:, :half], own[...])
    branch += nn(rel[:, half:], sib[...])
    x = jnp.concatenate([x0[...], x1[...], x2[...]], 0).astype(F32)
    first = x + branch + vectors[BO : BO + 1, :]
    center = first - lane_mean(first)
    scale = lax.rsqrt(lane_mean(center * center) + EPS_NORM)
    norm = center * scale
    normed[...] = norm
    spread[...] = jnp.broadcast_to(scale, spread.shape)
    middle_low[...] = (norm * vectors[AG : AG + 1, :] + vectors[AS : AS + 1, :]).astype(BF16)


def ffn_chunks(base, chunks, middle_low, own, sib, vectors, activated, slope):
    half = own.shape[0]
    width = 2 * half
    low = middle_low[...]
    total = None
    for chunk in range(chunks):
        lane = chunk * 2 * width
        row = 16 + UB + base + chunk
        for index, part in enumerate((own, sib)):
            cut = slice(index * half, (index + 1) * half)
            pre = nt(low, part[:, lane : lane + width]) + vectors[row : row + 1, cut]
            cdf = 0.5 + 0.5 * lax.erf(pre * math.sqrt(0.5))
            act = (pre * cdf).astype(BF16)
            bell = jnp.exp(-0.5 * pre * pre) * (1.0 / math.sqrt(2.0 * math.pi))
            cut = slice(chunk * width + index * half, chunk * width + (index + 1) * half)
            activated[:, cut] = act
            slope[:, cut] = (cdf + pre * bell).astype(BF16)
            product = nn(act, part[:, lane + width : lane + 2 * width])
            total = product if total is None else total + product
    return total


def ffn_first(base, chunks, middle_low, own, sib, vectors, activated, slope, total):
    total[...] = ffn_chunks(base, chunks, middle_low, own, sib, vectors, activated, slope)


def ffn_second(
    base, chunks, middle_low, own, sib, vectors, before, normed, c0, c1, c2,
    activated, slope, o0, o1, o2, second_grad, down_low, sums,
):
    total = ffn_chunks(base, chunks, middle_low, own, sib, vectors, activated, slope)
    mid = normed[...] * vectors[AG : AG + 1, :] + vectors[AS : AS + 1, :]
    second = mid + (before[...] + total) + vectors[DB : DB + 1, :]
    center = second - lane_mean(second)
    spread = lax.rsqrt(lane_mean(center * center) + EPS_NORM)
    norm = center * spread
    gain = vectors[FG : FG + 1, :]
    result = (norm * gain + vectors[FS : FS + 1, :]).astype(BF16)
    start = 0
    for out in (o0, o1, o2):
        out[...] = result[start : start + out.shape[0]]
        start += out.shape[0]
    upstream = jnp.concatenate([c0[...], c1[...], c2[...]], 0).astype(F32)
    grad = norm_back(upstream, norm, spread, gain)
    low = grad.astype(BF16)
    second_grad[...] = grad
    down_low[...] = low
    sums[...] = jnp.zeros(sums.shape, F32)
    sums[0:1, :] = column_sum(low.astype(F32))
    sums[1:2, :] = column_sum(upstream * norm)
    sums[2:3, :] = column_sum(upstream)


def back_down(activated, down_low, grad_own, grad_sib):
    half, lanes = grad_own.shape
    width = 2 * half
    down = down_low[...]
    for chunk in range(lanes // width):
        cut = slice(chunk * width, (chunk + 1) * width)
        middle_lane = chunk * width + half
        grad_own[:, cut] = tn(activated[:, chunk * width : middle_lane], down).astype(BF16)
        grad_sib[:, cut] = tn(activated[:, middle_lane : (chunk + 1) * width], down).astype(BF16)


def back_up(base, count, middle_low, down_low, own, sib, slope, total, small_own, small_sib, *grads):
    half = own.shape[0]
    width = 2 * half
    low = middle_low[...]
    down = down_low[...]
    result = None
    small = [None, None]
    for chunk in range(count):
        lane = chunk * 2 * width
        at = slice(chunk * width, (chunk + 1) * width)
        pick = (iota((low.shape[0], 128), 1) == UB + base + chunk).astype(F32).astype(BF16)
        for index, part in enumerate((own, sib)):
            cut = slice(chunk * width + index * half, chunk * width + (index + 1) * half)
            up = nt(down, part[:, lane + width : lane + 2 * width])
            up = (up * slope[:, cut].astype(F32)).astype(BF16)
            weight = tn(up, low).astype(BF16)
            row = 0
            for grad in grads[:1] if index == 0 else grads[1:]:
                grad[:, at] = weight[row : row + grad.shape[0]]
                row += grad.shape[0]
            bias = tn(up, pick)
            small[index] = bias if small[index] is None else small[index] + bias
            product = nn(up, part[:, lane : lane + width])
            result = product if result is None else result + product
    total[...] = result
    small_own[...] = small[0]
    small_sib[...] = small[1]


def turn(
    pieces, before, after, second_grad, normed, spread, vectors, own_attn, sib_attn,
    attended_rel, place, attended, over, over_feat, query_map,
    grad_own, grad_sib, packed, num_low, den_grad, first_grad, sums,
):
    half = own_attn.shape[0]
    width = 2 * half
    grad = second_grad[...] + (before[...] + after[...])
    norm = normed[...]
    first = norm_back(grad, norm, spread[:, 0:1], vectors[AG : AG + 1, :])
    branch = first.astype(BF16)
    first_grad[...] = first
    sums[...] = jnp.zeros(sums.shape, F32)
    sums[0:1, :] = column_sum(branch.astype(F32))
    sums[1:2, :] = column_sum(grad * norm)
    sums[2:3, :] = column_sum(grad)
    weight = tn(attended_rel[...], branch).astype(BF16)
    grad_own[...] = weight[:half]
    grad_sib[...] = weight[half:]
    rel = jnp.concatenate([nt(branch, own_attn[...]), nt(branch, sib_attn[...])], 1)
    rel_high, rel_low = split(rel)
    upstream = nt(rel_high, place[...]) + nt(rel_low, place[...])
    inverse = over[...]
    num = (upstream * inverse).astype(BF16)
    num_low[...] = num
    weighted_high, weighted_low = split(upstream * attended[...])
    mask = head_mask()
    narrow = spread_mask(GROUP, 64, FEAT, 32)
    totals = len(pieces) * (width // GROUP) * 64
    for group in range(width // GROUP):
        lanes = slice(group * GROUP, (group + 1) * GROUP)
        feats = slice(group * FEAT, (group + 1) * FEAT)
        den = nn(weighted_high[:, lanes], narrow) + nn(weighted_low[:, lanes], narrow)
        den = -den * over_feat[:, feats]
        den_grad[:, feats] = den
        feat = query_map[:, feats].astype(BF16)
        den = den * feat.astype(F32)
        for index, (start, stop) in enumerate(pieces):
            slot = index * (width // GROUP) + group
            state = tn(feat[start:stop], num[start:stop, lanes])
            packed[slot * 64 : (slot + 1) * 64, :] = compact(state, mask)
            packed[totals + slot : totals + slot + 1, :] = column_sum(den[start:stop])


def attend_back(
    pieces, mine, other, mine_grad, other_grad, num_low, den_grad, value_low, query_map, key_map,
    scaled_query, scaled_key, valid, cosine, sine_a, sine_b, lift,
    query_grad, key_grad, value_grad,
):
    width = value_low.shape[1]
    mask = head_mask()
    cos, sin_a, sin_b = cosine[...], sine_a[...], sine_b[...]
    ok = valid[...]
    lift_high, lift_low = split(lift[...])
    wide = spread_mask(FEAT, 32, GROUP, 64)
    totals = len(pieces) * (width // GROUP) * 64
    for group in range(width // GROUP):
        lanes = slice(group * GROUP, (group + 1) * GROUP)
        feats = slice(group * FEAT, (group + 1) * FEAT)
        query_parts, key_parts = [], []
        key_low = (key_map[:, feats].astype(BF16).astype(F32) * ok).astype(BF16)
        for index, (start, stop) in enumerate(pieces):
            slot = index * (width // GROUP) + group
            state_high, state_low = split(expand(both(mine, other, slot * 64, 64), mask))
            grads = expand(both(mine_grad, other_grad, slot * 64, 64), mask)
            sg_high, sg_low = split(grads)
            num = num_low[start:stop, lanes]
            part = den_grad[start:stop, feats] * both(mine, other, totals + slot, 1)
            query_parts.append(part + (nt(num, state_high) + nt(num, state_low)))
            value = value_low[start:stop, lanes]
            row = both(mine_grad, other_grad, totals + slot, 1)
            key_parts.append(row + (nt(value, sg_high) + nt(value, sg_low)))
            low = key_low[start:stop]
            value_grad[start:stop, lanes] = (nn(low, sg_high) + nn(low, sg_low)).astype(BF16)
        query_inner = jnp.concatenate(query_parts, 0) * query_map[:, feats]
        key_inner = jnp.concatenate(key_parts, 0) * ok * key_map[:, feats]
        for inner, scaled, grad in (
            (query_inner, scaled_query, query_grad),
            (key_inner, scaled_key, key_grad),
        ):
            high, low = split(inner)
            back = nt(high, lift_high) + (nt(high, lift_low) + nt(low, lift_high))
            back -= (nn(high, wide) + nn(low, wide)) * scaled[:, lanes]
            grad[:, lanes] = rotate(back, cos, -sin_a, -sin_b).astype(BF16)


def weights_back(
    query_grad, key_grad, value_grad, rows_rel, place, sums_ffn, sums_attn,
    small_0, small_1, small_2, small_3, grad_own, *grad_sib,
):
    half = grad_own.shape[0]
    width = 2 * half
    part = half // len(grad_sib)
    rel = rows_rel[...]
    rows = []

    def keep(cut, block):
        grad_own[:, cut] = block[:half]
        for index, grad in enumerate(grad_sib):
            grad[:, cut] = block[half + index * part : half + (index + 1) * part]

    for index, grad in enumerate((query_grad, key_grad, value_grad)):
        block = grad[...]
        keep(slice(index * width, (index + 1) * width), tn(rel, block).astype(BF16))
        rows.append(column_sum(block.astype(F32)))
    rows += [sums_attn[0:3, :], sums_ffn[0:3, :]]
    rows.append(jnp.zeros((128 - 9, width), F32))
    columns = nn(jnp.concatenate(rows, 0).astype(BF16), place[...]).T
    left = columns[:half] + small_0[...] + small_2[...]
    right = columns[half:] + small_1[...] + small_3[...]
    total = jnp.concatenate([left, right], 0).astype(BF16)
    keep(slice(3 * width, 3 * width + 128), total)


def rows_back(query_grad, key_grad, value_grad, own, sib, place, first_grad, i0, i1, i2):
    width = place.shape[0]
    back = []
    for part in (own, sib):
        total = None
        for index, grad in enumerate((query_grad, key_grad, value_grad)):
            product = nt(grad[...], part[:, index * width : (index + 1) * width])
            total = product if total is None else total + product
        back.append(total)
    rel_high, rel_low = split(jnp.concatenate(back, 1))
    total = first_grad[...] + (nt(rel_high, place[...]) + nt(rel_low, place[...]))
    result = total.astype(BF16)
    start = 0
    for out in (i0, i1, i2):
        out[...] = result[start : start + out.shape[0]]
        start += out.shape[0]


def finish_ffn(down_low, down_high, up_low, up_high, up, down):
    step = down_low.shape[0]
    width = up.shape[1]
    for low, high, out in ((up_low, up_high, up), (down_low, down_high, down)):
        total = low[...].astype(F32) + high[...].astype(F32)
        for chunk in range(total.shape[1] // width):
            out[chunk * step : (chunk + 1) * step, :] = total[:, chunk * width : (chunk + 1) * width]


def finish_attn(low, high, output_low, output_high, query, keys, value, output, small):
    step, width = query.shape
    for index, out in enumerate((query, keys, value)):
        cut = slice(index * width, (index + 1) * width)
        out[...] = low[:, cut].astype(F32) + high[:, cut].astype(F32)
    output[...] = output_low[...].astype(F32) + output_high[...].astype(F32)
    cut = slice(3 * width, 3 * width + 128)
    eye = (iota((step, step), 0) == iota((step, step), 1)).astype(F32).astype(BF16)
    small[...] = (tn(low[:, cut], eye) + tn(high[:, cut], eye))[0:16]


class Moves:
    def __init__(self, batch, seq):
        self.batch, self.seq = batch, seq
        self.cube = batch == 16 and seq == 2

    def send(self, block, flip, other=None, core_flip=0, name="send"):
        flips = (flip, flip if other is None else other)
        pairs = []
        for b in range(self.batch):
            for c in range(self.seq):
                pairs.append((b * self.seq + c, (b ^ flips[c]) * self.seq + (c ^ core_flip)))
        with jax.named_scope(name):
            return lax.ppermute(block, AXES, pairs)

    def across(self, block, name="across"):
        return self.send(block, 0, 0, 1, name)

    def order(self):
        b, c = lax.axis_index("batch"), lax.axis_index("seq")
        places = jnp.arange(self.batch, dtype=jnp.int32)
        if not self.cube:
            return jnp.concatenate([places * self.seq + c, places * self.seq + (1 - c)])
        flips = np.array([[p ^ z for p in o for z in (0, 8, 4, 12)] for o in ((0, 1, 2, 3), (0, 2, 1, 3))])
        flips = flips.astype(np.int32)
        mine = jnp.where(c == 0, flips[0], flips[1])
        theirs = jnp.where(c == 0, flips[1], flips[0])
        return jnp.concatenate(
            [jnp.bitwise_xor(b, mine) * self.seq + c, jnp.bitwise_xor(b, theirs) * self.seq + 1 - c]
        )

    def gather(self, whole, shares):
        if not self.cube:
            return None
        step = whole.shape[0]
        lanes, lane = [], 0
        for share in shares:
            lanes.append((lane, lane + share.shape[1]))
            lane += share.shape[1]
        got = {"ea": self.send(whole, 1, 2, name="early_a"), "f0": self.send(shares[0], 8, name="f0")}

        def move(name, flips, *parts):
            def run(after, micros):
                block = join([got[one] if isinstance(one, str) else one for one in parts], after, micros)
                got[name] = self.send(block, *flips, name=name)
                return block

            return run

        def finish(index):
            cut, key = lanes[index], "0-12"[index]

            def run(after, micros):
                first, second, early_b = got["a" + key], got["b" + key], got["eb"]
                parts = [
                    shares[index], got["f" + key], got["n" + key], (got["ea"], 0, step, *cut), first,
                    (early_b, 0, step, *cut), (second, 0, 3 * step, 0, second.shape[1]),
                    (early_b, step, 2 * step, *cut),
                    (second, 3 * step, 6 * step, 0, second.shape[1]),
                ]
                own = join(parts, after, micros)
                got["w" + key] = (own, self.across(own, "w" + key))
                return own

            return run

        steps = {"eb": move("eb", (2, 1), whole, "ea")}
        out_cut = lanes[1]

        def out_far(after, micros):
            early_a, early_b = got["ea"], got["eb"]
            parts = [shares[1], (early_a, 0, step, *out_cut), (early_b, 0, 2 * step, *out_cut)]
            got["plane"] = join(parts, after, micros)
            got["fo"] = self.send(got["plane"], 8, name="fo")
            return got["plane"]

        def out_finish(after, micros):
            parts = []
            for plane in range(4):
                cut = (plane * step, (plane + 1) * step, 0, out_cut[1] - out_cut[0])
                last = ((4 + plane) * step, (5 + plane) * step, *cut[2:])
                parts += [(got["plane"], *cut), (got["fo"], *cut), (got["no"], *cut), (got["no"], *last)]
            own = join(parts, after, micros)
            got["wo"] = (own, self.across(own, "wo"))
            return own

        steps.update(fo=out_far, no=move("no", (4,), "plane", "fo"), wo=out_finish)
        for index, share in enumerate(shares):
            if index == 1:
                continue
            key = "0-12"[index]
            steps["f" + key] = move("f" + key, (8,), share)
            steps["n" + key] = move("n" + key, (4,), share, "f" + key)
            steps["a" + key] = move("a" + key, (1, 2), "f" + key, "n" + key)
            steps["b" + key] = move("b" + key, (2, 1), "f" + key, "n" + key, "a" + key)
            steps["w" + key] = finish(index)
        return steps, got


class Scatter:
    def __init__(self, moves, own, sib, tag, z_first=False):
        self.moves, self.tag, self.kept, self.stage = moves, tag, own, 0
        self.coming = [[moves.across(part, tag + "_across") for part in parts] for parts in sib]
        plane = [((2, 1), 1), ((1, 2), 1)]
        self.plan = plane + [((4, 4), 1), ((8, 8), 1)]
        if z_first:
            self.plan = [((4, 4), 4), ((8, 8), 4)] + plane

    def step(self, after, micros=0):
        if not self.moves.cube:
            if self.stage == 0:
                coming = [jnp.concatenate(parts, 0) for parts in self.coming]
                self.kept = [add(jnp.concatenate(self.kept, 1), jnp.concatenate(coming, 1))]
                self.stage = 1
            return self.kept[0]
        flips, runs = self.plan[self.stage]
        rows, lanes = self.kept[0].shape[0], sum(part.shape[1] for part in self.kept)
        half, run = (rows // 2, lanes), rows // runs
        kept, coming = self.kept, self.coming

        def body(*refs):
            low, high = refs[-2:]
            lane, at = 0, len(kept)
            for ref, parts in zip(refs, coming):
                cut = slice(lane, lane + ref.shape[1])
                lane += ref.shape[1]
                block = jnp.concatenate([one[...] for one in refs[at : at + len(parts)]], 0)
                at += len(parts)
                total = (ref[...].astype(F32) + block.astype(F32)).astype(BF16)
                for index in range(runs):
                    out, start = slice(index * run // 2, (index + 1) * run // 2), index * run
                    low[out, cut] = total[start : start + run // 2]
                    high[out, cut] = total[start + run // 2 : start + run]

        name = f"{self.tag}_add{self.stage}"
        arrays = list(kept) + [part for parts in coming for part in parts]
        keep, out = call(body, [(half, BF16), (half, BF16)], name, micros, *arrays, after=after)
        self.kept = [keep]
        self.coming = [[self.moves.send(out, *flips, name=f"{self.tag}_{self.stage}")]]
        self.stage += 1
        return keep

    def total(self):
        if not self.moves.cube:
            total = lax.psum_scatter(self.kept[0], "batch", scatter_dimension=0, tiled=True)
            return total, jnp.zeros_like(total)
        return self.kept[0], self.coming[0][0]


def join(parts, after, micros):
    parts = [part if isinstance(part, tuple) else (part, 0, part.shape[0], 0, part.shape[1]) for part in parts]

    def body(*refs):
        row = 0
        for ref, (_, start, stop, left, right) in zip(refs, parts):
            refs[-1][row : row + stop - start, :] = ref[start:stop, left:right]
            row += stop - start

    rows = sum(stop - start for _, start, stop, _, _ in parts)
    shape = (rows, parts[0][4] - parts[0][3])
    arrays = [part[0] for part in parts]
    return call(body, [(shape, arrays[0].dtype)], "join", micros, *arrays, after=after)[0]


def add(*blocks):
    total = blocks[0].astype(F32)
    for block in blocks[1:]:
        total = total + block.astype(F32)
    return total.astype(BF16)


def on_device(moves, inputs, lengths, cotangents, attn, ffn, projection):
    query_weight, key_weight, value_weight, output_weight = attn[:4]
    up_weight, up_bias, down_weight, down_bias, ffn_gain, ffn_shift = ffn
    step, width = query_weight.shape
    hidden = up_bias.shape[0]
    chunks = hidden // step
    first_half = chunks // 2

    small = [*attn[4:], down_bias, ffn_gain, ffn_shift]
    small += [up_bias[i * step : (i + 1) * step] for i in range(chunks)]
    at = jnp.arange(16, dtype=jnp.int32)[:, None]
    small = sum(jnp.where(at == index, one[None, :], 0).astype(BF16) for index, one in enumerate(small))
    sizes = [3 * width + 128, width, first_half * 2 * width, (chunks - first_half) * 2 * width]
    sources = (*attn[:4], small, up_weight.T, down_weight)
    sources = [pltpu.with_memory_space_constraint(one, pltpu.HBM) for one in sources]
    *shares, whole = call(
        functools.partial(pack, chunks, first_half),
        [((step, lanes), BF16) for lanes in (*sizes, sum(sizes))],
        "pack",
        0,
        *sources,
        stage=True,
    )

    ranks = moves.order()
    rows_at = (ranks[:, None] * step + jnp.arange(step, dtype=jnp.int32)[None, :]).reshape(-1)
    place = (jnp.arange(width, dtype=jnp.int32)[:, None] == rows_at[None, :]).astype(BF16)

    blocks, valids, positions, pieces = [], [], [], []
    start = 0
    for block, limit in zip(inputs, lengths):
        count, local, _ = block.shape
        blocks.append(block.reshape(count * local, width))
        at = lax.axis_index("seq") * local + jnp.arange(local, dtype=jnp.int32)
        positions.append(jnp.tile(at, count))
        valids.append((at[None, :] < limit[:, None]).reshape(-1))
        for _ in range(count):
            pieces.append((start, start + local))
            start += local
    pieces = tuple(pieces)
    rows = start
    position = jnp.concatenate(positions).astype(F32)
    valid = jnp.broadcast_to(jnp.concatenate(valids).astype(F32)[:, None], (rows, FEAT))
    half_head = HD // 2
    rates = 10000.0 ** (-jnp.arange(half_head, dtype=F32) / half_head)
    angle = position[:, None] * rates[None, :]
    scale = HD ** (-0.25)
    cos, sin = jnp.cos(angle) * scale, jnp.sin(angle) * scale
    none = jnp.zeros_like(sin)
    cosine = jnp.concatenate([cos] * 4, 1)
    sine_a = jnp.concatenate([-sin, none] * 2, 1)
    sine_b = jnp.concatenate([none, sin] * 2, 1)
    same = np.arange(GROUP)[:, None] // 64 == np.arange(FEAT)[None, :] // 32
    lift = jnp.where(same, jnp.tile(projection, (4, 4)), 0.0)
    norm = jnp.asarray(np.where(same, -0.5, 0.0), F32)

    half = width // 2
    feats = width // 2
    slots = len(pieces) * (width // GROUP)
    wide, narrow = (rows, width), (rows, feats)
    packed_shape = (slots * 64 + -(-slots // 8) * 8, FEAT)
    tables = (place, cosine, sine_a, sine_b, valid, lift, norm)
    part = (rows, first_half * width)
    rest = (rows, (chunks - first_half) * width)
    square = (half, width)
    flat = [block.reshape(-1, width) for block in cotangents]
    flats = [(block.shape, BF16) for block in flat]
    planned = moves.gather(whole, shares)
    if planned is None:
        owns = [lax.all_gather(share, "batch", axis=0, tiled=True) for share in shares]
        steps, got = {}, {"w" + key: (own, moves.across(own)) for key, own in zip("0o12", owns)}
    else:
        steps, got = planned

    def kernel(name, body, outs, *args):
        def run(after, micros):
            got[name] = call(body, outs, name, micros, *args, after=after)
            return got[name][0]

        return run

    def front_run(after, micros):
        token = kernel(
            "front",
            functools.partial(front, pieces),
            [
                (packed_shape, F32), (narrow, F32), (narrow, F32), (wide, F32), (wide, F32),
                (wide, BF16), (wide, BF16), ((32, width), F32),
            ],
            *blocks, *got["w0"], *tables,
        )(after, micros)
        got["e1"] = moves.across(token, "e1")
        return token

    def middle_run(after, micros):
        kept = got["front"]
        return kernel(
            "middle",
            functools.partial(middle, pieces),
            [
                (wide, F32), (wide, F32), (narrow, F32), (wide, BF16), (wide, F32),
                ((rows, 128), F32), (wide, BF16),
            ],
            kept[0], got["e1"], kept[1], *blocks, *got["wo"], place, kept[-1],
        )(after, micros)

    def ffn_first_run(after, micros):
        return kernel(
            "ffn_first",
            functools.partial(ffn_first, 0, first_half),
            [(part, BF16), (part, BF16), (wide, F32)],
            got["middle"][-1], *got["w1"], got["front"][-1],
        )(after, micros)

    def ffn_second_run(after, micros):
        return kernel(
            "ffn_second",
            functools.partial(ffn_second, first_half, chunks - first_half),
            [(rest, BF16), (rest, BF16), *flats, (wide, F32), (wide, BF16), ((8, width), F32)],
            got["middle"][-1], *got["w2"], got["front"][-1], got["ffn_first"][2],
            got["middle"][4], *flat,
        )(after, micros)

    def scatter_run(name):
        return lambda after, micros: got[name].step(after, micros)

    def down_run(name, source, count):
        def run(after, micros):
            shape = (half, count * width)
            return kernel(
                name, back_down, [(shape, BF16)] * 2, got[source][0], got["ffn_second"][6]
            )(after, micros)

        return run

    down_first_run = down_run("down_first", "ffn_first", first_half)
    down_second_run = down_run("down_second", "ffn_second", chunks - first_half)

    def down_last_run(after, micros):
        token = down_second_run(after, micros)
        one, two = got["down_first"], got["down_second"]
        got["d"] = Scatter(moves, [one[0], two[0]], [one[1:], two[1:]], "d")
        return token

    def back_run(name, base, count, weights, slope, parts):
        def run(after, micros):
            return kernel(
                name,
                functools.partial(back_up, base, count),
                [(wide, F32), ((half, 128), F32), ((half, 128), F32)]
                + [((half // part, count * width), BF16) for part in parts],
                got["middle"][-1], got["ffn_second"][6], *got[weights], got[slope][1],
            )(after, micros)

        return run

    back_second_run = back_run(
        "back_second", first_half, chunks - first_half, "w2", "ffn_second",
        (1,) + (PIECES[0],) * PIECES[0],
    )
    back_first_only = back_run(
        "back_first", 0, first_half, "w1", "ffn_first", (1,) + (PIECES[1],) * PIECES[1]
    )

    def back_first_run(after, micros):
        token = back_first_only(after, micros)
        one, two = got["back_first"][3:], got["back_second"][3:]
        got["u"] = Scatter(moves, [one[0], two[0]], [one[1:], two[1:]], "u")
        return token

    def turn_run(after, micros):
        kept, more = got["front"], got["middle"]
        token = kernel(
            "turn",
            functools.partial(turn, pieces),
            [
                (square, BF16), (square, BF16), (packed_shape, F32), (wide, BF16), (narrow, F32),
                (wide, F32), ((8, width), F32),
            ],
            got["back_first"][0], got["back_second"][0], got["ffn_second"][5], more[4], more[5],
            kept[-1], *got["wo"], more[3], place, more[0], more[1], more[2], kept[1],
        )(after, micros)
        got["e2"] = moves.across(got["turn"][2], "e2")
        got["o"] = Scatter(moves, [token], [[got["turn"][1]]], "o", z_first=True)
        return token

    def attend_run(after, micros):
        kept, turned = got["front"], got["turn"]
        return kernel(
            "attend_back",
            functools.partial(attend_back, pieces),
            [(wide, BF16)] * 3,
            kept[0], got["e1"], turned[2], got["e2"], turned[3], turned[4], kept[5], kept[1],
            kept[2], kept[3], kept[4], valid, cosine, sine_a, sine_b, lift,
        )(after, micros)

    def weights_run(after, micros):
        lanes, count = 3 * width + 128, PIECES[2]
        token = kernel(
            "weights_back",
            weights_back,
            [((half, lanes), BF16)] + [((half // count, lanes), BF16)] * count,
            *got["attend_back"], got["front"][6], place, got["ffn_second"][-1], got["turn"][-1],
            *got["back_second"][1:3], *got["back_first"][1:3],
        )(after, micros)
        got["t"] = Scatter(moves, [token], [got["weights_back"][1:]], "t")
        return token

    def rows_run(after, micros):
        return kernel(
            "rows_back", rows_back, flats, *got["attend_back"], *got["w0"], place, got["turn"][5]
        )(after, micros)

    def finish_run(after, micros):
        return kernel(
            "finish_ffn", finish_ffn, [((hidden, width), F32)] * 2, *got["d"].total(), *got["u"].total()
        )(after, micros)

    steps.update(
        fr=front_run, mi=middle_run, g1=ffn_first_run, g2=ffn_second_run, bd=down_first_run, be=down_last_run,
        k2=back_second_run, k1=back_first_run, tu=turn_run, ab=attend_run, wb=weights_run,
        rb=rows_run, ff=finish_run,
        **{name + str(index): scatter_run(name) for name in "duot" for index in range(4)},
    )
    token, done = None, {}

    def found(name):
        if name == "tables":
            return tables
        if name[-1] == ".":
            return (done[name[:-1]],)
        return (got[name][-1] if isinstance(got[name], tuple) else got[name],)

    for name in PLAN:
        name, _, cost = name.partition("=")
        name, _, before = name.partition(":")
        if name in steps:
            after = () if token is None or (before and planned) else (token,)
            if before and planned:
                after = sum((found(one) for one in before.split(",")), ())
            token = done[name] = steps[name](after, int(cost or 0))
    grad_up, grad_down = got["finish_ffn"]
    i0, i1, i2 = got["rows_back"]
    o0, o1, o2 = got["ffn_second"][2:5]
    grad_query, grad_key, grad_value, grad_output, column = call(
        finish_attn, [((step, width), F32)] * 4 + [((16, step), F32)], "finish_attn", 0,
        *got["t"].total(), *got["o"].total(),
    )
    grad_up_bias = column[UB : UB + chunks].reshape(-1)
    outs = [o.reshape(block.shape) for o, block in zip((o0, o1, o2, i0, i1, i2), inputs * 2)]
    return (
        *outs,
        grad_query, grad_key, grad_value, grad_output,
        column[BQ], column[BK], column[BV], column[BO], column[AG], column[AS],
        grad_up.T, grad_up_bias, grad_down, column[DB], column[FG], column[FS],
    )


def solution(mesh):
    moves = Moves(mesh.shape["batch"], mesh.shape["seq"])

    def body(*args):
        return on_device(
            moves, args[0:3], args[3:6], args[6:9], args[9:19], args[19:25], args[25]
        )

    tokens = P("batch", "seq", None)
    shard = P(AXES)
    rows = P(AXES, None)
    attn = (rows,) * 4 + (shard,) * 6
    ffn = (P(None, AXES), shard, rows, shard, shard, shard)
    in_specs = (tokens,) * 3 + (P("batch"),) * 3 + (tokens,) * 3 + attn + ffn + (P(),)
    out_specs = (tokens,) * 6 + attn + ffn
    return jax.shard_map(
        body, mesh=mesh, in_specs=in_specs, out_specs=out_specs, check_vma=False
    )
```
